128 devices in a mesh: sp: 2 (over core), ep: 64 (over x, y, z).
Axes of the slice: x: 4, y: 4, z: 4, core: 2. Of those that a mesh axis runs over, the one named last changes fastest.
Arguments:
- tokens: bfloat16 [64, 256, 768], P('ep', 'sp'), may hold values from -6 to 6
- cotangent: bfloat16 [64, 256, 768], P('ep', 'sp'), may hold values from -6 to 6
- w_query: bfloat16 [768, 768], P(('sp', 'ep')), may hold values from -0.21875 to 0.21875
- w_key: bfloat16 [768, 768], P(('sp', 'ep')), may hold values from -0.21875 to 0.21875
- w_value: bfloat16 [768, 768], P(('sp', 'ep')), may hold values from -0.21875 to 0.21875
- w_output: bfloat16 [768, 768], P(('sp', 'ep')), may hold values from -1.25 to 1.25
- gain_attn: bfloat16 [768], P(('sp', 'ep')), may hold values from 0.25 to 1.75
- gain_ffn: bfloat16 [768], P(('sp', 'ep')), may hold values from 0.25 to 1.75
- router: bfloat16 [768, 64], P(('sp', 'ep')), may hold values from -0.15625 to 0.15625
- bias_table: bfloat16 [384], P(('sp', 'ep')), may hold values from -4 to 4
- w_in: bfloat16 [64, 768, 3072], P('ep', None, 'sp'), may hold values from -0.21875 to 0.21875
- w_out: bfloat16 [64, 3072, 768], P('ep', 'sp'), may hold values from -0.109375 to 0.109375
- routes: int32 [64, 256, 2], P('ep', 'sp'), may hold values from 0 to 63, all different within a row; in each aligned block of 128 rows (0 to 127, 128 to 255, ..., all dimensions but the last counted through in order) at most 6 rows name the same one
- buckets: int32 [256], replicated, may hold values from 0 to 31
Outputs:
- mixed: bfloat16 [64, 256, 768], P('ep', 'sp')
- d_tokens: float32 [64, 256, 768], P('ep', 'sp')
- grad_w_query: float32 [768, 768], P(('sp', 'ep'))
- grad_w_key: float32 [768, 768], P(('sp', 'ep'))
- grad_w_value: float32 [768, 768], P(('sp', 'ep'))
- grad_w_output: float32 [768, 768], P(('sp', 'ep'))
- grad_gain_attn: float32 [768], P(('sp', 'ep'))
- grad_gain_ffn: float32 [768], P(('sp', 'ep'))
- grad_router: float32 [768, 64], P(('sp', 'ep'))
- grad_bias_table: float32 [384], P(('sp', 'ep'))
- grad_w_in: float32 [64, 768, 3072], P('ep', None, 'sp')
- grad_w_out: float32 [64, 3072, 768], P('ep', 'sp')
The draws below stay inside these ranges and needn't reach their ends.
Inputs may be any that keep to these rules, and one draw needn't show every extreme that they name: `routes`: each row names two different experts; in the rows of one device (aligned blocks of 128 tokens in the order of sequences and positions) no expert is named by more than 6 rows.
All inputs are finite; a program needn't handle non-finite values.
Results may differ from the reference program's by a relative error of at most 0.024.
Values may be sent and summed in bfloat16 or wider, within the bound.
A program may use at most 192 MiB of HBM per device.

```python
import math
import jax
import jax.numpy as jnp
import numpy as np
from jax import lax

D = 768
H = 12
HD = 64
FF = 3072
NB = 32
TOK_DEV = 128
SEQ = 256
SEQS = 64
TOKENS = 16384
EXPERTS = 64
CAP = 6
N_SP = 2
N_EP = 64


def touch_ends(drawn, own_key, low, largest):
    longest = drawn.shape.index(max(drawn.shape))
    spots = []
    for shift in (0, 1):
        where = [jax.random.randint(jax.random.fold_in(own_key, axis), (), 0, length) for axis, length in enumerate(drawn.shape)]
        where[longest] = (where[longest] + shift) % drawn.shape[longest]
        spots.append(tuple(where))
    return drawn.at[spots[0]].set(low).at[spots[1]].set(largest)


def level_of(rng, dims, cuts, low, largest):
    loudness = 1.0
    for axis_at, blocks in cuts:
        heights = jax.random.uniform(jax.random.fold_in(jax.random.fold_in(rng, 6), axis_at), (blocks,), jnp.float32, low / len(cuts), largest / len(cuts))
        loudness = loudness * jnp.repeat(jnp.exp(heights), dims[axis_at] // blocks).reshape((-1,) + (1,) * (len(dims) - 1 - axis_at))
    return loudness


def routed_block(key, own, number, rows, amount, top, limit, slope):
    sequence = jax.random.permutation(key, amount)
    heavy_load, usual = shares(amount, rows * top, limit, slope, True), shares(amount, rows * top, limit, slope, False)
    places = jnp.arange(amount)

    def named(lengths, turn):
        used = int((lengths > 0).sum())
        fixed = max(1, used // 4)
        shifted = fixed + (places - fixed + turn * (used - fixed)) % max(1, amount - fixed)
        return jnp.zeros((amount,), jnp.int32).at[sequence[jnp.where(places < fixed, places, shifted)]].set(jnp.asarray(lengths, jnp.int32))

    lengths = jnp.where(number % 4 == 0, named(heavy_load, number // 4), named(usual, number - number // 4 - 1))
    mixed = jax.random.permutation(jax.random.fold_in(own, 3), amount)
    giver, receiver = mixed[0:amount // 2 * 2:2], mixed[1:amount // 2 * 2:2]
    margin = jnp.minimum(lengths[giver] - 1, limit - lengths[receiver]) // 2
    margin = jnp.where((giver == sequence[0]) | (receiver == sequence[0]) | (lengths[receiver] == 0), 0, jnp.maximum(margin, 0))
    shifted = jax.random.randint(jax.random.fold_in(own, 4), (amount // 2,), 0, 1 << 20) % (margin + 1)
    lengths = lengths.at[giver].add(-shifted).at[receiver].add(shifted)
    items = jnp.searchsorted(jnp.cumsum(lengths), jnp.arange(rows * top), side="right").astype(jnp.int32)
    listing = items.reshape(top, rows).T
    listing = listing[jax.random.permutation(jax.random.fold_in(own, 1), rows)]
    turn = jax.random.randint(jax.random.fold_in(own, 2), (rows, 1), 0, top)
    return jnp.take_along_axis(listing, (jnp.arange(top)[None, :] + turn) % top, axis=1)


def shares(number_of, total, limit, lean, full):
    portions = [(1 << 20) // math.isqrt(standing ** lean) + 1 for standing in range(1, number_of + 1)]
    largest = limit if full else min(limit, max(-(-total // number_of), total * portions[0] // sum(portions)))
    least = 1 if total - largest >= number_of - 1 else 0
    counts, spare = [largest] + [least] * (number_of - 1), total - largest - least * (number_of - 1)
    while spare > 0:
        free = [i for i in range(1, number_of) if counts[i] < largest] or [i for i in range(1, number_of) if counts[i] < limit]
        whole, left = sum([portions[i] for i in free]), spare
        for i in free:
            addition = min(limit - counts[i], max(1, left * portions[i] // whole), spare)
            counts[i] = counts[i] + addition
            spare = spare - addition
    return np.array(counts)


def normal_values(own_key, extent, scale, reach, pieces=(), kind=jnp.bfloat16):
    level = level_of(own_key, extent, pieces, -0.22, 0.18) if pieces else 1.0
    values = jax.random.normal(own_key, extent, jnp.float32) * scale * level
    return jnp.minimum(jnp.maximum(values, -reach), reach).astype(kind)


def setup_inputs(seed: int = 0) -> dict:
    splits = jax.random.split(jax.random.key(seed), 15)
    tokens = normal_values(splits[0], (SEQS, SEQ, D), 1.0, 6.0, ((0, 64), (1, 2)))
    cotangent = normal_values(splits[1], (SEQS, SEQ, D), 1.0, 6.0, ((0, 64), (1, 2)))
    w_query = normal_values(splits[2], (D, D), D ** -0.5, 0.21875, ((0, 128),))
    w_key = normal_values(splits[3], (D, D), D ** -0.5, 0.21875, ((0, 128),))
    w_value = normal_values(splits[4], (D, D), D ** -0.5, 0.21875, ((0, 128),))
    w_output = normal_values(splits[5], (D, D), (D // 32) ** -0.5, 1.25, ((0, 128),))
    gain_attn = jnp.clip(1.0 + 0.15 * jax.random.normal(splits[6], (D,), jnp.float32), 0.25, 1.75).astype(jnp.bfloat16)
    gain_ffn = jnp.clip(1.0 + 0.15 * jax.random.normal(splits[7], (D,), jnp.float32), 0.25, 1.75).astype(jnp.bfloat16)
    router = normal_values(splits[8], (D, EXPERTS), (2 * D) ** -0.5, 0.15625, ((0, 128),))
    bias_table = normal_values(splits[9], (NB * H,), 1.0, 4.0, ((0, 128),))
    w_in = normal_values(splits[10], (EXPERTS, D, FF), D ** -0.5, 0.21875, ((0, 64), (2, 2)))
    w_out = normal_values(splits[11], (EXPERTS, FF, D), FF ** -0.5, 0.109375, ((0, 64), (1, 2)))
    routes_keys = jax.random.split(jax.random.fold_in(splits[12], 1), SEQS * SEQ // TOK_DEV)
    routes_turns = jax.random.permutation(jax.random.fold_in(splits[12], 3), SEQS * SEQ // TOK_DEV)
    routes = jax.vmap(lambda own, number: routed_block(jax.random.fold_in(splits[12], 2), own, number, TOK_DEV, EXPERTS, 2, CAP, 1))(routes_keys, routes_turns).reshape((SEQS, SEQ, 2))
    buckets = touch_ends(jax.random.randint(splits[13], (SEQ,), 0, NB), jax.random.fold_in(splits[13], 1), 0, NB - 1).astype(jnp.int32)
    return {"tokens": tokens, "cotangent": cotangent, "w_query": w_query, "w_key": w_key, "w_value": w_value, "w_output": w_output, "gain_attn": gain_attn, "gain_ffn": gain_ffn, "router": router, "bias_table": bias_table, "w_in": w_in, "w_out": w_out, "routes": routes, "buckets": buckets}


@jax.custom_vjp
def low(v):
    return lax.optimization_barrier(v.astype(jnp.bfloat16)).astype(jnp.float32)

@jax.custom_vjp
def low_back(v):
    return v

def low_keep(v):
    return (low(v), None)

def low_pass(kept, grad):
    return (grad,)

def back_keep(v):
    return (v, None)

def back_low(kept, grad):
    return (low(grad),)
low.defvjp(low_keep, low_pass)
low_back.defvjp(back_keep, back_low)
epsilon = 1e-06
highest = lax.Precision.HIGHEST

def rms_norm(values, gain):
    return values * lax.rsqrt(lax.optimization_barrier(jnp.mean(values * values, axis=-1, keepdims=True)) + epsilon) * gain

def dense(left, right):
    return jnp.dot(left, right, precision=highest)

def reference(tokens, cotangent, w_query, w_key, w_value, w_output, gain_attn, gain_ffn, router, bias_table, w_in, w_out, routes, buckets):
    device_count = N_SP * N_EP
    scaling = HD ** (-0.5)
    flat_routes = routes.reshape(device_count, 2 * TOK_DEV).astype(jnp.int32)
    onehot = (flat_routes[:, :, None] == jnp.arange(EXPERTS, dtype=jnp.int32)[None, None, :]).astype(jnp.int32)
    ranking = lax.optimization_barrier(jnp.sum((jnp.cumsum(onehot, axis=1) - 1) * onehot, axis=2))
    position = flat_routes * (device_count * CAP) + jnp.arange(device_count, dtype=jnp.int32)[:, None] * CAP + ranking
    position = position.reshape(-1).astype(jnp.int32)
    picked = (routes.reshape(TOKENS, 2)[:, :, None] == jnp.arange(EXPERTS, dtype=jnp.int32)[None, None, :]).astype(jnp.float32)
    places = jnp.arange(SEQ, dtype=jnp.int32)
    relative = jnp.maximum(places[:, None] - places[None, :], 0)
    causal = places[None, :] <= places[:, None]

    def forward(inputs, query_weight, key_weight, value_weight, output_weight, norm_attn, norm_ffn, router_weight, table, first_weights, second_weights):
        normed = low(rms_norm(inputs, norm_attn))

        def project(weight):
            return low(low_back(dense(normed, weight))).reshape(SEQS, SEQ, H, HD)
        queries = project(query_weight)
        keys_all = project(key_weight)
        values_all = project(value_weight)
        per_distance = table.reshape(NB, H)[buckets]
        bias = jnp.transpose(per_distance[relative], (2, 0, 1))

        def attend(block):
            q_block, k_block, v_block = block
            scores = jnp.einsum('qhd,khd->hqk', q_block, k_block, precision=highest) * scaling + bias
            scores = low_back(jnp.where(causal[None], scores, -jnp.inf))
            probs = low(jax.nn.softmax(scores, axis=-1))
            return jnp.einsum('hqk,khd->qhd', probs, v_block, precision=highest)
        attended = lax.map(jax.checkpoint(attend), (queries, keys_all, values_all)).reshape(TOKENS, D)
        attended = low(low_back(attended))
        branch = low_back(dense(attended, output_weight))
        resid = inputs + branch
        normed_ffn = low(rms_norm(resid, norm_ffn))
        logits = low_back(dense(normed_ffn, router_weight))
        chosen = jnp.einsum('te,tke->tk', logits, picked, precision=highest)
        gates = jax.nn.softmax(chosen, axis=-1)
        repeated = jnp.repeat(normed_ffn, 2, axis=0)
        buffer = jnp.zeros((EXPERTS * device_count * CAP, D), jnp.float32).at[position].set(repeated)
        buffer = buffer.reshape(EXPERTS, device_count * CAP, D)

        def expert(block):
            rows_in, first, second = block
            pre = low_back(dense(rows_in, first))
            return dense(low(jax.nn.gelu(pre)), second)
        produced = lax.map(jax.checkpoint(expert), (buffer, first_weights, second_weights)).reshape(-1, D)
        expert_out = low_back(produced[position]).reshape(TOKENS, 2, D)
        return resid + lax.optimization_barrier(jnp.sum(gates[:, :, None] * expert_out, axis=1))
    floats = (tokens.reshape(TOKENS, D).astype(jnp.float32), w_query.astype(jnp.float32), w_key.astype(jnp.float32), w_value.astype(jnp.float32), w_output.astype(jnp.float32), gain_attn.astype(jnp.float32), gain_ffn.astype(jnp.float32), router.astype(jnp.float32), bias_table.astype(jnp.float32), w_in.astype(jnp.float32), w_out.astype(jnp.float32))
    outputs, pullback = jax.vjp(forward, *floats)
    grads = pullback(cotangent.reshape(TOKENS, D).astype(jnp.float32))
    return (outputs.reshape(SEQS, SEQ, D).astype(jnp.bfloat16), grads[0].reshape(SEQS, SEQ, D), grads[1], grads[2], grads[3], grads[4], grads[5], grads[6], grads[7], grads[8], grads[9], grads[10])
```

```python
import functools

import jax
import jax.numpy as jnp
from jax import lax
from jax.experimental import pallas as pl
from jax.experimental.pallas import tpu as pltpu
from jax.sharding import PartitionSpec as P

D = 768
H = 12
HD = 64
HH = H // 2
HW = HH * HD
EXP = 64
EPS = 1e-06
SLOT = 8
QROW = 16
QW = 3 * HW
PW = QW + 128
ROUTER = QW
GAIN = QW + 64
F32 = jnp.float32
BF16 = jnp.bfloat16
VMEM_LIMIT = 56 * 1024 * 1024


def iota(shape, axis):
    return lax.broadcasted_iota(jnp.int32, shape, axis)


def nn(left, right):
    return lax.dot_general(left, right, (((1,), (0,)), ((), ())), preferred_element_type=F32)


def nt(left, right):
    return lax.dot_general(left, right, (((1,), (1,)), ((), ())), preferred_element_type=F32)


def tn(left, right):
    return lax.dot_general(left, right, (((0,), (0,)), ((), ())), preferred_element_type=F32)


def chunk_feature(rows):
    owner = jnp.right_shift(rows, 4)
    inner = jnp.bitwise_and(rows, 15)
    half = (inner >= 6).astype(jnp.int32)
    feature = half * (D // 2) + owner * 6 + inner - 6 * half
    return jnp.where(inner < 12, feature, -1)


def chunk_entry(rows):
    owner = jnp.right_shift(rows, 4)
    inner = jnp.bitwise_and(rows, 15)
    half = (inner >= 6).astype(jnp.int32)
    inside = inner - 6 * half
    entry = half * (32 * H // 2) + owner * 3 + inside
    return jnp.where((inner < 12) & (inside < 3), entry, -1)


def hot(condition):
    return jnp.where(condition, 1.0, 0.0).astype(BF16)


def to_chunks():
    rows = iota((D, EXP * QROW), 1)
    return hot(chunk_feature(rows) == iota((D, EXP * QROW), 0))


def from_chunks():
    rows = iota((EXP * QROW, D), 0)
    return hot(chunk_feature(rows) == iota((EXP * QROW, D), 1))


def rms_of(values):
    return lax.rsqrt(jnp.mean(values * values, axis=-1, keepdims=True) + EPS)


def head_bias(bias_ref, head, seq):
    row = jnp.broadcast_to(bias_ref[head : head + 1, :], (seq, seq))
    return pltpu.roll(row, 0, 1, stride=1, stride_axis=0)


def first_kernel(seq_ref, pack_ref, bucket_ref, attended_ref, qkv_ref, full_ref, gains_ref, normed_ref, bias_ref, lse_ref):
    seq = seq_ref.shape[0]
    sp = lax.axis_index("sp")
    spread = to_chunks()
    full_ref[...] = nn(spread, pack_ref[...]).astype(BF16)
    tail = pack_ref[:, QW:]
    gains = tn(tail, from_chunks())
    gains_ref[...] = gains
    rows = iota((EXP * QROW, 128), 0)
    entry = chunk_entry(rows)
    bucket_of = jnp.right_shift(entry * 5462, 16)
    head_of = entry - bucket_of * H
    column = iota((EXP * QROW, 128), 1)
    table = jnp.where(
        (entry >= 0) & (head_of == sp * HH + column) & (column < HH),
        tail[:, 66:67].astype(F32),
        0.0,
    ).astype(BF16)
    entry_wide = chunk_entry(iota((EXP * QROW, seq), 0))
    bucket_wide = jnp.where(entry_wide >= 0, jnp.right_shift(entry_wide * 5462, 16), -1)
    bias_ref[...] = tn(table, hot(bucket_wide == bucket_ref[0:1, :]))[0:8, :]

    inputs = seq_ref[...].astype(F32)
    normed = (inputs * rms_of(inputs) * gains[64:65, :]).astype(BF16)
    normed_ref[...] = normed
    qkv_ref[...] = nn(normed, full_ref[:, :QW]).astype(BF16)
    causal = iota((seq, seq), 1) <= iota((seq, seq), 0)
    lse_ref[...] = jnp.zeros_like(lse_ref)
    for head in range(HH):
        at = head * HD
        query = qkv_ref[:, at : at + HD]
        key = qkv_ref[:, HW + at : HW + at + HD]
        value = qkv_ref[:, 2 * HW + at : 2 * HW + at + HD]
        scores = nt(query, key) * (HD**-0.5) + head_bias(bias_ref, head, seq)
        scores = jnp.where(causal, scores, -jnp.inf)
        peak = jnp.max(scores, axis=-1, keepdims=True)
        grown = jnp.exp(scores - peak)
        total = jnp.sum(grown, axis=-1, keepdims=True)
        probs = (grown / total).astype(BF16)
        attended_ref[:, at : at + HD] = nn(probs, value).astype(BF16)
        lse_ref[:, head : head + 1] = peak + jnp.log(total)


def route_hot(routes_ref, k, width):
    return (routes_ref[:, k : k + 1] == iota((routes_ref.shape[0], width), 1)).astype(F32)


def middle_kernel(parts_ref, tok_ref, cot_ref, gains_ref, full_ref, routes_ref, filled_ref, resid_ref, normed_ref, places_ref, gates_ref):
    count = tok_ref.shape[0]
    resid = tok_ref[...].astype(F32) + parts_ref[:count, :] + parts_ref[count:, :]
    resid_ref[...] = resid
    normed = (resid * rms_of(resid) * gains_ref[65:66, :]).astype(BF16)
    normed_ref[...] = normed
    logits = nn(normed, full_ref[:, ROUTER : ROUTER + EXP])
    named = [route_hot(routes_ref, k, EXP) for k in range(2)]
    chosen = [jnp.sum(logits * one, axis=-1, keepdims=True) for one in named]
    peak = jnp.maximum(chosen[0], chosen[1])
    grown = [jnp.exp(one - peak) for one in chosen]
    total = grown[0] + grown[1]
    gates = [one / total for one in grown]
    column = iota((count, 128), 1)
    gates_ref[...] = jnp.where(column == 0, gates[0], jnp.where(column == 1, gates[1], 0.0))
    before = hot(iota((count, count), 1) < iota((count, count), 0))
    earlier = nn(before, (named[0] + named[1]).astype(BF16))
    upstream = cot_ref[...].astype(F32)
    slots = iota((count, EXP * SLOT), 1)
    filled_d = jnp.zeros((EXP * SLOT, D), F32)
    either = jnp.zeros((count, EXP * SLOT), F32)
    for k in range(2):
        rank = jnp.sum(earlier * named[k], axis=-1, keepdims=True).astype(jnp.int32)
        place = (slots == routes_ref[:, k : k + 1] * SLOT + rank).astype(F32)
        either = either + place
        places_ref[:, k * EXP * SLOT : (k + 1) * EXP * SLOT] = place.astype(BF16)
        filled_d = filled_d + tn(place.astype(BF16), (gates[k] * upstream).astype(BF16))
    filled_ref[:, :D] = tn(either.astype(BF16), normed).astype(BF16)
    filled_ref[:, D:] = filled_d.astype(BF16)


def expert_kernel(rows_ref, win_ref, wout_ref, result_ref, act_ref, dpre_ref, out_acc, back_acc):
    step = pl.program_id(0)

    @pl.when(step == 0)
    def _():
        out_acc[...] = jnp.zeros_like(out_acc)
        back_acc[...] = jnp.zeros_like(back_acc)

    first = win_ref[...]
    second = wout_ref[...]
    pre = nn(rows_ref[:, :D], first)
    square = pre * pre
    slope = 0.7978845608028654
    t = jnp.tanh(slope * (pre + 0.044715 * (square * pre)))
    half = 0.5 * (1.0 + t)
    act = (pre * half).astype(BF16)
    act_ref[...] = act
    out_acc[...] += nn(act, second)
    d_act = nt(rows_ref[:, D:], second)
    bend = half + 0.5 * pre * (1.0 - t * t) * (slope * (1.0 + 3 * 0.044715 * square))
    d_pre = (d_act * bend).astype(BF16)
    dpre_ref[...] = d_pre
    back_acc[...] += nt(d_pre, first)

    @pl.when(step == pl.num_programs(0) - 1)
    def _():
        result_ref[:, :D] = out_acc[...].astype(BF16)
        result_ref[:, D:] = back_acc[...].astype(BF16)


def expert_grad_kernel(rows_ref, act_ref, dpre_ref, gin_ref, gout_ref, turned):
    @pl.when(pl.program_id(0) == 0)
    def _():
        turned[...] = rows_ref[:, :D].T

    gin_ref[0] = nn(turned[...], dpre_ref[...])
    gout_ref[0] = tn(act_ref[...], rows_ref[:, D:])


def mix_kernel(ret_ref, places_ref, gates_ref, resid_ref, cot_ref, gains_ref, full_ref, normed_ref, routes_ref, mixed_ref, dresid_ref, dbranch_ref, grouter_ref, ggain_ref):
    count = resid_ref.shape[0]
    slots = EXP * SLOT
    resid = resid_ref[...]
    upstream = cot_ref[...].astype(F32)
    gates = [gates_ref[:, k : k + 1] for k in range(2)]
    outs = [nn(places_ref[:, k * slots : (k + 1) * slots], ret_ref[:, :D]) for k in range(2)]
    mixed_ref[0] = (resid + (gates[0] * outs[0] + gates[1] * outs[1])).astype(BF16)
    d_gates = [jnp.sum(one * upstream, axis=-1, keepdims=True) for one in outs]
    inner = gates[0] * d_gates[0] + gates[1] * d_gates[1]
    d_logits = jnp.zeros((count, EXP), F32)
    for k in range(2):
        d_logits = d_logits + route_hot(routes_ref, k, EXP) * (gates[k] * (d_gates[k] - inner))
    d_logits = d_logits.astype(BF16)
    either = places_ref[:, :slots] + places_ref[:, slots:]
    d_normed = nn(either, ret_ref[:, D:]) + nt(d_logits, full_ref[:, ROUTER : ROUTER + EXP])
    chunked = nn(normed_ref[...], to_chunks()).astype(BF16)
    grouter_ref[...] = tn(chunked, d_logits)
    rms = rms_of(resid)
    u = d_normed * gains_ref[65:66, :]
    d_resid = upstream + rms * u - resid * (rms * rms * rms) * jnp.mean(u * resid, axis=-1, keepdims=True)
    ggain_ref[...] = jnp.broadcast_to(jnp.sum(d_normed * resid * rms, axis=0, keepdims=True), ggain_ref.shape)
    dresid_ref[...] = d_resid
    dbranch_ref[...] = d_resid.astype(BF16)


def split_two(values):
    high = values.astype(BF16)
    return high, (values - high.astype(F32)).astype(BF16)


def last_kernel(branch_ref, wo_ref, qkv_ref, lse_ref, bias_ref, normed_ref, seq_ref, full_ref, bucket_ref, grouter_ref, gffn_ref, pack_ref, dnorm_ref, dqkv, ddist):
    seq = seq_ref.shape[0]
    sp = lax.axis_index("sp")
    d_attended = nt(branch_ref[...], wo_ref[...]).astype(BF16)
    causal = iota((seq, seq), 1) <= iota((seq, seq), 0)
    flip = hot(iota((seq, seq), 0) + iota((seq, seq), 1) == seq - 1)
    ddist[...] = jnp.zeros_like(ddist)
    for head in range(HH):
        at = head * HD
        query = qkv_ref[:, at : at + HD]
        key = qkv_ref[:, HW + at : HW + at + HD]
        value = qkv_ref[:, 2 * HW + at : 2 * HW + at + HD]
        d_out = d_attended[:, at : at + HD]
        scores = nt(query, key) * (HD**-0.5) + head_bias(bias_ref, head, seq)
        probs = jnp.where(causal, jnp.exp(scores - lse_ref[:, head : head + 1]), 0.0)
        d_value = tn(probs.astype(BF16), d_out)
        d_probs = nt(d_out, value)
        row_dot = jnp.sum(probs * d_probs, axis=-1, keepdims=True)
        d_scores = (probs * (d_probs - row_dot)).astype(BF16)
        dqkv[:, at : at + HD] = (nn(d_scores, key) * (HD**-0.5)).astype(BF16)
        dqkv[:, HW + at : HW + at + HD] = (tn(d_scores, query) * (HD**-0.5)).astype(BF16)
        dqkv[:, 2 * HW + at : 2 * HW + at + HD] = d_value.astype(BF16)
        skewed = pltpu.roll(nn(d_scores, flip), 0, 1, stride=1, stride_axis=0)
        ddist[head : head + 1, :] = jnp.sum(skewed, axis=0, keepdims=True)
    d_normed = nt(dqkv[...], full_ref[:, :QW])
    dnorm_ref[...] = d_normed
    chunked = nn(normed_ref[...], to_chunks()).astype(BF16)
    turned = chunked.T
    pack_ref[:, :QW] = nn(turned, dqkv[...]).astype(BF16)
    inputs = seq_ref[...].astype(F32)
    g_first = jnp.sum(d_normed * inputs * rms_of(inputs), axis=0, keepdims=True)
    order = from_chunks()
    first_high, first_low = split_two(jnp.broadcast_to(g_first, (16, D)))
    second_high, second_low = split_two(jnp.broadcast_to(gffn_ref[0:1, :], (16, D)))
    gains = [nt(order, one)[:, 0:1] for one in (first_high, first_low, second_high, second_low)]
    rows = iota((EXP * QROW, seq), 0)
    entry = chunk_entry(rows)
    bucket_wide = jnp.where(entry >= 0, jnp.right_shift(entry * 5462, 16), -1)
    pick = hot(bucket_wide == bucket_ref[1:2, :])
    high, low = split_two(ddist[...])
    by_head = nt(pick, high) + nt(pick, low)
    entry = chunk_entry(iota(by_head.shape, 0))
    head_of = entry - jnp.right_shift(entry * 5462, 16) * H
    mine = (entry >= 0) & (head_of == sp * HH + iota(by_head.shape, 1)) & (iota(by_head.shape, 1) < HH)
    table = jnp.sum(jnp.where(mine, by_head, 0.0), axis=-1, keepdims=True)
    table_high, table_low = split_two(table)
    column = iota((EXP * QROW, 64), 1)
    tail = jnp.zeros((EXP * QROW, 64), F32)
    for place, values in enumerate(gains + [table_high.astype(F32), table_low.astype(F32)]):
        tail = jnp.where(column == place, values, tail)
    pack_ref[:, QW:] = jnp.concatenate([grouter_ref[...], tail], axis=1).astype(BF16)


def end_kernel(parts_ref, dresid_ref, tok_ref, gains_ref, out_ref):
    count = tok_ref.shape[0]
    inputs = tok_ref[...].astype(F32)
    d_normed = parts_ref[:count, :] + parts_ref[count:, :]
    rms = rms_of(inputs)
    v = d_normed * gains_ref[64:65, :]
    out_ref[0] = dresid_ref[...] + rms * v - inputs * (rms * rms * rms) * jnp.mean(v * inputs, axis=-1, keepdims=True)


def whole(kernel, outs, scratch=(), flops=0, moved=0):
    return pl.pallas_call(
        kernel,
        out_shape=[jax.ShapeDtypeStruct(shape, kind) for shape, kind in outs],
        scratch_shapes=list(scratch),
        compiler_params=pltpu.CompilerParams(vmem_limit_bytes=VMEM_LIMIT),
        cost_estimate=pl.CostEstimate(flops=flops, bytes_accessed=moved, transcendentals=0),
    )


def swap(values, axis="sp"):
    return lax.all_to_all(values, axis, split_axis=0, concat_axis=0, tiled=True)


def shards(tokens, cotangent, w_query, w_key, w_value, w_output, gain_attn, gain_ffn, router, bias_table, w_in, w_out, routes, buckets):
    count = tokens.shape[1]
    seq = 2 * count
    owners = lax.axis_size("ep")
    tok = tokens[0]
    cot = cotangent[0]
    route = routes[0]
    qkv = jnp.concatenate([w_query, w_key, w_value], axis=1).reshape(6, 3, 2, HW)
    qkv = qkv.transpose(2, 0, 1, 3).reshape(2, 6, QW)
    tail = jnp.concatenate(
        [
            router,
            gain_attn[:, None],
            gain_ffn[:, None],
            jnp.pad(bias_table, (0, 3))[:, None],
            jnp.zeros((6, 61), BF16),
        ],
        axis=1,
    )
    chunk = jnp.concatenate([qkv, jnp.broadcast_to(tail[None], (2, 6, 128))], axis=2)
    chunk = jnp.pad(swap(chunk).reshape(12, PW), ((0, QROW - 12), (0, 0)))
    pack = swap(jnp.broadcast_to(chunk[None], (owners, QROW, PW)), "ep").reshape(owners * QROW, PW)
    out_chunk = jnp.pad(w_output, ((0, SLOT - 6), (0, 0)))
    out_pack = swap(jnp.broadcast_to(out_chunk[None], (owners, SLOT, D)), "ep").reshape(owners * SLOT, D)
    sequence = swap(jnp.broadcast_to(tok[None], (2, count, D))).reshape(seq, D)
    turned_buckets = jnp.stack([jnp.roll(buckets[::-1], 1), jnp.roll(buckets, -1)])

    attended, qkv_all, full, gains, normed_attn, bias, lse = whole(
        first_kernel,
        [
            ((seq, HW), BF16),
            ((seq, QW), BF16),
            ((D, PW), BF16),
            ((128, D), F32),
            ((seq, D), BF16),
            ((8, seq), F32),
            ((seq, 128), F32),
        ],
        flops=4 * 10**9,
        moved=8 * 10**6,
    )(sequence, pack, turned_buckets)

    place = jnp.arange(owners * SLOT, dtype=jnp.int32)
    owner_row = jnp.where(place % SLOT < 6, place // SLOT * 6 + place % SLOT, -1)
    gather_rows = (owner_row[None, :] == jnp.arange(HW, dtype=jnp.int32)[:, None]).astype(BF16)
    output_mine = nn(gather_rows, out_pack).astype(BF16)
    branch = nn(attended, output_mine)
    parts = swap(branch.reshape(2, count, D)).reshape(seq, D)

    filled, resid, normed_ffn, places, gates = whole(
        middle_kernel,
        [
            ((EXP * SLOT, 2 * D), BF16),
            ((count, D), F32),
            ((count, D), BF16),
            ((count, 2 * EXP * SLOT), BF16),
            ((count, 128), F32),
        ],
        flops=10**9,
        moved=4 * 10**6,
    )(parts, tok, cot, gains, full, route)

    arrived = swap(filled.reshape(owners, SLOT, 2 * D), "ep")
    rows = swap(jnp.broadcast_to(arrived.reshape(1, owners * SLOT, 2 * D), (2, owners * SLOT, 2 * D)))
    rows = rows.reshape(2 * owners * SLOT, 2 * D)
    load = rows.shape[0]
    hidden = w_in.shape[2]
    step = 256
    resident = pl.BlockSpec((load, 2 * D), lambda f: (0, 0))
    by_column = pl.BlockSpec((load, step), lambda f: (0, f))
    result, act, d_pre = pl.pallas_call(
        expert_kernel,
        grid=(hidden // step,),
        in_specs=[
            resident,
            pl.BlockSpec((D, step), lambda f: (0, f)),
            pl.BlockSpec((step, D), lambda f: (f, 0)),
        ],
        out_specs=[resident, by_column, by_column],
        out_shape=[
            jax.ShapeDtypeStruct((load, 2 * D), BF16),
            jax.ShapeDtypeStruct((load, hidden), BF16),
            jax.ShapeDtypeStruct((load, hidden), BF16),
        ],
        scratch_shapes=[pltpu.VMEM((load, D), F32), pltpu.VMEM((load, D), F32)],
        compiler_params=pltpu.CompilerParams(vmem_limit_bytes=VMEM_LIMIT),
        cost_estimate=pl.CostEstimate(flops=8 * load * D * hidden, bytes_accessed=20 * 10**6, transcendentals=load * hidden),
    )(rows, w_in[0], w_out[0])
    halves = swap(result.reshape(2, owners * SLOT, 2 * D))
    joined = (halves[0].astype(F32) + halves[1].astype(F32)).astype(BF16)
    returned = swap(joined.reshape(owners, SLOT, 2 * D), "ep").reshape(owners * SLOT, 2 * D)

    grad_w_in, grad_w_out = pl.pallas_call(
        expert_grad_kernel,
        grid=(hidden // step,),
        in_specs=[resident, by_column, by_column],
        out_specs=[
            pl.BlockSpec((1, D, step), lambda f: (0, 0, f)),
            pl.BlockSpec((1, step, D), lambda f: (0, f, 0)),
        ],
        out_shape=[
            jax.ShapeDtypeStruct((1, D, hidden), F32),
            jax.ShapeDtypeStruct((1, hidden, D), F32),
        ],
        scratch_shapes=[pltpu.VMEM((D, load), BF16)],
        compiler_params=pltpu.CompilerParams(vmem_limit_bytes=VMEM_LIMIT),
        cost_estimate=pl.CostEstimate(flops=4 * load * D * hidden, bytes_accessed=20 * 10**6, transcendentals=0),
    )(rows, act, d_pre)

    mixed, d_resid, d_branch, g_router, g_ffn = whole(
        mix_kernel,
        [
            ((1, count, D), BF16),
            ((count, D), F32),
            ((count, D), BF16),
            ((owners * QROW, EXP), F32),
            ((8, D), F32),
        ],
        flops=10**9,
        moved=5 * 10**6,
    )(returned, places, gates, resid, cot, gains, full, normed_ffn, route)

    branch_seq = swap(jnp.broadcast_to(d_branch[None], (2, count, D))).reshape(seq, D)
    chunked = nn(attended, gather_rows).astype(BF16)
    g_output = tn(chunked, branch_seq).astype(BF16)
    g_output = swap(g_output.reshape(owners, SLOT, D), "ep")

    g_pack, d_norm = whole(
        last_kernel,
        [((owners * QROW, PW), BF16), ((seq, D), F32)],
        scratch=[pltpu.VMEM((seq, QW), BF16), pltpu.VMEM((8, seq), F32)],
        flops=5 * 10**9,
        moved=10 * 10**6,
    )(branch_seq, output_mine, qkv_all, lse, bias, normed_attn, sequence, full, turned_buckets, g_router, g_ffn)

    g_pack = swap(g_pack.reshape(owners, QROW, PW), "ep")
    d_parts = swap(d_norm.reshape(2, count, D)).reshape(seq, D)
    (d_tokens,) = whole(end_kernel, [((1, count, D), F32)], flops=10**6, moved=10**6)(d_parts, d_resid, tok, gains)

    grad_w_output = jnp.sum(g_output.astype(F32), axis=0)[:6]
    summed = jnp.sum(g_pack.astype(F32), axis=0)[:12].reshape(2, 6, PW)
    summed = swap(summed)
    weights = summed[:, :, :QW].reshape(2, 6, 3, HW).transpose(2, 1, 0, 3).reshape(3, 6, D)
    both = summed[0, :, QW:] + summed[1, :, QW:]
    extra = both[:, 64:70]
    return (
        mixed,
        d_tokens,
        weights[0],
        weights[1],
        weights[2],
        grad_w_output,
        extra[:, 0] + extra[:, 1],
        extra[:, 2] + extra[:, 3],
        both[:, :EXP],
        (extra[:, 4] + extra[:, 5])[:3],
        grad_w_in,
        grad_w_out,
    )


def solution(mesh):
    wide = P(("sp", "ep"), None)
    flat = P(("sp", "ep"))
    rows = P("ep", "sp", None)
    return jax.shard_map(
        shards,
        mesh=mesh,
        in_specs=(rows, rows, wide, wide, wide, wide, flat, flat, wide, flat, P("ep", None, "sp"), rows, rows, P()),
        out_specs=(rows, rows, wide, wide, wide, wide, flat, flat, wide, flat, P("ep", None, "sp"), rows),
        check_vma=False,
    )
```

```python
import functools

import jax
import jax.numpy as jnp
from jax import lax
from jax.experimental import pallas as pl
from jax.experimental.pallas import tpu as pltpu
from jax.sharding import PartitionSpec as P

D = 768
H = 12
HD = 64
HH = H // 2
HW = HH * HD
EXP = 64
EPS = 1e-06
SLOT = 8
QROW = 16
QW = 3 * HW
PW = QW + 128
SIDE = 4
STRIDES = (16, 4, 1)
PARTS = ((0, 512, (2, 1, 0)), (512, 384, (0, 2, 1)), (896, 384, (1, 0, 2)))
MESH = pl.DeviceIdType.MESH
ROUTER = QW
GAIN = QW + 64
F32 = jnp.float32
BF16 = jnp.bfloat16
VMEM_LIMIT = 56 * 1024 * 1024


def iota(shape, axis):
    return lax.broadcasted_iota(jnp.int32, shape, axis)


def nn(left, right):
    return lax.dot_general(left, right, (((1,), (0,)), ((), ())), preferred_element_type=F32)


def nt(left, right):
    return lax.dot_general(left, right, (((1,), (1,)), ((), ())), preferred_element_type=F32)


def tn(left, right):
    return lax.dot_general(left, right, (((0,), (0,)), ((), ())), preferred_element_type=F32)


def chunk_feature(rows):
    owner = jnp.right_shift(rows, 4)
    inner = jnp.bitwise_and(rows, 15)
    half = (inner >= 6).astype(jnp.int32)
    feature = half * (D // 2) + owner * 6 + inner - 6 * half
    return jnp.where(inner < 12, feature, -1)


def chunk_entry(rows):
    owner = jnp.right_shift(rows, 4)
    inner = jnp.bitwise_and(rows, 15)
    half = (inner >= 6).astype(jnp.int32)
    inside = inner - 6 * half
    entry = half * (32 * H // 2) + owner * 3 + inside
    return jnp.where((inner < 12) & (inside < 3), entry, -1)


def hot(condition):
    return jnp.where(condition, 1.0, 0.0).astype(BF16)


def to_chunks():
    return hot(chunk_feature(iota((1, EXP * QROW), 1)) == iota((D, EXP * QROW), 0))


def from_chunks():
    return hot(chunk_feature(iota((EXP * QROW, 1), 0)) == iota((EXP * QROW, D), 1))


def output_row(channel, half, third):
    owner = jnp.right_shift(channel * 10923, 16)
    inner = channel - owner * 6
    later = (inner >= 3).astype(jnp.int32)
    row = owner * QROW + 12 + 2 * later + half
    return jnp.where(inner - 3 * later == third, row, -1)


def rms_of(values):
    return lax.rsqrt(jnp.mean(values * values, axis=-1, keepdims=True) + EPS)


def head_bias(bias_ref, head, seq):
    row = jnp.broadcast_to(bias_ref[head : head + 1, :], (seq, seq))
    return pltpu.roll(row, 0, 1, stride=1, stride_axis=0)


def first_kernel(seq_ref, pack_ref, bucket_ref, branch_ref, output_ref, attended_ref, qkv_ref, full_ref, gains_ref, normed_ref, bias_ref, lse_ref):
    seq = seq_ref.shape[0]
    sp = lax.axis_index("sp")
    spread = to_chunks()
    full_ref[...] = nn(spread, pack_ref[...]).astype(BF16)
    tail = pack_ref[:, QW:]
    gains = tn(tail, from_chunks())
    gains_ref[...] = gains
    entry = chunk_entry(iota((EXP * QROW, 1), 0))
    bucket_of = jnp.right_shift(entry * 5462, 16)
    head_of = entry - bucket_of * H
    column = iota((EXP * QROW, 128), 1)
    table = jnp.where(
        (entry >= 0) & (head_of == sp * HH + column) & (column < HH),
        tail[:, 66:67].astype(F32),
        0.0,
    ).astype(BF16)
    bucket_here = jnp.where(entry >= 0, bucket_of, -1)
    bias_ref[...] = tn(table, hot(bucket_here == bucket_ref[0:1, :]))[0:8, :]
    channel = iota((HW, 1), 0)
    for half in range(2):
        rows = jnp.zeros((HW, HW), F32)
        for third in range(3):
            pick = hot(output_row(channel, half, third) == iota((HW, EXP * QROW), 1))
            rows = rows + nn(pick, pack_ref[:, third * HW : (third + 1) * HW])
        output_ref[:, half * HW : (half + 1) * HW] = rows.astype(BF16)

    inputs = seq_ref[...].astype(F32)
    normed = (inputs * rms_of(inputs) * gains[64:65, :]).astype(BF16)
    normed_ref[...] = normed
    qkv_ref[...] = nn(normed, full_ref[:, :QW]).astype(BF16)
    causal = iota((seq, seq), 1) <= iota((seq, seq), 0)
    lse_ref[...] = jnp.zeros_like(lse_ref)
    for head in range(HH):
        at = head * HD
        query = qkv_ref[:, at : at + HD]
        key = qkv_ref[:, HW + at : HW + at + HD]
        value = qkv_ref[:, 2 * HW + at : 2 * HW + at + HD]
        scores = nt(query, key) * (HD**-0.5) + head_bias(bias_ref, head, seq)
        scores = jnp.where(causal, scores, -jnp.inf)
        peak = jnp.max(scores, axis=-1, keepdims=True)
        grown = jnp.exp(scores - peak)
        total = jnp.sum(grown, axis=-1, keepdims=True)
        probs = (grown / total).astype(BF16)
        attended_ref[:, at : at + HD] = nn(probs, value).astype(BF16)
        lse_ref[:, head : head + 1] = peak + jnp.log(total)
    branch_ref[...] = nn(attended_ref[...], output_ref[...])


def route_hot(routes_ref, k, width):
    return (routes_ref[:, k : k + 1] == iota((routes_ref.shape[0], width), 1)).astype(F32)


def middle_kernel(parts_ref, tok_ref, cot_ref, gains_ref, full_ref, routes_ref, filled_ref, resid_ref, normed_ref, places_ref, gates_ref):
    count = tok_ref.shape[0]
    resid = tok_ref[...].astype(F32) + parts_ref[:count, :] + parts_ref[count:, :]
    resid_ref[...] = resid
    normed = (resid * rms_of(resid) * gains_ref[65:66, :]).astype(BF16)
    normed_ref[...] = normed
    logits = nn(normed, full_ref[:, ROUTER : ROUTER + EXP])
    named = [route_hot(routes_ref, k, EXP) for k in range(2)]
    chosen = [jnp.sum(logits * one, axis=-1, keepdims=True) for one in named]
    peak = jnp.maximum(chosen[0], chosen[1])
    grown = [jnp.exp(one - peak) for one in chosen]
    total = grown[0] + grown[1]
    gates = [one / total for one in grown]
    column = iota((count, 128), 1)
    gates_ref[...] = jnp.where(column == 0, gates[0], jnp.where(column == 1, gates[1], 0.0))
    before = hot(iota((count, count), 1) < iota((count, count), 0))
    earlier = nn(before, (named[0] + named[1]).astype(BF16))
    upstream = cot_ref[...].astype(F32)
    slots = iota((count, EXP * SLOT), 1)
    filled_d = jnp.zeros((EXP * SLOT, D), F32)
    either = jnp.zeros((count, EXP * SLOT), F32)
    for k in range(2):
        rank = jnp.sum(earlier * named[k], axis=-1, keepdims=True).astype(jnp.int32)
        place = (slots == routes_ref[:, k : k + 1] * SLOT + rank).astype(F32)
        either = either + place
        places_ref[:, k * EXP * SLOT : (k + 1) * EXP * SLOT] = place.astype(BF16)
        filled_d = filled_d + tn(place.astype(BF16), (gates[k] * upstream).astype(BF16))
    filled_ref[:, :D] = tn(either.astype(BF16), normed).astype(BF16)
    filled_ref[:, D:] = filled_d.astype(BF16)


def expert_kernel(rows_ref, win_ref, wout_ref, result_ref, act_ref, dpre_ref, out_acc, back_acc):
    step = pl.program_id(0)

    @pl.when(step == 0)
    def _():
        out_acc[...] = jnp.zeros_like(out_acc)
        back_acc[...] = jnp.zeros_like(back_acc)

    first = win_ref[...]
    second = wout_ref[...]
    pre = nn(rows_ref[:, :D], first)
    square = pre * pre
    slope = 0.7978845608028654
    t = jnp.tanh(slope * (pre + 0.044715 * (square * pre)))
    half = 0.5 * (1.0 + t)
    act = (pre * half).astype(BF16)
    act_ref[...] = act
    out_acc[...] += nn(act, second)
    d_act = nt(rows_ref[:, D:], second)
    bend = half + 0.5 * pre * (1.0 - t * t) * (slope * (1.0 + 3 * 0.044715 * square))
    d_pre = (d_act * bend).astype(BF16)
    dpre_ref[...] = d_pre
    back_acc[...] += nt(d_pre, first)

    @pl.when(step == pl.num_programs(0) - 1)
    def _():
        result_ref[:, :D] = out_acc[...].astype(BF16)
        result_ref[:, D:] = back_acc[...].astype(BF16)


def expert_grad_kernel(rows_ref, act_ref, dpre_ref, gin_ref, gout_ref, turned):
    @pl.when(pl.program_id(0) == 0)
    def _():
        turned[...] = rows_ref[:, :D].T

    gin_ref[0] = nn(turned[...], dpre_ref[...])
    gout_ref[0] = tn(act_ref[...], rows_ref[:, D:])


def mix_kernel(ret_ref, places_ref, gates_ref, resid_ref, cot_ref, gains_ref, full_ref, normed_ref, routes_ref, mixed_ref, dresid_ref, dbranch_ref, grouter_ref, ggain_ref):
    count = resid_ref.shape[0]
    slots = EXP * SLOT
    resid = resid_ref[...]
    upstream = cot_ref[...].astype(F32)
    gates = [gates_ref[:, k : k + 1] for k in range(2)]
    outs = [nn(places_ref[:, k * slots : (k + 1) * slots], ret_ref[:, :D]) for k in range(2)]
    mixed_ref[0] = (resid + (gates[0] * outs[0] + gates[1] * outs[1])).astype(BF16)
    d_gates = [jnp.sum(one * upstream, axis=-1, keepdims=True) for one in outs]
    inner = gates[0] * d_gates[0] + gates[1] * d_gates[1]
    d_logits = jnp.zeros((count, EXP), F32)
    for k in range(2):
        d_logits = d_logits + route_hot(routes_ref, k, EXP) * (gates[k] * (d_gates[k] - inner))
    d_logits = d_logits.astype(BF16)
    either = places_ref[:, :slots] + places_ref[:, slots:]
    d_normed = nn(either, ret_ref[:, D:]) + nt(d_logits, full_ref[:, ROUTER : ROUTER + EXP])
    chunked = nn(normed_ref[...], to_chunks()).astype(BF16)
    grouter_ref[...] = tn(chunked, d_logits)
    rms = rms_of(resid)
    u = d_normed * gains_ref[65:66, :]
    d_resid = upstream + rms * u - resid * (rms * rms * rms) * jnp.mean(u * resid, axis=-1, keepdims=True)
    ggain_ref[...] = jnp.broadcast_to(jnp.sum(d_normed * resid * rms, axis=0, keepdims=True), ggain_ref.shape)
    dresid_ref[...] = d_resid
    dbranch_ref[...] = d_resid.astype(BF16)


def split_two(values):
    high = values.astype(BF16)
    return high, (values - high.astype(F32)).astype(BF16)


def last_kernel(branch_ref, wo_ref, attended_ref, qkv_ref, lse_ref, bias_ref, normed_ref, seq_ref, full_ref, bucket_ref, grouter_ref, gffn_ref, pack_ref, dnorm_ref, dqkv, ddist):
    seq = seq_ref.shape[0]
    sp = lax.axis_index("sp")
    d_attended = nt(branch_ref[...], wo_ref[...]).astype(BF16)
    causal = iota((seq, seq), 1) <= iota((seq, seq), 0)
    flip = hot(iota((seq, seq), 0) + iota((seq, seq), 1) == seq - 1)
    ddist[...] = jnp.zeros_like(ddist)
    for head in range(HH):
        at = head * HD
        query = qkv_ref[:, at : at + HD]
        key = qkv_ref[:, HW + at : HW + at + HD]
        value = qkv_ref[:, 2 * HW + at : 2 * HW + at + HD]
        d_out = d_attended[:, at : at + HD]
        scores = nt(query, key) * (HD**-0.5) + head_bias(bias_ref, head, seq)
        probs = jnp.where(causal, jnp.exp(scores - lse_ref[:, head : head + 1]), 0.0)
        d_value = tn(probs.astype(BF16), d_out)
        d_probs = nt(d_out, value)
        row_dot = jnp.sum(probs * d_probs, axis=-1, keepdims=True)
        d_scores = (probs * (d_probs - row_dot)).astype(BF16)
        dqkv[:, at : at + HD] = (nn(d_scores, key) * (HD**-0.5)).astype(BF16)
        dqkv[:, HW + at : HW + at + HD] = (tn(d_scores, query) * (HD**-0.5)).astype(BF16)
        dqkv[:, 2 * HW + at : 2 * HW + at + HD] = d_value.astype(BF16)
        skewed = pltpu.roll(nn(d_scores, flip), 0, 1, stride=1, stride_axis=0)
        ddist[head : head + 1, :] = jnp.sum(skewed, axis=0, keepdims=True)
    d_normed = nt(dqkv[...], full_ref[:, :QW])
    dnorm_ref[...] = d_normed
    chunked = nn(normed_ref[...], to_chunks()).astype(BF16)
    turned = chunked.T
    g_output = tn(attended_ref[...], branch_ref[...]).astype(BF16)
    channel = iota((1, HW), 1)
    for third in range(3):
        there = slice(third * HW, (third + 1) * HW)
        total = nn(turned, dqkv[:, there])
        for half in range(2):
            place = hot(output_row(channel, half, third) == iota((EXP * QROW, HW), 0))
            total = total + nn(place, g_output[:, half * HW : (half + 1) * HW])
        pack_ref[:, there] = total.astype(BF16)
    inputs = seq_ref[...].astype(F32)
    g_first = jnp.sum(d_normed * inputs * rms_of(inputs), axis=0, keepdims=True)
    order = from_chunks()
    first_high, first_low = split_two(jnp.broadcast_to(g_first, (16, D)))
    second_high, second_low = split_two(jnp.broadcast_to(gffn_ref[0:1, :], (16, D)))
    gains = [nt(order, one)[:, 0:1] for one in (first_high, first_low, second_high, second_low)]
    entry = chunk_entry(iota((EXP * QROW, 1), 0))
    bucket_of = jnp.right_shift(entry * 5462, 16)
    pick = hot(jnp.where(entry >= 0, bucket_of, -1) == bucket_ref[1:2, :])
    high, low = split_two(ddist[...])
    by_head = nt(pick, high) + nt(pick, low)
    head_of = entry - bucket_of * H
    mine = (entry >= 0) & (head_of == sp * HH + iota(by_head.shape, 1)) & (iota(by_head.shape, 1) < HH)
    table = jnp.sum(jnp.where(mine, by_head, 0.0), axis=-1, keepdims=True)
    table_high, table_low = split_two(table)
    column = iota((EXP * QROW, 64), 1)
    tail = jnp.zeros((EXP * QROW, 64), F32)
    for place, values in enumerate(gains + [table_high.astype(F32), table_low.astype(F32)]):
        tail = jnp.where(column == place, values, tail)
    pack_ref[:, QW:] = jnp.concatenate([grouter_ref[...], tail], axis=1).astype(BF16)


def end_kernel(parts_ref, dresid_ref, tok_ref, gains_ref, out_ref):
    count = tok_ref.shape[0]
    inputs = tok_ref[...].astype(F32)
    d_normed = parts_ref[:count, :] + parts_ref[count:, :]
    rms = rms_of(inputs)
    v = d_normed * gains_ref[64:65, :]
    out_ref[0] = dresid_ref[...] + rms * v - inputs * (rms * rms * rms) * jnp.mean(v * inputs, axis=-1, keepdims=True)


def here():
    owner = lax.axis_index("ep")
    return (owner // 16, owner // 4 % 4, owner % 4)


def across(axis, shift):
    owner, place = lax.axis_index("ep"), here()[axis]
    return {"ep": owner + ((place + shift) % SIDE - place) * STRIDES[axis]}


def other_core():
    return {"sp": 1 - lax.axis_index("sp")}


def greet():
    barrier = pltpu.get_barrier_semaphore()
    pl.semaphore_signal(barrier, inc=1, device_id=other_core(), device_id_type=MESH)
    for axis in range(3):
        for shift in range(1, SIDE):
            pl.semaphore_signal(barrier, inc=1, device_id=across(axis, shift), device_id_type=MESH)


def meet():
    pl.semaphore_wait(pltpu.get_barrier_semaphore(), 1 + 3 * (SIDE - 1))


def remote(source, target, send, receive, device):
    copy = pltpu.make_async_remote_copy(
        src_ref=source, dst_ref=target, send_sem=send, recv_sem=receive, device_id=device, device_id_type=MESH
    )
    copy.start()
    return copy


def gather_kernel(wq_ref, wk_ref, wv_ref, wo_ref, router_ref, attn_ref, ffn_ref, table_ref, tok_ref, pack_ref, seq_ref, stage, got, out16, core_send, core_recv, send, recv):
    greet()
    sp = lax.axis_index("sp")
    place = here()
    stage[...] = jnp.zeros_like(stage)
    out16[...] = jnp.zeros_like(out16)
    out16[0:6, :] = wo_ref[...]

    def standing(ref):
        size = ref.shape[1]
        values = jnp.broadcast_to(ref[...].astype(F32), (QROW, size))
        kept = jnp.where(iota((QROW, size), 0) == iota((QROW, size), 1), values, 0.0)
        return jnp.sum(kept, axis=1, keepdims=True)

    column = iota((QROW, 64), 1)
    tail = jnp.where(column == 0, standing(attn_ref), 0.0)
    tail = jnp.where(column == 1, standing(ffn_ref), tail)
    tail = jnp.where(column == 2, standing(table_ref), tail).astype(BF16)
    for half in range(2):
        for n, ref in enumerate((wq_ref, wk_ref, wv_ref)):
            stage[half, 0:6, n * HW : (n + 1) * HW] = ref[:, half * HW : (half + 1) * HW]
        stage[half, 0:6, ROUTER : ROUTER + EXP] = router_ref[...]
        stage[half, :, GAIN:] = tail
    seq_ref[sp] = tok_ref[...]
    meet()
    chunk_copy = remote(stage.at[1 - sp], got, core_send.at[0], core_recv.at[0], other_core())
    tok_copy = remote(tok_ref, seq_ref.at[sp], core_send.at[1], core_recv.at[1], other_core())
    row, col = iota((QROW, QROW), 0), iota((QROW, QROW), 1)
    low = jnp.where((row == col) & (col < 6), 1.0, 0.0)
    high = jnp.where((row == col + 6) & (col < 6), 1.0, 0.0)
    own = jnp.where(sp == 0, low, high).astype(BF16)
    others = jnp.where(sp == 0, high, low).astype(BF16)
    later = (col >= 3).astype(jnp.int32)
    chunk_copy.wait()
    mine = nn(own, stage[sp]) + nn(others, got[...])
    pack_ref[place[0], place[1], place[2], :, QW:] = mine[:, QW:].astype(BF16)
    for third in range(3):
        there = slice(third * HW, (third + 1) * HW)
        total = mine[:, there]
        for half in range(2):
            pick = hot((col < 6) & (col - 3 * later == third) & (row == 12 + 2 * later + half))
            total = total + nn(pick, out16[:, half * HW : (half + 1) * HW])
        pack_ref[place[0], place[1], place[2], :, there] = total.astype(BF16)
    copies = {}
    for phase in range(3):
        for part, (first, width, order) in enumerate(PARTS):
            index = [pl.ds(0, SIDE) if axis in order[:phase] else place[axis] for axis in range(3)]
            block = pack_ref.at[index[0], index[1], index[2], :, pl.ds(first, width)]
            if phase:
                for shift in range(1, SIDE):
                    copies[phase - 1, part, shift].wait_recv()
            for shift in range(1, SIDE):
                copies[phase, part, shift] = remote(
                    block, block, send.at[phase, part, shift - 1], recv.at[phase, part, shift - 1], across(order[phase], shift)
                )
    for part in range(3):
        for shift in range(1, SIDE):
            copies[2, part, shift].wait_recv()
    for copy in copies.values():
        copy.wait_send()
    tok_copy.wait()


def reduce_kernel(pack_ref, q_ref, k_ref, v_ref, o_ref, rest_ref, *scratch):
    firsts, sums, seconds, pairs, thirds = (scratch[3 * n : 3 * n + 3] for n in range(5))
    total, theirs, core_send, core_recv, send, recv = scratch[15:]
    greet()
    sp = lax.axis_index("sp")
    place = here()
    meet()
    copies = {}

    def push(phase, part, axis, shift, source, target):
        copies[phase, part, shift] = remote(
            source,
            target.at[shift - 1],
            send.at[phase, part, shift - 1],
            recv.at[phase, part, shift - 1],
            across(axis, shift),
        )

    def added(phase, part, own, arrived):
        values = own.astype(F32)
        for shift in range(1, SIDE):
            copies[phase, part, shift].wait_recv()
            values = values + arrived[shift - 1].astype(F32)
        return values

    def at(axes, axis, value):
        return tuple(value if one == axis else pl.ds(0, SIDE) for one in axes)

    for part, (first, width, order) in enumerate(PARTS):
        axis = order[2]
        for shift in (2, 1, 3):
            index = at((0, 1, 2), axis, (place[axis] + shift) % SIDE)
            push(0, part, axis, shift, pack_ref.at[index + (slice(None), pl.ds(first, width))], firsts[part])
    for part, (first, width, order) in enumerate(PARTS):
        own = pack_ref[at((0, 1, 2), order[2], place[order[2]]) + (slice(None), pl.ds(first, width))]
        sums[part][...] = added(0, part, own, firsts[part]).astype(BF16)
        axis = order[1]
        for shift in (2, 1, 3):
            index = at(sorted(order[:2]), axis, (place[axis] + shift) % SIDE)
            push(1, part, axis, shift, sums[part].at[index], seconds[part])
    for part, (first, width, order) in enumerate(PARTS):
        own = sums[part][at(sorted(order[:2]), order[1], place[order[1]])]
        pairs[part][...] = added(1, part, own, seconds[part]).astype(BF16)
        axis = order[0]
        for shift in (2, 1, 3):
            push(2, part, axis, shift, pairs[part].at[(place[axis] + shift) % SIDE], thirds[part])
    for part, (first, width, order) in enumerate(PARTS):
        own = pairs[part][place[order[0]]]
        total[:, first : first + width] = added(2, part, own, thirds[part])
    core = remote(total, theirs, core_send, core_recv, other_core())
    for row in range(6):
        for half in range(2):
            there = 12 + row // 3 * 2 + half
            third = row % 3 * HW
            o_ref[row : row + 1, half * HW : (half + 1) * HW] = total[there : there + 1, third : third + HW]
    core.wait_recv()
    mine = jnp.where(sp == 0, total[0:6, :], total[6:12, :])
    other = jnp.where(sp == 0, theirs[0:6, :], theirs[6:12, :])
    for n, ref in enumerate((q_ref, k_ref, v_ref)):
        there = slice(n * HW, (n + 1) * HW)
        ref[:, :HW] = jnp.where(sp == 0, mine[:, there], other[:, there])
        ref[:, HW:] = jnp.where(sp == 0, other[:, there], mine[:, there])
    rest_ref[...] = mine[:, QW:] + other[:, QW:]
    core.wait_send()
    for copy in copies.values():
        copy.wait_send()


def whole(kernel, outs, scratch=(), flops=0, moved=0, collective=None):
    remote_params = {} if collective is None else {"collective_id": collective, "has_side_effects": True}
    return pl.pallas_call(
        kernel,
        out_shape=[jax.ShapeDtypeStruct(shape, kind) for shape, kind in outs],
        scratch_shapes=list(scratch),
        compiler_params=pltpu.CompilerParams(vmem_limit_bytes=VMEM_LIMIT, **remote_params),
        cost_estimate=pl.CostEstimate(flops=flops, bytes_accessed=moved, transcendentals=0),
    )


def swap(values, axis="sp"):
    return lax.all_to_all(values, axis, split_axis=0, concat_axis=0, tiled=True)


def shards(tokens, cotangent, w_query, w_key, w_value, w_output, gain_attn, gain_ffn, router, bias_table, w_in, w_out, routes, buckets):
    count = tokens.shape[1]
    seq = 2 * count
    owners = lax.axis_size("ep")
    tok = tokens[0]
    cot = cotangent[0]
    route = routes[0]
    pack, sequence = whole(
        gather_kernel,
        [((SIDE, SIDE, SIDE, QROW, PW), BF16), ((2, count, D), BF16)],
        scratch=[
            pltpu.VMEM((2, QROW, PW), BF16),
            pltpu.VMEM((QROW, PW), BF16),
            pltpu.VMEM((QROW, D), BF16),
            pltpu.SemaphoreType.DMA((2,)),
            pltpu.SemaphoreType.DMA((2,)),
            pltpu.SemaphoreType.DMA((3, 3, SIDE - 1)),
            pltpu.SemaphoreType.DMA((3, 3, SIDE - 1)),
        ],
        flops=10**6,
        moved=6 * 10**6,
        collective=0,
    )(w_query, w_key, w_value, w_output, router, gain_attn[None], gain_ffn[None], bias_table[None], tok)
    pack = pack.reshape(owners * QROW, PW)
    sequence = sequence.reshape(seq, D)
    turned_buckets = jnp.stack([jnp.roll(buckets[::-1], 1), jnp.roll(buckets, -1)])

    branch, output_mine, attended, qkv_all, full, gains, normed_attn, bias, lse = whole(
        first_kernel,
        [
            ((seq, D), F32),
            ((HW, D), BF16),
            ((seq, HW), BF16),
            ((seq, QW), BF16),
            ((D, PW), BF16),
            ((128, D), F32),
            ((seq, D), BF16),
            ((8, seq), F32),
            ((seq, 128), F32),
        ],
        flops=4 * 10**9,
        moved=8 * 10**6,
    )(sequence, pack, turned_buckets)

    parts = swap(branch.reshape(2, count, D)).reshape(seq, D)

    filled, resid, normed_ffn, places, gates = whole(
        middle_kernel,
        [
            ((EXP * SLOT, 2 * D), BF16),
            ((count, D), F32),
            ((count, D), BF16),
            ((count, 2 * EXP * SLOT), BF16),
            ((count, 128), F32),
        ],
        flops=10**9,
        moved=4 * 10**6,
    )(parts, tok, cot, gains, full, route)

    arrived = swap(filled.reshape(owners, SLOT, 2 * D), "ep")
    rows = swap(jnp.broadcast_to(arrived.reshape(1, owners * SLOT, 2 * D), (2, owners * SLOT, 2 * D)))
    rows = rows.reshape(2 * owners * SLOT, 2 * D)
    load = rows.shape[0]
    hidden = w_in.shape[2]
    step = 256
    resident = pl.BlockSpec((load, 2 * D), lambda f: (0, 0))
    by_column = pl.BlockSpec((load, step), lambda f: (0, f))
    result, act, d_pre = pl.pallas_call(
        expert_kernel,
        grid=(hidden // step,),
        in_specs=[
            resident,
            pl.BlockSpec((D, step), lambda f: (0, f)),
            pl.BlockSpec((step, D), lambda f: (f, 0)),
        ],
        out_specs=[resident, by_column, by_column],
        out_shape=[
            jax.ShapeDtypeStruct((load, 2 * D), BF16),
            jax.ShapeDtypeStruct((load, hidden), BF16),
            jax.ShapeDtypeStruct((load, hidden), BF16),
        ],
        scratch_shapes=[pltpu.VMEM((load, D), F32), pltpu.VMEM((load, D), F32)],
        compiler_params=pltpu.CompilerParams(vmem_limit_bytes=VMEM_LIMIT),
        cost_estimate=pl.CostEstimate(flops=8 * load * D * hidden, bytes_accessed=20 * 10**6, transcendentals=load * hidden),
    )(rows, w_in[0], w_out[0])
    halves = swap(result.reshape(2, owners * SLOT, 2 * D))
    joined = (halves[0].astype(F32) + halves[1].astype(F32)).astype(BF16)
    returned = swap(joined.reshape(owners, SLOT, 2 * D), "ep").reshape(owners * SLOT, 2 * D)

    grad_w_in, grad_w_out = pl.pallas_call(
        expert_grad_kernel,
        grid=(hidden // step,),
        in_specs=[resident, by_column, by_column],
        out_specs=[
            pl.BlockSpec((1, D, step), lambda f: (0, 0, f)),
            pl.BlockSpec((1, step, D), lambda f: (0, f, 0)),
        ],
        out_shape=[
            jax.ShapeDtypeStruct((1, D, hidden), F32),
            jax.ShapeDtypeStruct((1, hidden, D), F32),
        ],
        scratch_shapes=[pltpu.VMEM((D, load), BF16)],
        compiler_params=pltpu.CompilerParams(vmem_limit_bytes=VMEM_LIMIT),
        cost_estimate=pl.CostEstimate(flops=4 * load * D * hidden, bytes_accessed=20 * 10**6, transcendentals=0),
    )(rows, act, d_pre)

    mixed, d_resid, d_branch, g_router, g_ffn = whole(
        mix_kernel,
        [
            ((1, count, D), BF16),
            ((count, D), F32),
            ((count, D), BF16),
            ((owners * QROW, EXP), F32),
            ((8, D), F32),
        ],
        flops=10**9,
        moved=5 * 10**6,
    )(returned, places, gates, resid, cot, gains, full, normed_ffn, route)

    branch_seq = swap(jnp.broadcast_to(d_branch[None], (2, count, D))).reshape(seq, D)
    g_pack, d_norm = whole(
        last_kernel,
        [((owners * QROW, PW), BF16), ((seq, D), F32)],
        scratch=[pltpu.VMEM((seq, QW), BF16), pltpu.VMEM((8, seq), F32)],
        flops=5 * 10**9,
        moved=10 * 10**6,
    )(branch_seq, output_mine, attended, qkv_all, lse, bias, normed_attn, sequence, full, turned_buckets, g_router, g_ffn)

    d_parts = swap(d_norm.reshape(2, count, D)).reshape(seq, D)
    (d_tokens,) = whole(end_kernel, [((1, count, D), F32)], flops=10**6, moved=10**6)(d_parts, d_resid, tok, gains)

    widths = [width for _, width, _ in PARTS]
    g_query, g_key, g_value, g_output, rest = whole(
        reduce_kernel,
        [((6, D), F32)] * 4 + [((6, 128), F32)],
        scratch=[pltpu.VMEM((SIDE - 1, SIDE, SIDE, QROW, width), BF16) for width in widths]
        + [pltpu.VMEM((SIDE, SIDE, QROW, width), BF16) for width in widths]
        + [pltpu.VMEM((SIDE - 1, SIDE, QROW, width), BF16) for width in widths]
        + [pltpu.VMEM((SIDE, QROW, width), BF16) for width in widths]
        + [pltpu.VMEM((SIDE - 1, QROW, width), BF16) for width in widths]
        + [pltpu.VMEM((QROW, PW), F32)] * 2
        + [pltpu.SemaphoreType.DMA] * 2
        + [pltpu.SemaphoreType.DMA((3, 3, SIDE - 1))] * 2,
        flops=10**7,
        moved=6 * 10**6,
        collective=1,
    )(g_pack.reshape(SIDE, SIDE, SIDE, QROW, PW))
    extra = rest[:, 64:70]
    return (
        mixed,
        d_tokens,
        g_query,
        g_key,
        g_value,
        g_output,
        extra[:, 0] + extra[:, 1],
        extra[:, 2] + extra[:, 3],
        rest[:, :EXP],
        (extra[:, 4] + extra[:, 5])[:3],
        grad_w_in,
        grad_w_out,
    )


def solution(mesh):
    wide = P(("sp", "ep"), None)
    flat = P(("sp", "ep"))
    rows = P("ep", "sp", None)
    return jax.shard_map(
        shards,
        mesh=mesh,
        in_specs=(rows, rows, wide, wide, wide, wide, flat, flat, wide, flat, P("ep", None, "sp"), rows, rows, P()),
        out_specs=(rows, rows, wide, wide, wide, wide, flat, flat, wide, flat, P("ep", None, "sp"), rows),
        check_vma=False,
    )
```

```python
import functools

import jax
import jax.numpy as jnp
from jax import lax
from jax.experimental import pallas as pl
from jax.experimental.pallas import tpu as pltpu
from jax.sharding import PartitionSpec as P

D = 768
H = 12
HD = 64
HH = H // 2
HW = HH * HD
EXP = 64
EPS = 1e-06
CAP = 6
SLOT = 8
SLOTS = EXP * SLOT
ROW = 3 * HW
QROW = 16
QW = 3 * HW
PW = QW + 128
SIDE = 4
STRIDES = (16, 4, 1)
PARTS = ((0, 512, (2, 1, 0)), (512, 384, (0, 2, 1)), (896, 384, (1, 0, 2)))
MESH = pl.DeviceIdType.MESH
ROUTER = QW
GAIN = QW + 64
F32 = jnp.float32
BF16 = jnp.bfloat16
VMEM_LIMIT = 56 * 1024 * 1024


def iota(shape, axis):
    return lax.broadcasted_iota(jnp.int32, shape, axis)


def nn(left, right):
    return lax.dot_general(left, right, (((1,), (0,)), ((), ())), preferred_element_type=F32)


def nt(left, right):
    return lax.dot_general(left, right, (((1,), (1,)), ((), ())), preferred_element_type=F32)


def tn(left, right):
    return lax.dot_general(left, right, (((0,), (0,)), ((), ())), preferred_element_type=F32)


def chunk_feature(rows):
    owner = jnp.right_shift(rows, 4)
    inner = jnp.bitwise_and(rows, 15)
    half = (inner >= 6).astype(jnp.int32)
    feature = half * (D // 2) + owner * 6 + inner - 6 * half
    return jnp.where(inner < 12, feature, -1)


def chunk_entry(rows):
    owner = jnp.right_shift(rows, 4)
    inner = jnp.bitwise_and(rows, 15)
    half = (inner >= 6).astype(jnp.int32)
    inside = inner - 6 * half
    entry = half * (32 * H // 2) + owner * 3 + inside
    return jnp.where((inner < 12) & (inside < 3), entry, -1)


def hot(condition):
    return jnp.where(condition, 1.0, 0.0).astype(BF16)


def to_chunks():
    return hot(chunk_feature(iota((1, EXP * QROW), 1)) == iota((D, EXP * QROW), 0))


def from_chunks():
    return hot(chunk_feature(iota((EXP * QROW, 1), 0)) == iota((EXP * QROW, D), 1))


def output_row(channel, half, third):
    owner = jnp.right_shift(channel * 10923, 16)
    inner = channel - owner * 6
    later = (inner >= 3).astype(jnp.int32)
    row = owner * QROW + 12 + 2 * later + half
    return jnp.where(inner - 3 * later == third, row, -1)


def rms_of(values):
    return lax.rsqrt(jnp.mean(values * values, axis=-1, keepdims=True) + EPS)


def head_bias(bias_ref, head, seq):
    row = jnp.broadcast_to(bias_ref[head : head + 1, :], (seq, seq))
    return pltpu.roll(row, 0, 1, stride=1, stride_axis=0)


def front_kernel(seq_ref, pack_ref, bucket_ref, tok_ref, cot_ref, routes_ref, output_ref, attended_ref, qkv_ref, full_ref, gains_ref, normed_ref, bias_ref, lse_ref, *rest):
    middle, (halves, got, send, recv) = rest[:5], rest[5:]
    greet_core()
    seq = seq_ref.shape[0]
    sp = lax.axis_index("sp")
    spread = to_chunks()
    full_ref[...] = nn(spread, pack_ref[...]).astype(BF16)
    tail = pack_ref[:, QW:]
    gains = tn(tail, from_chunks())
    gains_ref[...] = gains
    entry = chunk_entry(iota((EXP * QROW, 1), 0))
    bucket_of = jnp.right_shift(entry * 5462, 16)
    head_of = entry - bucket_of * H
    column = iota((EXP * QROW, 128), 1)
    table = jnp.where(
        (entry >= 0) & (head_of == sp * HH + column) & (column < HH),
        tail[:, 66:67].astype(F32),
        0.0,
    ).astype(BF16)
    bucket_here = jnp.where(entry >= 0, bucket_of, -1)
    by_distance = tn(table, hot(bucket_here == bucket_ref[...]))[0:16, :].astype(BF16)
    turn = hot(jnp.bitwise_and(iota((seq, seq), 0) + iota((seq, seq), 1), seq - 1) == 0)
    bias_ref[...] = nn(by_distance, turn)
    channel = iota((HW, 1), 0)
    for half in range(2):
        rows = jnp.zeros((HW, HW), F32)
        for third in range(3):
            pick = hot(output_row(channel, half, third) == iota((HW, EXP * QROW), 1))
            rows = rows + nn(pick, pack_ref[:, third * HW : (third + 1) * HW])
        output_ref[:, half * HW : (half + 1) * HW] = rows.astype(BF16)

    inputs = seq_ref[...].astype(F32)
    normed = (inputs * rms_of(inputs) * gains[64:65, :]).astype(BF16)
    normed_ref[...] = normed
    qkv_ref[...] = nn(normed, full_ref[:, :QW]).astype(BF16)
    causal = iota((seq, seq), 1) <= iota((seq, seq), 0)
    lse_ref[...] = jnp.zeros_like(lse_ref)
    for head in range(HH):
        at = head * HD
        query = qkv_ref[:, at : at + HD]
        key = qkv_ref[:, HW + at : HW + at + HD]
        value = qkv_ref[:, 2 * HW + at : 2 * HW + at + HD]
        scores = nt(query, key) * (HD**-0.5) + head_bias(bias_ref, head, seq)
        scores = jnp.where(causal, scores, -jnp.inf)
        peak = jnp.max(scores, axis=-1, keepdims=True)
        grown = jnp.exp(scores - peak)
        total = jnp.sum(grown, axis=-1, keepdims=True)
        probs = (grown / total).astype(BF16)
        attended_ref[:, at : at + HD] = nn(probs, value).astype(BF16)
        lse_ref[:, head : head + 1] = peak + jnp.log(total)
    count = seq // 2
    meet_core()
    halves[...] = nn(attended_ref[...], output_ref[...]).reshape(halves.shape)
    copy = remote(halves.at[1 - sp], got, send, recv, other_core())
    copy.wait_recv()
    resid = tok_ref[...].astype(F32) + halves[sp] + got[...]
    middle_part(resid, cot_ref, gains_ref, full_ref, routes_ref, *middle)
    copy.wait_send()


def route_hot(routes_ref, k, width):
    return (routes_ref[:, k : k + 1] == iota((routes_ref.shape[0], width), 1)).astype(F32)


def middle_part(resid, cot_ref, gains_ref, full_ref, routes_ref, filled_ref, resid_ref, normed_ref, places_ref, gates_ref):
    count = resid.shape[0]
    resid_ref[...] = resid
    normed = (resid * rms_of(resid) * gains_ref[65:66, :]).astype(BF16)
    normed_ref[...] = normed
    logits = nn(normed, full_ref[:, ROUTER : ROUTER + EXP])
    named = [route_hot(routes_ref, k, EXP) for k in range(2)]
    chosen = [jnp.sum(logits * one, axis=-1, keepdims=True) for one in named]
    peak = jnp.maximum(chosen[0], chosen[1])
    grown = [jnp.exp(one - peak) for one in chosen]
    total = grown[0] + grown[1]
    gates = [one / total for one in grown]
    column = iota((count, 128), 1)
    gates_ref[...] = jnp.where(column == 0, gates[0], jnp.where(column == 1, gates[1], 0.0))
    before = hot(iota((count, count), 1) < iota((count, count), 0))
    earlier = nn(before, (named[0] + named[1]).astype(BF16))
    upstream = cot_ref[...].astype(F32)
    slots = iota((count, SLOTS), 1)
    filled = [0.0, 0.0, 0.0]
    tails = [0.0, 0.0, 0.0]
    either = 0.0
    for k in range(2):
        rank = jnp.sum(earlier * named[k], axis=-1, keepdims=True).astype(jnp.int32)
        start = routes_ref[:, k : k + 1] * SLOT
        place = hot(slots == start + rank)
        places_ref[:, k * SLOTS : (k + 1) * SLOTS] = place
        either = either + place
        upper = (rank >= 3).astype(jnp.int32)
        spread = (gates[k] * upstream).astype(BF16)
        filled[2] = filled[2] + tn(place, spread[:, :HW])
        for third in range(3):
            tail = hot(slots == jnp.where(rank - 3 * upper == third, start + CAP + upper, -1))
            tails[third] = tails[third] + tail
            filled[third] = filled[third] + tn(tail, spread[:, HW:])
    for third in range(3):
        places_ref[:, (2 + third) * SLOTS : (3 + third) * SLOTS] = tails[third]
        total = filled[third]
        if third < 2:
            total = total + tn(either, normed[:, third * HW : (third + 1) * HW])
        filled_ref[:, third * HW : (third + 1) * HW] = total.astype(BF16)


def unpacking():
    row = iota((EXP * CAP, 1), 0)
    owner = jnp.right_shift(row * 10923, 16)
    inner = row - owner * CAP
    upper = (inner >= 3).astype(jnp.int32)
    slots = iota((EXP * CAP, SLOTS), 1)
    tails = [hot(slots == jnp.where(inner - 3 * upper == third, owner * SLOT + CAP + upper, -1)) for third in range(3)]
    return hot(slots == owner * SLOT + inner), tails


def expert_grad_kernel(rows_ref, act_ref, dpre_ref, gin_ref, gout_ref, turned):
    @pl.when(pl.program_id(0) == 0)
    def _():
        turned[...] = rows_ref[:, :D].T

    gin_ref[0] = nn(turned[...], dpre_ref[...])
    gout_ref[0] = tn(act_ref[...], rows_ref[:, D:])


def split_two(values):
    high = values.astype(BF16)
    return high, (values - high.astype(F32)).astype(BF16)


def back_kernel(ret_ref, places_ref, gates_ref, resid_ref, cot_ref, gains_ref, full_ref, ffn_ref, routes_ref, wo_ref, attended_ref, qkv_ref, lse_ref, bias_ref, normed_ref, seq_ref, bucket_ref, mixed_ref, dresid_ref, pack_ref, dnorm_ref, branch_ref, dqkv, ddist, send, recv):
    greet_core()
    count = resid_ref.shape[0]
    sp = lax.axis_index("sp")
    resid = resid_ref[...]
    upstream = cot_ref[...].astype(F32)
    gates = [gates_ref[:, k : k + 1] for k in range(2)]
    outs = [nn(places_ref[:, k * SLOTS : (k + 1) * SLOTS], ret_ref[:, :D]) for k in range(2)]
    mixed_ref[0] = (resid + (gates[0] * outs[0] + gates[1] * outs[1])).astype(BF16)
    d_gates = [jnp.sum(one * upstream, axis=-1, keepdims=True) for one in outs]
    inner = gates[0] * d_gates[0] + gates[1] * d_gates[1]
    d_logits = jnp.zeros((count, EXP), F32)
    for k in range(2):
        d_logits = d_logits + route_hot(routes_ref, k, EXP) * (gates[k] * (d_gates[k] - inner))
    d_logits = d_logits.astype(BF16)
    either = places_ref[:, :SLOTS] + places_ref[:, SLOTS : 2 * SLOTS]
    upper = 0.0
    for third in range(3):
        upper = upper + nn(places_ref[:, (2 + third) * SLOTS : (3 + third) * SLOTS], ret_ref[:, third * HW : (third + 1) * HW])
    d_normed = jnp.concatenate([nn(either, ret_ref[:, D:]), upper], axis=1)
    d_normed = d_normed + nt(d_logits, full_ref[:, ROUTER : ROUTER + EXP])
    rms = rms_of(resid)
    u = d_normed * gains_ref[65:66, :]
    d_resid = upstream + rms * u - resid * (rms * rms * rms) * jnp.mean(u * resid, axis=-1, keepdims=True)
    branch_ref[sp] = d_resid.astype(BF16)
    meet_core()
    copy = remote(branch_ref.at[sp], branch_ref.at[sp], send, recv, other_core())
    dresid_ref[...] = d_resid
    g_second = jnp.sum(d_normed * resid * rms, axis=0, keepdims=True)
    to_owners = to_chunks()
    g_router = tn(nn(ffn_ref[...], to_owners).astype(BF16), d_logits)
    turned = nn(normed_ref[...], to_owners).astype(BF16).T
    copy.wait_recv()
    seq = seq_ref.shape[0]
    d_branch = branch_ref[...].reshape(seq, D)
    d_attended = nt(d_branch, wo_ref[...]).astype(BF16)
    causal = iota((seq, seq), 1) <= iota((seq, seq), 0)
    flip = hot(iota((seq, seq), 0) + iota((seq, seq), 1) == seq - 1)
    ddist[...] = jnp.zeros_like(ddist)
    for head in range(HH):
        at = head * HD
        query = qkv_ref[:, at : at + HD]
        key = qkv_ref[:, HW + at : HW + at + HD]
        value = qkv_ref[:, 2 * HW + at : 2 * HW + at + HD]
        d_out = d_attended[:, at : at + HD]
        scores = nt(query, key) * (HD**-0.5) + head_bias(bias_ref, head, seq)
        probs = jnp.where(causal, jnp.exp(scores - lse_ref[:, head : head + 1]), 0.0)
        d_value = tn(probs.astype(BF16), d_out)
        d_probs = nt(d_out, value)
        row_dot = jnp.sum(probs * d_probs, axis=-1, keepdims=True)
        d_scores = (probs * (d_probs - row_dot)).astype(BF16)
        dqkv[:, at : at + HD] = (nn(d_scores, key) * (HD**-0.5)).astype(BF16)
        dqkv[:, HW + at : HW + at + HD] = (tn(d_scores, query) * (HD**-0.5)).astype(BF16)
        dqkv[:, 2 * HW + at : 2 * HW + at + HD] = d_value.astype(BF16)
        skewed = pltpu.roll(nn(d_scores, flip), 0, 1, stride=1, stride_axis=0)
        ddist[head : head + 1, :] = jnp.sum(skewed, axis=0, keepdims=True)
    d_normed = nt(dqkv[...], full_ref[:, :QW])
    dnorm_ref[...] = d_normed.reshape(dnorm_ref.shape)
    g_output = tn(attended_ref[...], d_branch).astype(BF16)
    channel = iota((1, HW), 1)
    for third in range(3):
        there = slice(third * HW, (third + 1) * HW)
        total = nn(turned, dqkv[:, there])
        for half in range(2):
            place = hot(output_row(channel, half, third) == iota((EXP * QROW, HW), 0))
            total = total + nn(place, g_output[:, half * HW : (half + 1) * HW])
        pack_ref[:, there] = total.astype(BF16)
    inputs = seq_ref[...].astype(F32)
    g_first = jnp.sum(d_normed * inputs * rms_of(inputs), axis=0, keepdims=True)
    order = from_chunks()
    first_high, first_low = split_two(jnp.broadcast_to(g_first, (16, D)))
    second_high, second_low = split_two(jnp.broadcast_to(g_second, (16, D)))
    gains = [nt(order, one)[:, 0:1] for one in (first_high, first_low, second_high, second_low)]
    entry = chunk_entry(iota((EXP * QROW, 1), 0))
    bucket_of = jnp.right_shift(entry * 5462, 16)
    pick = hot(jnp.where(entry >= 0, bucket_of, -1) == bucket_ref[...])
    high, low = split_two(pltpu.roll(ddist[...], 1, 1))
    by_head = nt(pick, high) + nt(pick, low)
    head_of = entry - bucket_of * H
    mine = (entry >= 0) & (head_of == sp * HH + iota(by_head.shape, 1)) & (iota(by_head.shape, 1) < HH)
    table = jnp.sum(jnp.where(mine, by_head, 0.0), axis=-1, keepdims=True)
    table_high, table_low = split_two(table)
    column = iota((EXP * QROW, 64), 1)
    tail = jnp.zeros((EXP * QROW, 64), F32)
    for place, values in enumerate(gains + [table_high.astype(F32), table_low.astype(F32)]):
        tail = jnp.where(column == place, values, tail)
    pack_ref[:, QW:] = jnp.concatenate([g_router, tail], axis=1).astype(BF16)
    copy.wait_send()


def here():
    owner = lax.axis_index("ep")
    return (owner // 16, owner // 4 % 4, owner % 4)


def across(axis, shift):
    owner, place = lax.axis_index("ep"), here()[axis]
    return {"ep": owner + ((place + shift) % SIDE - place) * STRIDES[axis]}


def other_core():
    return {"sp": 1 - lax.axis_index("sp")}


def greet_core():
    pl.semaphore_signal(pltpu.get_barrier_semaphore(), inc=1, device_id=other_core(), device_id_type=MESH)


def meet_core():
    pl.semaphore_wait(pltpu.get_barrier_semaphore(), 1)


def greet():
    barrier = pltpu.get_barrier_semaphore()
    pl.semaphore_signal(barrier, inc=1, device_id=other_core(), device_id_type=MESH)
    for axis in range(3):
        for shift in range(1, SIDE):
            pl.semaphore_signal(barrier, inc=1, device_id=across(axis, shift), device_id_type=MESH)


def meet():
    pl.semaphore_wait(pltpu.get_barrier_semaphore(), 1 + 3 * (SIDE - 1))


def remote(source, target, send, receive, device):
    copy = pltpu.make_async_remote_copy(
        src_ref=source, dst_ref=target, send_sem=send, recv_sem=receive, device_id=device, device_id_type=MESH
    )
    copy.start()
    return copy


def gather_kernel(wq_ref, wk_ref, wv_ref, wo_ref, router_ref, attn_ref, ffn_ref, table_ref, tok_ref, pack_ref, seq_ref, stage, got, out16, core_send, core_recv, send, recv):
    greet()
    sp = lax.axis_index("sp")
    place = here()
    stage[...] = jnp.zeros_like(stage)
    out16[...] = jnp.zeros_like(out16)
    out16[0:6, :] = wo_ref[...]

    def standing(ref):
        size = ref.shape[1]
        values = jnp.broadcast_to(ref[...].astype(F32), (QROW, size))
        kept = jnp.where(iota((QROW, size), 0) == iota((QROW, size), 1), values, 0.0)
        return jnp.sum(kept, axis=1, keepdims=True)

    column = iota((QROW, 64), 1)
    tail = jnp.where(column == 0, standing(attn_ref), 0.0)
    tail = jnp.where(column == 1, standing(ffn_ref), tail)
    tail = jnp.where(column == 2, standing(table_ref), tail).astype(BF16)
    for half in range(2):
        for n, ref in enumerate((wq_ref, wk_ref, wv_ref)):
            stage[half, 0:6, n * HW : (n + 1) * HW] = ref[:, half * HW : (half + 1) * HW]
        stage[half, 0:6, ROUTER : ROUTER + EXP] = router_ref[...]
        stage[half, :, GAIN:] = tail
    seq_ref[sp] = tok_ref[...]
    meet()
    chunk_copy = remote(stage.at[1 - sp], got, core_send.at[0], core_recv.at[0], other_core())
    tok_copy = remote(tok_ref, seq_ref.at[sp], core_send.at[1], core_recv.at[1], other_core())
    row, col = iota((QROW, QROW), 0), iota((QROW, QROW), 1)
    low = jnp.where((row == col) & (col < 6), 1.0, 0.0)
    high = jnp.where((row == col + 6) & (col < 6), 1.0, 0.0)
    own = jnp.where(sp == 0, low, high).astype(BF16)
    others = jnp.where(sp == 0, high, low).astype(BF16)
    later = (col >= 3).astype(jnp.int32)
    chunk_copy.wait()
    mine = nn(own, stage[sp]) + nn(others, got[...])
    pack_ref[place[0], place[1], place[2], :, QW:] = mine[:, QW:].astype(BF16)
    for third in range(3):
        there = slice(third * HW, (third + 1) * HW)
        total = mine[:, there]
        for half in range(2):
            pick = hot((col < 6) & (col - 3 * later == third) & (row == 12 + 2 * later + half))
            total = total + nn(pick, out16[:, half * HW : (half + 1) * HW])
        pack_ref[place[0], place[1], place[2], :, there] = total.astype(BF16)
    copies = {}
    for phase in range(3):
        for part, (first, width, order) in enumerate(PARTS):
            index = [pl.ds(0, SIDE) if axis in order[:phase] else place[axis] for axis in range(3)]
            block = pack_ref.at[index[0], index[1], index[2], :, pl.ds(first, width)]
            if phase:
                for shift in range(1, SIDE):
                    copies[phase - 1, part, shift].wait_recv()
            for shift in range(1, SIDE):
                copies[phase, part, shift] = remote(
                    block, block, send.at[phase, part, shift - 1], recv.at[phase, part, shift - 1], across(order[phase], shift)
                )
    for part in range(3):
        for shift in range(1, SIDE):
            copies[2, part, shift].wait_recv()
    for copy in copies.values():
        copy.wait_send()
    tok_copy.wait()


def reduce_kernel(pack_ref, dnorm_ref, dresid_ref, tok_ref, gains_ref, q_ref, k_ref, v_ref, o_ref, rest_ref, dtok_ref, *scratch):
    firsts, sums, seconds, pairs, thirds = (scratch[3 * n : 3 * n + 3] for n in range(5))
    total, theirs, got, core_send, core_recv, send, recv = scratch[15:]
    greet()
    sp = lax.axis_index("sp")
    place = here()
    meet()
    copies = {}

    def push(phase, part, axis, shift, source, target):
        copies[phase, part, shift] = remote(
            source,
            target.at[shift - 1],
            send.at[phase, part, shift - 1],
            recv.at[phase, part, shift - 1],
            across(axis, shift),
        )

    def added(phase, part, own, arrived):
        values = own.astype(F32)
        for shift in range(1, SIDE):
            copies[phase, part, shift].wait_recv()
            values = values + arrived[shift - 1].astype(F32)
        return values

    def at(axes, axis, value):
        return tuple(value if one == axis else pl.ds(0, SIDE) for one in axes)

    for part, (first, width, order) in enumerate(PARTS):
        axis = order[2]
        for shift in (2, 1, 3):
            index = at((0, 1, 2), axis, (place[axis] + shift) % SIDE)
            push(0, part, axis, shift, pack_ref.at[index + (slice(None), pl.ds(first, width))], firsts[part])
    norm_copy = remote(dnorm_ref.at[1 - sp], got, core_send.at[1], core_recv.at[1], other_core())
    norm_copy.wait_recv()
    inputs = tok_ref[...].astype(F32)
    d_normed = dnorm_ref[sp] + got[...]
    rms = rms_of(inputs)
    v = d_normed * gains_ref[64:65, :]
    drop = inputs * (rms * rms * rms) * jnp.mean(v * inputs, axis=-1, keepdims=True)
    dtok_ref[0] = dresid_ref[...] + rms * v - drop
    for part, (first, width, order) in enumerate(PARTS):
        own = pack_ref[at((0, 1, 2), order[2], place[order[2]]) + (slice(None), pl.ds(first, width))]
        sums[part][...] = added(0, part, own, firsts[part]).astype(BF16)
        axis = order[1]
        for shift in (2, 1, 3):
            index = at(sorted(order[:2]), axis, (place[axis] + shift) % SIDE)
            push(1, part, axis, shift, sums[part].at[index], seconds[part])
    for part, (first, width, order) in enumerate(PARTS):
        own = sums[part][at(sorted(order[:2]), order[1], place[order[1]])]
        pairs[part][...] = added(1, part, own, seconds[part]).astype(BF16)
        axis = order[0]
        for shift in (2, 1, 3):
            push(2, part, axis, shift, pairs[part].at[(place[axis] + shift) % SIDE], thirds[part])
    for part, (first, width, order) in enumerate(PARTS):
        own = pairs[part][place[order[0]]]
        total[:, first : first + width] = added(2, part, own, thirds[part])
    core = remote(total, theirs, core_send.at[0], core_recv.at[0], other_core())
    for row in range(6):
        for half in range(2):
            there = 12 + row // 3 * 2 + half
            third = row % 3 * HW
            o_ref[row : row + 1, half * HW : (half + 1) * HW] = total[there : there + 1, third : third + HW]
    core.wait_recv()
    mine = jnp.where(sp == 0, total[0:6, :], total[6:12, :])
    other = jnp.where(sp == 0, theirs[0:6, :], theirs[6:12, :])
    for n, ref in enumerate((q_ref, k_ref, v_ref)):
        there = slice(n * HW, (n + 1) * HW)
        ref[:, :HW] = jnp.where(sp == 0, mine[:, there], other[:, there])
        ref[:, HW:] = jnp.where(sp == 0, other[:, there], mine[:, there])
    rest_ref[...] = mine[:, QW:] + other[:, QW:]
    core.wait_send()
    norm_copy.wait_send()
    for copy in copies.values():
        copy.wait_send()


def expert_kernel(filled_ref, win_hbm, wout_hbm, rows_ref, act_ref, dpre_ref, joined_ref, one, two, arrived, theirs, win, wout, outgoing, back, load_sem, local_sem, core_send, core_recv, send, recv):
    greet()
    loads = [pltpu.make_async_copy(win_hbm.at[0], win, load_sem.at[0]), pltpu.make_async_copy(wout_hbm.at[0], wout, load_sem.at[1])]
    for load in loads:
        load.start()
    place = here()
    buffers = (filled_ref, one, two, arrived)
    parts = ((0, (2, 1, 0)), (1, (0, 2, 1)), (2, (1, 0, 2)))
    copies, kept = {}, {}

    def block(ref, axis, value, third):
        index = tuple(value if other == axis else pl.ds(0, SIDE) for other in range(3))
        return ref.at[index + (slice(None), pl.ds(third * HW, HW))]

    def settle(phase, third):
        for shift in range(1, SIDE):
            copies[phase, third, shift].wait_recv()
        kept[phase, third].wait()

    meet()
    for phase in range(3):
        for third, order in parts:
            if phase:
                settle(phase - 1, third)
            axis = order[phase]
            source, target = buffers[phase], buffers[phase + 1]
            for shift in (2, 1, 3):
                copies[phase, third, shift] = remote(
                    block(source, axis, (place[axis] + shift) % SIDE, third),
                    block(target, axis, place[axis], third),
                    send.at[phase, third, shift - 1],
                    recv.at[phase, third, shift - 1],
                    across(axis, shift),
                )
            kept[phase, third] = pltpu.make_async_copy(
                block(source, axis, place[axis], third), block(target, axis, place[axis], third), local_sem.at[phase, third]
            )
            kept[phase, third].start()
    pushes = []
    for third in range(3):
        settle(2, third)
        columns = (slice(None), slice(None), slice(None), slice(None), pl.ds(third * HW, HW))
        pushes.append(remote(arrived.at[columns], theirs.at[columns], core_send.at[third], core_recv.at[third], other_core()))
    for load in loads:
        load.wait()
    main, tails = unpacking()

    def half(first, source):
        there = slice(first, first + EXP * CAP)
        packed = source[...].reshape(SLOTS, ROW)
        rows_ref[there, :ROW] = nn(main, packed).astype(BF16)
        rest = 0.0
        for third in range(3):
            rest = rest + nn(tails[third], packed[:, third * HW : (third + 1) * HW])
        rows_ref[there, ROW:] = rest.astype(BF16)
        rows = rows_ref[there, :D]
        d_rows = rows_ref[there, D:]
        hidden = win.shape[1]
        step = 512
        for start in range(0, hidden, step):
            columns = slice(start, start + step)
            pre = nn(rows, win[:, columns])
            d_act = nt(d_rows, wout[columns, :])
            square = pre * pre
            slope = 0.7978845608028654
            t = jnp.tanh(slope * (pre + 0.044715 * (square * pre)))
            upper = 0.5 * (1.0 + t)
            act_ref[there, columns] = (pre * upper).astype(BF16)
            bend = upper + 0.5 * pre * (1.0 - t * t) * (slope * (1.0 + 3 * 0.044715 * square))
            dpre_ref[there, columns] = (d_act * bend).astype(BF16)
        out = nn(act_ref[there, :], wout[...]).astype(BF16)
        return out, nt(dpre_ref[there, :], win[...]).astype(BF16)

    def repack(out, grad):
        parts = (out[:, :HW], out[:, HW:], grad[:, :HW])
        return [tn(main, parts[third]) + tn(tails[third], grad[:, HW:]) for third in range(3)]

    out, grad = half(0, arrived)
    for push in pushes:
        push.wait_recv()
    out_theirs, grad_theirs = half(EXP * CAP, theirs)
    for third, values in enumerate(repack(out_theirs, grad_theirs)):
        outgoing[third] = values.astype(BF16)
        pushes.append(remote(outgoing.at[third], back.at[third], core_send.at[3 + third], core_recv.at[3 + third], other_core()))
    mine = repack(out, grad)
    for third in range(3):
        pushes[3 + third].wait_recv()
        joined_ref[:, third * HW : (third + 1) * HW] = (mine[third] + back[third].astype(F32)).astype(BF16)
    for copy in pushes + list(copies.values()):
        copy.wait_send()


def whole(kernel, outs, scratch=(), flops=0, moved=0, collective=None):
    remote_params = {} if collective is None else {"collective_id": collective, "has_side_effects": True}
    return pl.pallas_call(
        kernel,
        out_shape=[jax.ShapeDtypeStruct(shape, kind) for shape, kind in outs],
        scratch_shapes=list(scratch),
        compiler_params=pltpu.CompilerParams(vmem_limit_bytes=VMEM_LIMIT, **remote_params),
        cost_estimate=pl.CostEstimate(flops=flops, bytes_accessed=moved, transcendentals=0),
    )


def swap(values, axis="sp"):
    return lax.all_to_all(values, axis, split_axis=0, concat_axis=0, tiled=True)


def shards(tokens, cotangent, w_query, w_key, w_value, w_output, gain_attn, gain_ffn, router, bias_table, w_in, w_out, routes, buckets):
    count = tokens.shape[1]
    seq = 2 * count
    owners = lax.axis_size("ep")
    tok = tokens[0]
    cot = cotangent[0]
    route = routes[0]
    pack, sequence = whole(
        gather_kernel,
        [((SIDE, SIDE, SIDE, QROW, PW), BF16), ((2, count, D), BF16)],
        scratch=[
            pltpu.VMEM((2, QROW, PW), BF16),
            pltpu.VMEM((QROW, PW), BF16),
            pltpu.VMEM((QROW, D), BF16),
            pltpu.SemaphoreType.DMA((2,)),
            pltpu.SemaphoreType.DMA((2,)),
            pltpu.SemaphoreType.DMA((3, 3, SIDE - 1)),
            pltpu.SemaphoreType.DMA((3, 3, SIDE - 1)),
        ],
        flops=10**6,
        moved=6 * 10**6,
        collective=0,
    )(w_query, w_key, w_value, w_output, router, gain_attn[None], gain_ffn[None], bias_table[None], tok)
    pack = pack.reshape(owners * QROW, PW)
    sequence = sequence.reshape(seq, D)
    (output_mine, attended, qkv_all, full, gains, normed_attn, bias, lse, filled, resid, normed_ffn, places, gates) = whole(
        front_kernel,
        [
            ((HW, D), BF16),
            ((seq, HW), BF16),
            ((seq, QW), BF16),
            ((D, PW), BF16),
            ((128, D), F32),
            ((seq, D), BF16),
            ((16, seq), F32),
            ((seq, 128), F32),
            ((SLOTS, ROW), BF16),
            ((count, D), F32),
            ((count, D), BF16),
            ((count, 5 * SLOTS), BF16),
            ((count, 128), F32),
        ],
        scratch=[
            pltpu.VMEM((2, count, D), F32),
            pltpu.VMEM((count, D), F32),
            pltpu.SemaphoreType.DMA,
            pltpu.SemaphoreType.DMA,
        ],
        flops=6 * 10**9,
        moved=10 * 10**6,
        collective=2,
    )(sequence, pack, buckets[None], tok, cot, route)

    load = 2 * EXP * CAP
    hidden = w_in.shape[2]
    step = 256
    resident = pl.BlockSpec((load, 2 * D), lambda f: (0, 0))
    by_column = pl.BlockSpec((load, step), lambda f: (0, f))
    in_vmem = pl.BlockSpec(memory_space=pltpu.VMEM)
    anywhere = pl.BlockSpec(memory_space=pl.ANY)
    exchanged = pltpu.VMEM((SIDE, SIDE, SIDE, SLOT, ROW), BF16)
    rows, act, d_pre, joined = pl.pallas_call(
        expert_kernel,
        in_specs=[in_vmem, anywhere, anywhere],
        out_specs=[in_vmem] * 4,
        out_shape=[
            jax.ShapeDtypeStruct((load, 2 * D), BF16),
            jax.ShapeDtypeStruct((load, hidden), BF16),
            jax.ShapeDtypeStruct((load, hidden), BF16),
            jax.ShapeDtypeStruct((SLOTS, ROW), BF16),
        ],
        scratch_shapes=[exchanged] * 4
        + [
            pltpu.VMEM((D, hidden), BF16),
            pltpu.VMEM((hidden, D), BF16),
            pltpu.VMEM((3, SLOTS, HW), BF16),
            pltpu.VMEM((3, SLOTS, HW), BF16),
            pltpu.SemaphoreType.DMA((2,)),
            pltpu.SemaphoreType.DMA((3, 3)),
            pltpu.SemaphoreType.DMA((6,)),
            pltpu.SemaphoreType.DMA((6,)),
            pltpu.SemaphoreType.DMA((3, 3, SIDE - 1)),
            pltpu.SemaphoreType.DMA((3, 3, SIDE - 1)),
        ],
        compiler_params=pltpu.CompilerParams(vmem_limit_bytes=VMEM_LIMIT, collective_id=4, has_side_effects=True),
        cost_estimate=pl.CostEstimate(flops=8 * load * D * hidden, bytes_accessed=20 * 10**6, transcendentals=load * hidden),
    )(filled.reshape(SIDE, SIDE, SIDE, SLOT, ROW), w_in, w_out)
    returned = swap(joined.reshape(owners, SLOT, ROW), "ep").reshape(SLOTS, ROW)

    grad_w_in, grad_w_out = pl.pallas_call(
        expert_grad_kernel,
        grid=(hidden // step,),
        in_specs=[resident, by_column, by_column],
        out_specs=[
            pl.BlockSpec((1, D, step), lambda f: (0, 0, f)),
            pl.BlockSpec((1, step, D), lambda f: (0, f, 0)),
        ],
        out_shape=[
            jax.ShapeDtypeStruct((1, D, hidden), F32),
            jax.ShapeDtypeStruct((1, hidden, D), F32),
        ],
        scratch_shapes=[pltpu.VMEM((D, load), BF16)],
        compiler_params=pltpu.CompilerParams(vmem_limit_bytes=VMEM_LIMIT),
        cost_estimate=pl.CostEstimate(flops=4 * load * D * hidden, bytes_accessed=20 * 10**6, transcendentals=0),
    )(rows, act, d_pre)

    mixed, d_resid, g_pack, d_norm = whole(
        back_kernel,
        [
            ((1, count, D), BF16),
            ((count, D), F32),
            ((owners * QROW, PW), BF16),
            ((2, count, D), F32),
        ],
        scratch=[
            pltpu.VMEM((2, count, D), BF16),
            pltpu.VMEM((seq, QW), BF16),
            pltpu.VMEM((16, seq), F32),
            pltpu.SemaphoreType.DMA,
            pltpu.SemaphoreType.DMA,
        ],
        flops=8 * 10**9,
        moved=12 * 10**6,
        collective=3,
    )(returned, places, gates, resid, cot, gains, full, normed_ffn, route, output_mine, attended, qkv_all, lse, bias, normed_attn, sequence, buckets[None])

    widths = [width for _, width, _ in PARTS]
    g_query, g_key, g_value, g_output, rest, d_tokens = whole(
        reduce_kernel,
        [((6, D), F32)] * 4 + [((6, 128), F32), ((1, count, D), F32)],
        scratch=[pltpu.VMEM((SIDE - 1, SIDE, SIDE, QROW, width), BF16) for width in widths]
        + [pltpu.VMEM((SIDE, SIDE, QROW, width), BF16) for width in widths]
        + [pltpu.VMEM((SIDE - 1, SIDE, QROW, width), BF16) for width in widths]
        + [pltpu.VMEM((SIDE, QROW, width), BF16) for width in widths]
        + [pltpu.VMEM((SIDE - 1, QROW, width), BF16) for width in widths]
        + [pltpu.VMEM((QROW, PW), F32)] * 2
        + [pltpu.VMEM((count, D), F32)]
        + [pltpu.SemaphoreType.DMA((2,))] * 2
        + [pltpu.SemaphoreType.DMA((3, 3, SIDE - 1))] * 2,
        flops=10**7,
        moved=6 * 10**6,
        collective=1,
    )(g_pack.reshape(SIDE, SIDE, SIDE, QROW, PW), d_norm, d_resid, tok, gains)
    extra = rest[:, 64:70]
    return (
        mixed,
        d_tokens,
        g_query,
        g_key,
        g_value,
        g_output,
        extra[:, 0] + extra[:, 1],
        extra[:, 2] + extra[:, 3],
        rest[:, :EXP],
        (extra[:, 4] + extra[:, 5])[:3],
        grad_w_in,
        grad_w_out,
    )


def solution(mesh):
    wide = P(("sp", "ep"), None)
    flat = P(("sp", "ep"))
    rows = P("ep", "sp", None)
    return jax.shard_map(
        shards,
        mesh=mesh,
        in_specs=(rows, rows, wide, wide, wide, wide, flat, flat, wide, flat, P("ep", None, "sp"), rows, rows, P()),
        out_specs=(rows, rows, wide, wide, wide, wide, flat, flat, wide, flat, P("ep", None, "sp"), rows),
        check_vma=False,
    )
```

```python
import functools

import jax
import jax.numpy as jnp
from jax import lax
from jax.experimental import pallas as pl
from jax.experimental.pallas import tpu as pltpu
from jax.sharding import PartitionSpec as P

D = 768
H = 12
HD = 64
HH = H // 2
HW = HH * HD
EXP = 64
EPS = 1e-06
CAP = 6
SLOT = 8
SLOTS = EXP * SLOT
BIG = 256
SMALL = 128
QROW = 16
QW = 3 * HW
PW = QW + 128
SIDE = 4
STRIDES = (16, 4, 1)
PARTS = ((0, 512, (2, 1, 0)), (512, 384, (0, 2, 1)), (896, 384, (1, 0, 2)))
MESH = pl.DeviceIdType.MESH
ROUTER = QW
GAIN = QW + 64
F32 = jnp.float32
BF16 = jnp.bfloat16
VMEM_LIMIT = 56 * 1024 * 1024


def iota(shape, axis):
    return lax.broadcasted_iota(jnp.int32, shape, axis)


def nn(left, right):
    return lax.dot_general(left, right, (((1,), (0,)), ((), ())), preferred_element_type=F32)


def nt(left, right):
    return lax.dot_general(left, right, (((1,), (1,)), ((), ())), preferred_element_type=F32)


def tn(left, right):
    return lax.dot_general(left, right, (((0,), (0,)), ((), ())), preferred_element_type=F32)


def chunk_feature(rows):
    owner = jnp.right_shift(rows, 4)
    inner = jnp.bitwise_and(rows, 15)
    half = (inner >= 6).astype(jnp.int32)
    feature = half * (D // 2) + owner * 6 + inner - 6 * half
    return jnp.where(inner < 12, feature, -1)


def chunk_entry(rows):
    owner = jnp.right_shift(rows, 4)
    inner = jnp.bitwise_and(rows, 15)
    half = (inner >= 6).astype(jnp.int32)
    inside = inner - 6 * half
    entry = half * (32 * H // 2) + owner * 3 + inside
    return jnp.where((inner < 12) & (inside < 3), entry, -1)


def hot(condition):
    return jnp.where(condition, 1.0, 0.0).astype(BF16)


def to_chunks():
    return hot(chunk_feature(iota((1, EXP * QROW), 1)) == iota((D, EXP * QROW), 0))


def from_chunks():
    return hot(chunk_feature(iota((EXP * QROW, 1), 0)) == iota((EXP * QROW, D), 1))


def output_row(channel, half, third):
    owner = jnp.right_shift(channel * 10923, 16)
    inner = channel - owner * 6
    later = (inner >= 3).astype(jnp.int32)
    row = owner * QROW + 12 + 2 * later + half
    return jnp.where(inner - 3 * later == third, row, -1)


def rms_of(values):
    return lax.rsqrt(jnp.mean(values * values, axis=-1, keepdims=True) + EPS)


def head_bias(bias_ref, head, seq):
    row = jnp.broadcast_to(bias_ref[head : head + 1, :], (seq, seq))
    return pltpu.roll(row, 0, 1, stride=1, stride_axis=0)


def front_kernel(seq_ref, pack_ref, bucket_ref, tok_ref, cot_ref, routes_ref, output_ref, attended_ref, qkv_ref, full_ref, gains_ref, normed_ref, bias_ref, lse_ref, *rest):
    middle, (halves, got, send, recv) = rest[:6], rest[6:]
    greet_core()
    seq = seq_ref.shape[0]
    sp = lax.axis_index("sp")
    spread = to_chunks()
    full_ref[...] = nn(spread, pack_ref[...]).astype(BF16)
    tail = pack_ref[:, QW:]
    gains = tn(tail, from_chunks())
    gains_ref[...] = gains
    entry = chunk_entry(iota((EXP * QROW, 1), 0))
    bucket_of = jnp.right_shift(entry * 5462, 16)
    head_of = entry - bucket_of * H
    column = iota((EXP * QROW, 128), 1)
    table = jnp.where(
        (entry >= 0) & (head_of == sp * HH + column) & (column < HH),
        tail[:, 66:67].astype(F32),
        0.0,
    ).astype(BF16)
    bucket_here = jnp.where(entry >= 0, bucket_of, -1)
    by_distance = tn(table, hot(bucket_here == bucket_ref[...]))[0:16, :].astype(BF16)
    turn = hot(jnp.bitwise_and(iota((seq, seq), 0) + iota((seq, seq), 1), seq - 1) == 0)
    bias_ref[...] = nn(by_distance, turn)
    channel = iota((HW, 1), 0)
    for half in range(2):
        rows = jnp.zeros((HW, HW), F32)
        for third in range(3):
            pick = hot(output_row(channel, half, third) == iota((HW, EXP * QROW), 1))
            rows = rows + nn(pick, pack_ref[:, third * HW : (third + 1) * HW])
        output_ref[:, half * HW : (half + 1) * HW] = rows.astype(BF16)

    inputs = seq_ref[...].astype(F32)
    normed = (inputs * rms_of(inputs) * gains[64:65, :]).astype(BF16)
    normed_ref[...] = normed
    qkv_ref[...] = nn(normed, full_ref[:, :QW]).astype(BF16)
    causal = iota((seq, seq), 1) <= iota((seq, seq), 0)
    lse_ref[...] = jnp.zeros_like(lse_ref)
    for head in range(HH):
        at = head * HD
        query = qkv_ref[:, at : at + HD]
        key = qkv_ref[:, HW + at : HW + at + HD]
        value = qkv_ref[:, 2 * HW + at : 2 * HW + at + HD]
        scores = nt(query, key) * (HD**-0.5) + head_bias(bias_ref, head, seq)
        scores = jnp.where(causal, scores, -jnp.inf)
        peak = jnp.max(scores, axis=-1, keepdims=True)
        grown = jnp.exp(scores - peak)
        total = jnp.sum(grown, axis=-1, keepdims=True)
        probs = (grown / total).astype(BF16)
        attended_ref[:, at : at + HD] = nn(probs, value).astype(BF16)
        lse_ref[:, head : head + 1] = peak + jnp.log(total)
    count = seq // 2
    meet_core()
    halves[...] = nn(attended_ref[...], output_ref[...]).reshape(halves.shape)
    copy = remote(halves.at[1 - sp], got, send, recv, other_core())
    copy.wait_recv()
    resid = tok_ref[...].astype(F32) + halves[sp] + got[...]
    middle_part(resid, cot_ref, gains_ref, full_ref, routes_ref, *middle)
    copy.wait_send()


def route_hot(routes_ref, k, width):
    return (routes_ref[:, k : k + 1] == iota((routes_ref.shape[0], width), 1)).astype(F32)


def middle_part(resid, cot_ref, gains_ref, full_ref, routes_ref, big_ref, small_ref, resid_ref, normed_ref, places_ref, gates_ref):
    count = resid.shape[0]
    resid_ref[...] = resid
    normed = (resid * rms_of(resid) * gains_ref[65:66, :]).astype(BF16)
    normed_ref[...] = normed
    logits = nn(normed, full_ref[:, ROUTER : ROUTER + EXP])
    named = [route_hot(routes_ref, k, EXP) for k in range(2)]
    chosen = [jnp.sum(logits * one, axis=-1, keepdims=True) for one in named]
    peak = jnp.maximum(chosen[0], chosen[1])
    grown = [jnp.exp(one - peak) for one in chosen]
    total = grown[0] + grown[1]
    gates = [one / total for one in grown]
    column = iota((count, 128), 1)
    gates_ref[...] = jnp.where(column == 0, gates[0], jnp.where(column == 1, gates[1], 0.0))
    before = hot(iota((count, count), 1) < iota((count, count), 0))
    earlier = nn(before, (named[0] + named[1]).astype(BF16))
    upstream = cot_ref[...].astype(F32)
    slots = iota((count, SLOTS), 1)
    slots_turned = iota((SLOTS, count), 0)
    starts = []
    for k in range(2):
        rank = jnp.sum(earlier * named[k], axis=-1, keepdims=True)
        start = routes_ref[:, k : k + 1].astype(F32) * SLOT
        upper = (rank >= 3).astype(F32)
        starts.append(start + rank)
        starts += [jnp.where(rank - 3 * upper == third, start + CAP + upper, -1.0) for third in range(3)]
    table = jnp.full((count, 128), -1.0, F32)
    for n, start in enumerate(starts):
        places_ref[:, n * SLOTS : (n + 1) * SLOTS] = hot(slots == start.astype(jnp.int32))
        table = jnp.where(column == n, start, table)
    turned = table.T.astype(jnp.int32)
    place = [hot(slots_turned == turned[n : n + 1, :]) for n in range(8)]
    spread = [(gates[k] * upstream).astype(BF16) for k in range(2)]
    either = place[0] + place[4]
    for third in range(3):
        there = slice(third * BIG, (third + 1) * BIG)
        big = nn(either, normed[:, there])
        there_small = slice(third * SMALL, (third + 1) * SMALL)
        small = 0.0
        for k in range(2):
            tail = place[4 * k + 1 + third]
            big = big + nn(tail, spread[k][:, D - BIG :])
            small = small + nn(place[4 * k], spread[k][:, there_small]) + nn(tail, spread[k][:, 3 * SMALL : 4 * SMALL])
        big_ref[:, there] = big.astype(BF16)
        small_ref[:, there_small] = small.astype(BF16)


GROUP = 32
LOAD = GROUP * CAP
HELD = GROUP * SLOT


def unpacking(turned):
    axis = 1 if turned else 0
    row = iota((1, LOAD) if turned else (LOAD, 1), axis)
    slots = iota((HELD, LOAD) if turned else (LOAD, HELD), 1 - axis)
    owner = jnp.right_shift(row * 10923, 16)
    inner = row - owner * CAP
    upper = (inner >= 3).astype(jnp.int32)
    tails = [hot(slots == jnp.where(inner - 3 * upper == third, owner * SLOT + CAP + upper, -1)) for third in range(3)]
    return hot(slots == owner * SLOT + inner), tails


def expert_grad_kernel(turned_ref, drows_ref, act_ref, dpre_ref, gin_ref, gout_ref):
    gin_ref[0] = nn(turned_ref[...], dpre_ref[...])
    gout_ref[0] = nn(act_ref[...], drows_ref[...])


def split_two(values):
    high = values.astype(BF16)
    return high, (values - high.astype(F32)).astype(BF16)


def back_kernel(big_ref, small_ref, places_ref, gates_ref, resid_ref, cot_ref, gains_ref, full_ref, ffn_ref, routes_ref, wo_ref, attended_ref, qkv_ref, lse_ref, bias_ref, normed_ref, seq_ref, bucket_ref, mixed_ref, dresid_ref, pack_ref, dnorm_ref, branch_ref, dqkv, ddist, send, recv):
    greet_core()
    count = resid_ref.shape[0]
    sp = lax.axis_index("sp")
    resid = resid_ref[...]
    upstream = cot_ref[...].astype(F32)
    gates = [gates_ref[:, k : k + 1] for k in range(2)]
    outs = []
    for k in range(2):
        last, most = 0.0, 0.0
        for third in range(3):
            at = 4 * k + 1 + third
            tail = places_ref[:, at * SLOTS : (at + 1) * SLOTS]
            last = last + nn(tail, small_ref[:, third * SMALL : (third + 1) * SMALL])
            most = most + nn(tail, big_ref[:, third * BIG : (third + 1) * BIG])
        outs.append(jnp.concatenate([nn(places_ref[:, 4 * k * SLOTS : (4 * k + 1) * SLOTS], small_ref[...]), last, most], axis=1))
    mixed_ref[0] = (resid + (gates[0] * outs[0] + gates[1] * outs[1])).astype(BF16)
    d_gates = [jnp.sum(one * upstream, axis=-1, keepdims=True) for one in outs]
    inner = gates[0] * d_gates[0] + gates[1] * d_gates[1]
    d_logits = jnp.zeros((count, EXP), F32)
    for k in range(2):
        d_logits = d_logits + route_hot(routes_ref, k, EXP) * (gates[k] * (d_gates[k] - inner))
    d_logits = d_logits.astype(BF16)
    either = places_ref[:, :SLOTS] + places_ref[:, 4 * SLOTS : 5 * SLOTS]
    d_normed = nn(either, big_ref[...])
    d_normed = d_normed + nt(d_logits, full_ref[:, ROUTER : ROUTER + EXP])
    rms = rms_of(resid)
    u = d_normed * gains_ref[65:66, :]
    d_resid = upstream + rms * u - resid * (rms * rms * rms) * jnp.mean(u * resid, axis=-1, keepdims=True)
    branch_ref[sp] = d_resid.astype(BF16)
    meet_core()
    copy = remote(branch_ref.at[sp], branch_ref.at[sp], send, recv, other_core())
    dresid_ref[...] = d_resid
    g_second = jnp.sum(d_normed * resid * rms, axis=0, keepdims=True)
    order = from_chunks()
    g_router = nn(order, tn(ffn_ref[...], d_logits).astype(BF16))
    turned = nt(order, normed_ref[...]).astype(BF16)
    copy.wait_recv()
    seq = seq_ref.shape[0]
    d_branch = branch_ref[...].reshape(seq, D)
    d_attended = nt(d_branch, wo_ref[...]).astype(BF16)
    causal = iota((seq, seq), 1) <= iota((seq, seq), 0)
    flip = hot(iota((seq, seq), 0) + iota((seq, seq), 1) == seq - 1)
    ddist[...] = jnp.zeros_like(ddist)
    for head in range(HH):
        at = head * HD
        query = qkv_ref[:, at : at + HD]
        key = qkv_ref[:, HW + at : HW + at + HD]
        value = qkv_ref[:, 2 * HW + at : 2 * HW + at + HD]
        d_out = d_attended[:, at : at + HD]
        scores = nt(query, key) * (HD**-0.5) + head_bias(bias_ref, head, seq)
        probs = jnp.where(causal, jnp.exp(scores - lse_ref[:, head : head + 1]), 0.0)
        d_value = tn(probs.astype(BF16), d_out)
        d_probs = nt(d_out, value)
        row_dot = jnp.sum(probs * d_probs, axis=-1, keepdims=True)
        d_scores = (probs * (d_probs - row_dot)).astype(BF16)
        dqkv[:, at : at + HD] = (nn(d_scores, key) * (HD**-0.5)).astype(BF16)
        dqkv[:, HW + at : HW + at + HD] = (tn(d_scores, query) * (HD**-0.5)).astype(BF16)
        dqkv[:, 2 * HW + at : 2 * HW + at + HD] = d_value.astype(BF16)
        skewed = pltpu.roll(nn(d_scores, flip), 0, 1, stride=1, stride_axis=0)
        ddist[head : head + 1, :] = jnp.sum(skewed, axis=0, keepdims=True)
    d_normed = nt(dqkv[...], full_ref[:, :QW])
    dnorm_ref[...] = d_normed.reshape(dnorm_ref.shape)
    g_output = tn(attended_ref[...], d_branch).astype(BF16)
    channel = iota((1, HW), 1)
    for third in range(3):
        there = slice(third * HW, (third + 1) * HW)
        total = nn(turned, dqkv[:, there])
        for half in range(2):
            place = hot(output_row(channel, half, third) == iota((EXP * QROW, HW), 0))
            total = total + nn(place, g_output[:, half * HW : (half + 1) * HW])
        pack_ref[:, there] = total.astype(BF16)
    inputs = seq_ref[...].astype(F32)
    g_first = jnp.sum(d_normed * inputs * rms_of(inputs), axis=0, keepdims=True)
    first_high, first_low = split_two(jnp.broadcast_to(g_first, (16, D)))
    second_high, second_low = split_two(jnp.broadcast_to(g_second, (16, D)))
    gains = [nt(order, one)[:, 0:1] for one in (first_high, first_low, second_high, second_low)]
    entry = chunk_entry(iota((EXP * QROW, 1), 0))
    bucket_of = jnp.right_shift(entry * 5462, 16)
    pick = hot(jnp.where(entry >= 0, bucket_of, -1) == bucket_ref[...])
    high, low = split_two(pltpu.roll(ddist[...], 1, 1))
    by_head = nt(pick, high) + nt(pick, low)
    head_of = entry - bucket_of * H
    mine = (entry >= 0) & (head_of == sp * HH + iota(by_head.shape, 1)) & (iota(by_head.shape, 1) < HH)
    table = jnp.sum(jnp.where(mine, by_head, 0.0), axis=-1, keepdims=True)
    table_high, table_low = split_two(table)
    column = iota((EXP * QROW, 64), 1)
    tail = jnp.zeros((EXP * QROW, 64), F32)
    for place, values in enumerate(gains + [table_high.astype(F32), table_low.astype(F32)]):
        tail = jnp.where(column == place, values, tail)
    pack_ref[:, QW:] = jnp.concatenate([g_router, tail], axis=1).astype(BF16)
    copy.wait_send()


def here():
    owner = lax.axis_index("ep")
    return (owner // 16, owner // 4 % 4, owner % 4)


def across(axis, shift):
    owner, place = lax.axis_index("ep"), here()[axis]
    return {"ep": owner + ((place + shift) % SIDE - place) * STRIDES[axis]}


def other_core():
    return {"sp": 1 - lax.axis_index("sp")}


def greet_core():
    pl.semaphore_signal(pltpu.get_barrier_semaphore(), inc=1, device_id=other_core(), device_id_type=MESH)


def meet_core():
    pl.semaphore_wait(pltpu.get_barrier_semaphore(), 1)


def greet():
    barrier = pltpu.get_barrier_semaphore()
    pl.semaphore_signal(barrier, inc=1, device_id=other_core(), device_id_type=MESH)
    for axis in range(3):
        for shift in range(1, SIDE):
            pl.semaphore_signal(barrier, inc=1, device_id=across(axis, shift), device_id_type=MESH)


def meet():
    pl.semaphore_wait(pltpu.get_barrier_semaphore(), 1 + 3 * (SIDE - 1))


def remote(source, target, send, receive, device):
    copy = pltpu.make_async_remote_copy(
        src_ref=source, dst_ref=target, send_sem=send, recv_sem=receive, device_id=device, device_id_type=MESH
    )
    copy.start()
    return copy


def gather_kernel(wq_ref, wk_ref, wv_ref, wo_ref, router_ref, attn_ref, ffn_ref, table_ref, tok_ref, pack_ref, seq_ref, stage, got, out16, core_send, core_recv, send, recv):
    greet()
    sp = lax.axis_index("sp")
    place = here()
    stage[...] = jnp.zeros_like(stage)
    out16[...] = jnp.zeros_like(out16)
    out16[0:6, :] = wo_ref[...]

    def standing(ref):
        size = ref.shape[1]
        values = jnp.broadcast_to(ref[...].astype(F32), (QROW, size))
        kept = jnp.where(iota((QROW, size), 0) == iota((QROW, size), 1), values, 0.0)
        return jnp.sum(kept, axis=1, keepdims=True)

    column = iota((QROW, 64), 1)
    tail = jnp.where(column == 0, standing(attn_ref), 0.0)
    tail = jnp.where(column == 1, standing(ffn_ref), tail)
    tail = jnp.where(column == 2, standing(table_ref), tail).astype(BF16)
    for half in range(2):
        for n, ref in enumerate((wq_ref, wk_ref, wv_ref)):
            stage[half, 0:6, n * HW : (n + 1) * HW] = ref[:, half * HW : (half + 1) * HW]
        stage[half, 0:6, ROUTER : ROUTER + EXP] = router_ref[...]
        stage[half, :, GAIN:] = tail
    seq_ref[sp] = tok_ref[...]
    meet()
    chunk_copy = remote(stage.at[1 - sp], got, core_send.at[0], core_recv.at[0], other_core())
    tok_copy = remote(tok_ref, seq_ref.at[sp], core_send.at[1], core_recv.at[1], other_core())
    row, col = iota((QROW, QROW), 0), iota((QROW, QROW), 1)
    low = jnp.where((row == col) & (col < 6), 1.0, 0.0)
    high = jnp.where((row == col + 6) & (col < 6), 1.0, 0.0)
    own = jnp.where(sp == 0, low, high).astype(BF16)
    others = jnp.where(sp == 0, high, low).astype(BF16)
    later = (col >= 3).astype(jnp.int32)
    chunk_copy.wait()
    mine = nn(own, stage[sp]) + nn(others, got[...])
    pack_ref[place[0], place[1], place[2], :, QW:] = mine[:, QW:].astype(BF16)
    for third in range(3):
        there = slice(third * HW, (third + 1) * HW)
        total = mine[:, there]
        for half in range(2):
            pick = hot((col < 6) & (col - 3 * later == third) & (row == 12 + 2 * later + half))
            total = total + nn(pick, out16[:, half * HW : (half + 1) * HW])
        pack_ref[place[0], place[1], place[2], :, there] = total.astype(BF16)
    copies = {}
    for phase in range(3):
        for part, (first, width, order) in enumerate(PARTS):
            index = [pl.ds(0, SIDE) if axis in order[:phase] else place[axis] for axis in range(3)]
            block = pack_ref.at[index[0], index[1], index[2], :, pl.ds(first, width)]
            if phase:
                for shift in range(1, SIDE):
                    copies[phase - 1, part, shift].wait_recv()
            for shift in range(1, SIDE):
                copies[phase, part, shift] = remote(
                    block, block, send.at[phase, part, shift - 1], recv.at[phase, part, shift - 1], across(order[phase], shift)
                )
    for part in range(3):
        for shift in range(1, SIDE):
            copies[2, part, shift].wait_recv()
    for copy in copies.values():
        copy.wait_send()
    tok_copy.wait()


def reduce_kernel(pack_ref, dnorm_ref, dresid_ref, tok_ref, gains_ref, total, theirs, dtok_ref, *scratch):
    firsts, sums, seconds, pairs, thirds = (scratch[3 * n : 3 * n + 3] for n in range(5))
    got, core_send, core_recv, send, recv = scratch[15:]
    greet()
    sp = lax.axis_index("sp")
    place = here()
    meet()
    copies = {}

    def push(phase, part, axis, shift, source, target):
        copies[phase, part, shift] = remote(
            source,
            target.at[shift - 1],
            send.at[phase, part, shift - 1],
            recv.at[phase, part, shift - 1],
            across(axis, shift),
        )

    def added(phase, part, own, arrived):
        values = own.astype(F32)
        for shift in range(1, SIDE):
            copies[phase, part, shift].wait_recv()
            values = values + arrived[shift - 1].astype(F32)
        return values

    def at(axes, axis, value):
        return tuple(value if one == axis else pl.ds(0, SIDE) for one in axes)

    for part, (first, width, order) in enumerate(PARTS):
        axis = order[2]
        for shift in (2, 1, 3):
            index = at((0, 1, 2), axis, (place[axis] + shift) % SIDE)
            push(0, part, axis, shift, pack_ref.at[index + (slice(None), pl.ds(first, width))], firsts[part])
    norm_copy = remote(dnorm_ref.at[1 - sp], got, core_send.at[1], core_recv.at[1], other_core())
    norm_copy.wait_recv()
    inputs = tok_ref[...].astype(F32)
    d_normed = dnorm_ref[sp] + got[...]
    rms = rms_of(inputs)
    v = d_normed * gains_ref[64:65, :]
    drop = inputs * (rms * rms * rms) * jnp.mean(v * inputs, axis=-1, keepdims=True)
    dtok_ref[0] = dresid_ref[...] + rms * v - drop
    for part, (first, width, order) in enumerate(PARTS):
        own = pack_ref[at((0, 1, 2), order[2], place[order[2]]) + (slice(None), pl.ds(first, width))]
        sums[part][...] = added(0, part, own, firsts[part]).astype(BF16)
        axis = order[1]
        for shift in (2, 1, 3):
            index = at(sorted(order[:2]), axis, (place[axis] + shift) % SIDE)
            push(1, part, axis, shift, sums[part].at[index], seconds[part])
    for part, (first, width, order) in enumerate(PARTS):
        own = sums[part][at(sorted(order[:2]), order[1], place[order[1]])]
        pairs[part][...] = added(1, part, own, seconds[part]).astype(BF16)
        axis = order[0]
        for shift in (2, 1, 3):
            push(2, part, axis, shift, pairs[part].at[(place[axis] + shift) % SIDE], thirds[part])
    for part, (first, width, order) in enumerate(PARTS):
        own = pairs[part][place[order[0]]]
        total[:, first : first + width] = added(2, part, own, thirds[part])
    core = remote(total, theirs, core_send.at[0], core_recv.at[0], other_core())
    core.wait_recv()
    core.wait_send()
    norm_copy.wait_send()
    for copy in copies.values():
        copy.wait_send()


class Wave:
    ORDERS = ((2, 1, 0), (0, 2, 1), (1, 0, 2))

    def __init__(self, width, buffers, send, recv, local):
        self.width, self.buffers, self.send, self.recv, self.local = width, buffers, send, recv, local
        self.place, self.copies, self.kept = here(), {}, {}

    def block(self, ref, axis, value, third):
        index = tuple(value if other == axis else pl.ds(0, SIDE) for other in range(3))
        return ref.at[index + (slice(None), pl.ds(third * self.width, self.width))]

    def step(self, phase):
        for third, order in enumerate(self.ORDERS):
            if phase:
                self.settle(phase - 1, third)
            axis = order[phase]
            source, target = self.buffers[phase], self.buffers[phase + 1]
            spot = self.place[axis]
            for shift in (2, 1, 3):
                self.copies[phase, third, shift] = remote(
                    self.block(source, axis, (spot + shift) % SIDE, third),
                    self.block(target, axis, spot, third),
                    self.send.at[phase, third, shift - 1],
                    self.recv.at[phase, third, shift - 1],
                    across(axis, shift),
                )
            own = pltpu.make_async_copy(
                self.block(source, axis, spot, third), self.block(target, axis, spot, third), self.local.at[phase, third]
            )
            own.start()
            self.kept[phase, third] = own

    def settle(self, phase, third):
        for shift in range(1, SIDE):
            self.copies[phase, third, shift].wait_recv()
        self.kept[phase, third].wait()

    def land(self):
        for third in range(3):
            self.settle(2, third)

    def push(self, target, send, recv):
        source = self.buffers[3]
        pushes = []
        for third in range(3):
            self.settle(2, third)
            columns = (slice(None),) * 4 + (pl.ds(third * self.width, self.width),)
            pushes.append(remote(source.at[columns], target.at[columns], send.at[third], recv.at[third], other_core()))
        return pushes

    def sent(self):
        for copy in self.copies.values():
            copy.wait_send()


def expert_kernel(big_ref, small_ref, win_hbm, wout_hbm, turned_ref, drows_ref, act_ref, dpre_ref, back_big_ref, back_small_ref, *scratch):
    big_mid, small_mid, rbig_mid, rsmall_mid = (scratch[2 * n : 2 * n + 2] for n in range(4))
    big_here, small_here, big_theirs, small_theirs, rbig_first, rsmall_first = scratch[8:14]
    rows, act, bend, win, wout, win_turned, wout_turned, big_out, small_out, big_in, small_in = scratch[14:25]
    load_sem, core_send, core_recv, local, send, recv = scratch[25:]
    greet()
    loads = [pltpu.make_async_copy(win_hbm.at[0], win, load_sem.at[0]), pltpu.make_async_copy(wout_hbm.at[0], wout, load_sem.at[1])]
    for load in loads:
        load.start()

    def wave(n, width, buffers):
        return Wave(width, buffers, send.at[n], recv.at[n], local.at[n])

    big = wave(0, BIG, (big_ref, *big_mid, big_here))
    small = wave(1, SMALL, (small_ref, *small_mid, small_here))
    back_small = wave(2, SMALL, (rsmall_first, *rsmall_mid, back_small_ref))
    back_big = wave(3, BIG, (rbig_first, *rbig_mid, back_big_ref))
    meet()
    for phase in range(3):
        big.step(phase)
        small.step(phase)
    for load in loads:
        load.wait()
    win_turned[...] = win[...].T
    wout_turned[...] = wout[...].T
    pushes = big.push(big_theirs, core_send.at[0], core_recv.at[0])
    main, tails = unpacking(False)
    main_turned, tails_turned = unpacking(True)
    load = EXP * CAP
    hidden = win.shape[1]
    step = 512

    def groups(half, ref, width):
        packed = ref[...].reshape(SLOTS, 3 * width)
        for group in range(2):
            held = packed[group * HELD : (group + 1) * HELD]
            rest = 0.0
            for third in range(3):
                rest = rest + nn(tails[third], held[:, third * width : (third + 1) * width])
            first = half * load + group * LOAD
            yield slice(first, first + LOAD), nn(main, held).astype(BF16), rest.astype(BF16)

    def forward(half, source):
        there = slice(half * load, (half + 1) * load)
        for where, first, rest in groups(half, source, BIG):
            rows[where, :] = first
            drows_ref[where, D - BIG :] = rest
        normed = rows[there, :]
        for start in range(0, hidden, step):
            columns = slice(start, start + step)
            pre = nn(normed, win[:, columns])
            square = pre * pre
            slope = 0.7978845608028654
            upper = 0.5 + 0.5 * jnp.tanh(pre * (slope + (slope * 0.044715) * square))
            grown = pre * upper
            act[there, columns] = grown.astype(BF16)
            bend[there, columns] = upper + grown * (1.0 - upper) * (2 * slope + (6 * slope * 0.044715) * square)
        return nn(act[there, :], wout[...]).astype(BF16)

    def backward(half, source):
        there = slice(half * load, (half + 1) * load)
        for where, first, rest in groups(half, source, SMALL):
            drows_ref[where, : 3 * SMALL] = first
            drows_ref[where, 3 * SMALL : 4 * SMALL] = rest
        d_rows = drows_ref[there, :]
        for start in range(0, hidden, step):
            columns = slice(start, start + step)
            dpre_ref[there, columns] = (nn(d_rows, wout_turned[:, columns]) * bend[there, columns]).astype(BF16)
        return nn(dpre_ref[there, :], win_turned[...]).astype(BF16)

    def pack(values, last, width):
        for third in range(3):
            for group in range(2):
                there = slice(group * LOAD, (group + 1) * LOAD)
                own = nn(main_turned, values[there, third * width : (third + 1) * width])
                yield third, group, own + nn(tails_turned[third], last[there, :])

    def pack_small(out):
        return pack(out, out[:, 3 * SMALL : 4 * SMALL], SMALL)

    def pack_big(grad, out):
        return pack(grad, out[:, D - BIG :], BIG)

    def hand_over(packed, outgoing, incoming, n):
        copies = []
        for third, group, values in packed:
            outgoing[third, group * HELD : (group + 1) * HELD] = values.astype(BF16)
            if group:
                copies.append(
                    remote(outgoing.at[third], incoming.at[third], core_send.at[n, third], core_recv.at[n, third], other_core())
                )
        return copies

    def join(packed, incoming, copies, target, width):
        for third, group, values in packed:
            if group == 0:
                copies[third].wait_recv()
            total = (values + incoming[third, group * HELD : (group + 1) * HELD].astype(F32)).astype(BF16)
            target[2 * group : 2 * group + 2, :, :, :, third * width : (third + 1) * width] = total.reshape(
                SIDE // 2, SIDE, SIDE, SLOT, width
            )

    out = forward(0, big_here)
    for push in pushes:
        push.wait_recv()
    pushes += small.push(small_theirs, core_send.at[1], core_recv.at[1])
    out_theirs = forward(1, big_theirs)
    small_copies = hand_over(pack_small(out_theirs), small_out, small_in, 2)
    grad = backward(0, small_here)
    join(pack_small(out), small_in, small_copies, rsmall_first, SMALL)
    back_small.step(0)
    for push in pushes[3:]:
        push.wait_recv()
    grad_theirs = backward(1, small_theirs)
    big_copies = hand_over(pack_big(grad_theirs, out_theirs), big_out, big_in, 3)
    back_small.step(1)
    join(pack_big(grad, out), big_in, big_copies, rbig_first, BIG)
    back_big.step(0)
    back_small.step(2)
    turned_ref[...] = rows[...].T
    back_big.step(1)
    act_ref[...] = act[...].T
    back_big.step(2)
    back_small.land()
    back_big.land()
    for copy in pushes + small_copies + big_copies:
        copy.wait_send()
    for one in (big, small, back_small, back_big):
        one.sent()


def end_kernel(total_ref, theirs_ref, dtok_ref, mixed_ref, q_ref, k_ref, v_ref, o_ref, rest_ref, dtok_out, mixed_out):
    sp = lax.axis_index("sp")
    dtok_out[...] = dtok_ref[...]
    mixed_out[...] = mixed_ref[...]
    total, theirs = total_ref, theirs_ref
    for row in range(6):
        for half in range(2):
            there = 12 + row // 3 * 2 + half
            third = row % 3 * HW
            o_ref[row : row + 1, half * HW : (half + 1) * HW] = total[there : there + 1, third : third + HW]
    mine = jnp.where(sp == 0, total[0:6, :], total[6:12, :])
    other = jnp.where(sp == 0, theirs[0:6, :], theirs[6:12, :])
    for n, ref in enumerate((q_ref, k_ref, v_ref)):
        there = slice(n * HW, (n + 1) * HW)
        ref[:, :HW] = jnp.where(sp == 0, mine[:, there], other[:, there])
        ref[:, HW:] = jnp.where(sp == 0, other[:, there], mine[:, there])
    rest_ref[...] = mine[:, QW:] + other[:, QW:]


def whole(kernel, outs, scratch=(), flops=0, moved=0, collective=None):
    remote_params = {} if collective is None else {"collective_id": collective, "has_side_effects": True}
    return pl.pallas_call(
        kernel,
        out_shape=[jax.ShapeDtypeStruct(shape, kind) for shape, kind in outs],
        scratch_shapes=list(scratch),
        compiler_params=pltpu.CompilerParams(vmem_limit_bytes=VMEM_LIMIT, **remote_params),
        cost_estimate=pl.CostEstimate(flops=flops, bytes_accessed=moved, transcendentals=0),
    )


def swap(values, axis="sp"):
    return lax.all_to_all(values, axis, split_axis=0, concat_axis=0, tiled=True)


def shards(tokens, cotangent, w_query, w_key, w_value, w_output, gain_attn, gain_ffn, router, bias_table, w_in, w_out, routes, buckets):
    count = tokens.shape[1]
    seq = 2 * count
    owners = lax.axis_size("ep")
    tok = tokens[0]
    cot = cotangent[0]
    route = routes[0]
    pack, sequence = whole(
        gather_kernel,
        [((SIDE, SIDE, SIDE, QROW, PW), BF16), ((2, count, D), BF16)],
        scratch=[
            pltpu.VMEM((2, QROW, PW), BF16),
            pltpu.VMEM((QROW, PW), BF16),
            pltpu.VMEM((QROW, D), BF16),
            pltpu.SemaphoreType.DMA((2,)),
            pltpu.SemaphoreType.DMA((2,)),
            pltpu.SemaphoreType.DMA((3, 3, SIDE - 1)),
            pltpu.SemaphoreType.DMA((3, 3, SIDE - 1)),
        ],
        flops=10**6,
        moved=6 * 10**6,
        collective=0,
    )(w_query, w_key, w_value, w_output, router, gain_attn[None], gain_ffn[None], bias_table[None], tok)
    pack = pack.reshape(owners * QROW, PW)
    sequence = sequence.reshape(seq, D)
    (output_mine, attended, qkv_all, full, gains, normed_attn, bias, lse, big, small, resid, normed_ffn, places, gates) = whole(
        front_kernel,
        [
            ((HW, D), BF16),
            ((seq, HW), BF16),
            ((seq, QW), BF16),
            ((D, PW), BF16),
            ((128, D), F32),
            ((seq, D), BF16),
            ((16, seq), F32),
            ((seq, 128), F32),
            ((SLOTS, 3 * BIG), BF16),
            ((SLOTS, 3 * SMALL), BF16),
            ((count, D), F32),
            ((count, D), BF16),
            ((count, 8 * SLOTS), BF16),
            ((count, 128), F32),
        ],
        scratch=[
            pltpu.VMEM((2, count, D), F32),
            pltpu.VMEM((count, D), F32),
            pltpu.SemaphoreType.DMA,
            pltpu.SemaphoreType.DMA,
        ],
        flops=6 * 10**9,
        moved=10 * 10**6,
        collective=2,
    )(sequence, pack, buckets[None], tok, cot, route)

    load = 2 * EXP * CAP
    hidden = w_in.shape[2]
    step = 256
    by_column = pl.BlockSpec((load, step), lambda f: (0, f))
    in_vmem = pl.BlockSpec(memory_space=pltpu.VMEM)
    anywhere = pl.BlockSpec(memory_space=pl.ANY)
    cube = (SIDE, SIDE, SIDE, SLOT)
    bigs = pltpu.VMEM((*cube, 3 * BIG), BF16)
    smalls = pltpu.VMEM((*cube, 3 * SMALL), BF16)
    turned, d_rows, act, d_pre, back_big, back_small = pl.pallas_call(
        expert_kernel,
        in_specs=[in_vmem, in_vmem, anywhere, anywhere],
        out_specs=[in_vmem] * 6,
        out_shape=[
            jax.ShapeDtypeStruct((D, load), BF16),
            jax.ShapeDtypeStruct((load, D), BF16),
            jax.ShapeDtypeStruct((hidden, load), BF16),
            jax.ShapeDtypeStruct((load, hidden), BF16),
            jax.ShapeDtypeStruct((*cube, 3 * BIG), BF16),
            jax.ShapeDtypeStruct((*cube, 3 * SMALL), BF16),
        ],
        scratch_shapes=[bigs, bigs, smalls, smalls, bigs, bigs, smalls, smalls, bigs, smalls, bigs, smalls, bigs, smalls]
        + [
            pltpu.VMEM((load, D), BF16),
            pltpu.VMEM((load, hidden), BF16),
            pltpu.VMEM((load, hidden), F32),
            pltpu.VMEM((D, hidden), BF16),
            pltpu.VMEM((hidden, D), BF16),
            pltpu.VMEM((hidden, D), BF16),
            pltpu.VMEM((D, hidden), BF16),
            pltpu.VMEM((3, SLOTS, BIG), BF16),
            pltpu.VMEM((3, SLOTS, SMALL), BF16),
            pltpu.VMEM((3, SLOTS, BIG), BF16),
            pltpu.VMEM((3, SLOTS, SMALL), BF16),
            pltpu.SemaphoreType.DMA((2,)),
            pltpu.SemaphoreType.DMA((4, 3)),
            pltpu.SemaphoreType.DMA((4, 3)),
            pltpu.SemaphoreType.DMA((4, 3, 3)),
            pltpu.SemaphoreType.DMA((4, 3, 3, SIDE - 1)),
            pltpu.SemaphoreType.DMA((4, 3, 3, SIDE - 1)),
        ],
        compiler_params=pltpu.CompilerParams(vmem_limit_bytes=VMEM_LIMIT, collective_id=4, has_side_effects=True),
        cost_estimate=pl.CostEstimate(flops=8 * load * D * hidden, bytes_accessed=20 * 10**6, transcendentals=load * hidden),
    )(big.reshape(*cube, 3 * BIG), small.reshape(*cube, 3 * SMALL), w_in, w_out)

    grad_w_in, grad_w_out = pl.pallas_call(
        expert_grad_kernel,
        grid=(hidden // step,),
        in_specs=[
            pl.BlockSpec((D, load), lambda f: (0, 0)),
            pl.BlockSpec((load, D), lambda f: (0, 0)),
            pl.BlockSpec((step, load), lambda f: (f, 0)),
            by_column,
        ],
        out_specs=[
            pl.BlockSpec((1, D, step), lambda f: (0, 0, f)),
            pl.BlockSpec((1, step, D), lambda f: (0, f, 0)),
        ],
        out_shape=[
            jax.ShapeDtypeStruct((1, D, hidden), F32),
            jax.ShapeDtypeStruct((1, hidden, D), F32),
        ],
        compiler_params=pltpu.CompilerParams(vmem_limit_bytes=VMEM_LIMIT),
        cost_estimate=pl.CostEstimate(flops=4 * load * D * hidden, bytes_accessed=20 * 10**6, transcendentals=0),
    )(turned, d_rows, act, d_pre)

    mixed, d_resid, g_pack, d_norm = whole(
        back_kernel,
        [
            ((1, count, D), BF16),
            ((count, D), F32),
            ((owners * QROW, PW), BF16),
            ((2, count, D), F32),
        ],
        scratch=[
            pltpu.VMEM((2, count, D), BF16),
            pltpu.VMEM((seq, QW), BF16),
            pltpu.VMEM((16, seq), F32),
            pltpu.SemaphoreType.DMA,
            pltpu.SemaphoreType.DMA,
        ],
        flops=8 * 10**9,
        moved=12 * 10**6,
        collective=3,
    )(back_big.reshape(SLOTS, 3 * BIG), back_small.reshape(SLOTS, 3 * SMALL), places, gates, resid, cot, gains, full, normed_ffn, route, output_mine, attended, qkv_all, lse, bias, normed_attn, sequence, buckets[None])

    widths = [width for _, width, _ in PARTS]
    total, theirs, d_tokens = whole(
        reduce_kernel,
        [((QROW, PW), F32)] * 2 + [((1, count, D), F32)],
        scratch=[pltpu.VMEM((SIDE - 1, SIDE, SIDE, QROW, width), BF16) for width in widths]
        + [pltpu.VMEM((SIDE, SIDE, QROW, width), BF16) for width in widths]
        + [pltpu.VMEM((SIDE - 1, SIDE, QROW, width), BF16) for width in widths]
        + [pltpu.VMEM((SIDE, QROW, width), BF16) for width in widths]
        + [pltpu.VMEM((SIDE - 1, QROW, width), BF16) for width in widths]
        + [pltpu.VMEM((count, D), F32)]
        + [pltpu.SemaphoreType.DMA((2,))] * 2
        + [pltpu.SemaphoreType.DMA((3, 3, SIDE - 1))] * 2,
        flops=10**7,
        moved=6 * 10**6,
        collective=1,
    )(g_pack.reshape(SIDE, SIDE, SIDE, QROW, PW), d_norm, d_resid, tok, gains)
    g_query, g_key, g_value, g_output, rest, d_tokens, mixed = whole(
        end_kernel,
        [((6, D), F32)] * 4 + [((6, 128), F32), ((1, count, D), F32), ((1, count, D), BF16)],
        flops=10**5,
        moved=2 * 10**6,
    )(total, theirs, d_tokens, mixed)
    extra = rest[:, 64:70]
    return (
        mixed,
        d_tokens,
        g_query,
        g_key,
        g_value,
        g_output,
        extra[:, 0] + extra[:, 1],
        extra[:, 2] + extra[:, 3],
        rest[:, :EXP],
        (extra[:, 4] + extra[:, 5])[:3],
        grad_w_in,
        grad_w_out,
    )


def solution(mesh):
    wide = P(("sp", "ep"), None)
    flat = P(("sp", "ep"))
    rows = P("ep", "sp", None)
    return jax.shard_map(
        shards,
        mesh=mesh,
        in_specs=(rows, rows, wide, wide, wide, wide, flat, flat, wide, flat, P("ep", None, "sp"), rows, rows, P()),
        out_specs=(rows, rows, wide, wide, wide, wide, flat, flat, wide, flat, P("ep", None, "sp"), rows),
        check_vma=False,
    )
```

```python
from types import SimpleNamespace

import jax
import jax.numpy as jnp
from jax import lax
from jax.experimental import pallas as pl
from jax.experimental.pallas import tpu as pltpu
from jax.sharding import PartitionSpec as P

D = 768
H = 12
HD = 64
HH = H // 2
HW = HH * HD
EXP = 64
EPS = 1e-06
CAP = 6
SLOT = 8
SLOTS = EXP * SLOT
BIG = 256
SMALL = 128
QROW = 16
QW = 3 * HW
PW = QW + 128
SIDE = 4
STRIDES = (16, 4, 1)
PARTS = ((0, 512, (2, 1, 0)), (512, 384, (0, 2, 1)), (896, 384, (1, 0, 2)))
MESH = pl.DeviceIdType.MESH
ROUTER = QW
GAIN = QW + 64
F32 = jnp.float32
BF16 = jnp.bfloat16
VMEM_LIMIT = 59 * 1024 * 1024


def iota(shape, axis):
    return lax.broadcasted_iota(jnp.int32, shape, axis)


def nn(left, right):
    return lax.dot_general(left, right, (((1,), (0,)), ((), ())), preferred_element_type=F32)


def nt(left, right):
    return lax.dot_general(left, right, (((1,), (1,)), ((), ())), preferred_element_type=F32)


def tn(left, right):
    return lax.dot_general(left, right, (((0,), (0,)), ((), ())), preferred_element_type=F32)


def chunk_entry(rows):
    owner = jnp.right_shift(rows, 4)
    inner = jnp.bitwise_and(rows, 15)
    half = (inner >= 6).astype(jnp.int32)
    inside = inner - 6 * half
    entry = half * (32 * H // 2) + owner * 3 + inside
    return jnp.where((inner < 12) & (inside < 3), entry, -1)


def hot(condition):
    return jnp.where(condition, 1.0, 0.0).astype(BF16)


PLANE = SIDE * SIDE
WIDE = 2 * 6 * PLANE
THICK = PLANE * QROW


def chunk_hot(turned, place):
    axis = 1 if turned else 0
    row = iota((1, WIDE) if turned else (WIDE, 1), axis)
    rows = iota((THICK, WIDE) if turned else (WIDE, THICK), 1 - axis)
    half = (row >= WIDE // 2).astype(jnp.int32)
    row = row - half * (WIDE // 2)
    owner = jnp.right_shift(row * 10923, 16)
    inner = row - owner * 6
    return hot(rows == place(half, owner * QROW, inner))


def projection_row(half, start, inner):
    return start + 6 * half + inner


def output_row(third):
    def place(half, start, inner):
        later = (inner >= 3).astype(jnp.int32)
        return jnp.where(inner - 3 * later == third, start + 12 + 2 * later + half, -1)

    return place


def rms_of(values):
    return lax.rsqrt(jnp.mean(values * values, axis=-1, keepdims=True) + EPS)


def unpack_chunks(v):
    pick = chunk_hot(False, projection_row)
    picks = [chunk_hot(False, output_row(third)) for third in range(3)]
    rows = WIDE // 2
    for x in range(SIDE):
        held = v.pack[x].reshape(THICK, PW)
        own = nn(pick, held).astype(BF16)
        v.full[x * rows : (x + 1) * rows, :] = own[:rows]
        v.full[D // 2 + x * rows : D // 2 + (x + 1) * rows, :] = own[rows:]
        out = sum(nn(picks[third], held[:, third * HW : (third + 1) * HW]) for third in range(3)).astype(BF16)
        v.output[x * rows : (x + 1) * rows, :HW] = out[:rows]
        v.output[x * rows : (x + 1) * rows, HW:] = out[rows:]
    v.gains[...] = v.full[:, QW:].astype(F32).T


def distance_bias(v, bucket_ref, seq):
    entry = chunk_entry(iota((EXP * QROW, 1), 0))
    bucket_of = jnp.right_shift(entry * 5462, 16)
    head_of = entry - bucket_of * H
    column = iota((EXP * QROW, 128), 1)
    tail = v.pack[:, :, :, :, QW:].reshape(EXP * QROW, 128)
    here_now = (entry >= 0) & (head_of == lax.axis_index("sp") * HH + column) & (column < HH)
    table = jnp.where(here_now, tail[:, 66:67].astype(F32), 0.0).astype(BF16)
    bucket_here = jnp.where(entry >= 0, bucket_of, -1)
    by_distance = tn(table, hot(bucket_here == bucket_ref[...]))[0:16, :].astype(BF16)
    turn = hot(jnp.bitwise_and(iota((seq, seq), 0) + iota((seq, seq), 1), seq - 1) == 0)
    v.bias[...] = nn(by_distance, turn)


def attend(v, seq):
    v.qkv[...] = nn(v.normed[...], v.full[:, :QW]).astype(BF16)
    causal = iota((seq, seq), 1) <= iota((seq, seq), 0)
    for head in range(HH):
        at = head * HD
        query = v.qkv[:, at : at + HD]
        key = v.qkv[:, HW + at : HW + at + HD]
        value = v.qkv[:, 2 * HW + at : 2 * HW + at + HD]
        bias = pltpu.roll(jnp.broadcast_to(v.bias[head : head + 1, :], (seq, seq)), 0, 1, stride=1, stride_axis=0)
        scores = jnp.where(causal, nt(query, key) * (HD**-0.5) + bias, -jnp.inf)
        peak = jnp.max(scores, axis=-1, keepdims=True)
        grown = jnp.exp(scores - peak)
        probs = grown / jnp.sum(grown, axis=-1, keepdims=True)
        v.probs[head] = probs
        v.attended[:, at : at + HD] = nn(probs.astype(BF16), value).astype(BF16)


def named_experts(v, count):
    return [(v.table[:, 8 + k : 9 + k].astype(jnp.int32) == iota((count, EXP), 1)).astype(F32) for k in range(2)]


def place_rows(v, routes_ref, count):
    row = iota((128, count), 0)
    routes = jnp.where(row == 0, routes_ref[0:1, :], jnp.where(row == 1, routes_ref[1:2, :], 0)).astype(F32).T
    column = iota((count, 128), 1)
    table = jnp.where(column == 8, routes[:, 0:1], jnp.where(column == 9, routes[:, 1:2], -1.0))
    v.table[...] = table
    named = named_experts(v, count)
    before = hot(iota((count, count), 1) < iota((count, count), 0))
    earlier = nn(before, (named[0] + named[1]).astype(BF16))
    for k in range(2):
        rank = jnp.sum(earlier * named[k], axis=-1, keepdims=True)
        start = routes[:, k : k + 1] * SLOT
        upper = (rank >= 3).astype(F32)
        table = jnp.where(column == 4 * k, start + rank, table)
        for third in range(3):
            value = jnp.where(rank - 3 * upper == third, start + CAP + upper, -1.0)
            table = jnp.where(column == 4 * k + 1 + third, value, table)
    v.table[...] = table


def fill_waves(v, cot_ref, count):
    normed = (v.resid[...] * rms_of(v.resid[...]) * v.gains[65:66, :]).astype(BF16)
    v.ffn[...] = normed
    logits = nn(normed, v.full[:, ROUTER : ROUTER + EXP])
    chosen = [jnp.sum(logits * one, axis=-1, keepdims=True) for one in named_experts(v, count)]
    peak = jnp.maximum(chosen[0], chosen[1])
    grown = [jnp.exp(one - peak) for one in chosen]
    total = grown[0] + grown[1]
    gates = [one / total for one in grown]
    column = iota((count, 128), 1)
    v.gates[...] = jnp.where(column == 0, gates[0], jnp.where(column == 1, gates[1], 0.0))
    upstream = cot_ref[...].astype(F32)
    slots = iota((SLOTS, count), 0)
    turned = v.table[...].T.astype(jnp.int32)
    place = [hot(slots == turned[n : n + 1, :]) for n in range(8)]
    spread = [(gates[k] * upstream).astype(BF16) for k in range(2)]
    either = place[0] + place[4]
    for third in range(3):
        there = slice(third * BIG, (third + 1) * BIG)
        big = nn(either, normed[:, there])
        there_small = slice(third * SMALL, (third + 1) * SMALL)
        small = 0.0
        for k in range(2):
            tail = place[4 * k + 1 + third]
            big = big + nn(tail, spread[k][:, D - BIG :])
            small = small + nn(place[4 * k], spread[k][:, there_small]) + nn(tail, spread[k][:, 3 * SMALL : 4 * SMALL])
        v.big0[:, :, :, :, there] = big.astype(BF16).reshape(SIDE, SIDE, SIDE, SLOT, BIG)
        v.small0[:, :, :, :, there_small] = small.astype(BF16).reshape(SIDE, SIDE, SIDE, SLOT, SMALL)


GROUP = 32
LOAD = GROUP * CAP
HELD = GROUP * SLOT


def unpacking(turned):
    axis = 1 if turned else 0
    row = iota((1, LOAD) if turned else (LOAD, 1), axis)
    slots = iota((HELD, LOAD) if turned else (LOAD, HELD), 1 - axis)
    owner = jnp.right_shift(row * 10923, 16)
    inner = row - owner * CAP
    upper = (inner >= 3).astype(jnp.int32)
    tails = [hot(slots == jnp.where(inner - 3 * upper == third, owner * SLOT + CAP + upper, -1)) for third in range(3)]
    return hot(slots == owner * SLOT + inner), tails


def expert_grad_kernel(turned_ref, drows_ref, act_ref, dpre_ref, gin_ref, gout_ref):
    gin_ref[0] = nn(turned_ref[...], dpre_ref[...])
    gout_ref[0] = nn(act_ref[...], drows_ref[...])


def split_two(values):
    high = values.astype(BF16)
    return high, (values - high.astype(F32)).astype(BF16)


def combine(v, cot_ref, mixed_ref, count):
    resid = v.resid[...]
    upstream = cot_ref[...].astype(F32)
    gates = [v.gates[:, k : k + 1] for k in range(2)]
    table = v.table[...].astype(jnp.int32)
    slots = iota((count, SLOTS), 1)
    place = [hot(slots == table[:, n : n + 1]) for n in range(8)]
    big = v.big_back[...].reshape(SLOTS, 3 * BIG)
    small = v.small_back[...].reshape(SLOTS, 3 * SMALL)
    outs = []
    for k in range(2):
        last, most = 0.0, 0.0
        for third in range(3):
            tail = place[4 * k + 1 + third]
            last = last + nn(tail, small[:, third * SMALL : (third + 1) * SMALL])
            most = most + nn(tail, big[:, third * BIG : (third + 1) * BIG])
        outs.append(jnp.concatenate([nn(place[4 * k], small), last, most], axis=1))
    mixed_ref[0] = (resid + (gates[0] * outs[0] + gates[1] * outs[1])).astype(BF16)
    d_gates = [jnp.sum(one * upstream, axis=-1, keepdims=True) for one in outs]
    inner = gates[0] * d_gates[0] + gates[1] * d_gates[1]
    named = named_experts(v, count)
    d_logits = sum(named[k] * (gates[k] * (d_gates[k] - inner)) for k in range(2)).astype(BF16)
    d_normed = nn(place[0] + place[4], big) + nt(d_logits, v.full[:, ROUTER : ROUTER + EXP])
    rms = rms_of(resid)
    u = d_normed * v.gains[65:66, :]
    v.dresid[...] = upstream + rms * u - resid * (rms * rms * rms) * jnp.mean(u * resid, axis=-1, keepdims=True)
    return d_logits, jnp.sum(d_normed * resid * rms, axis=0, keepdims=True)


def attend_back(v, seq):
    d_attended = nt(v.branch[...].reshape(seq, D), v.output[...]).astype(BF16)
    flip = hot(iota((seq, seq), 0) + iota((seq, seq), 1) == seq - 1)
    v.ddist[...] = jnp.zeros_like(v.ddist)
    for head in range(HH):
        at = head * HD
        query = v.qkv[:, at : at + HD]
        key = v.qkv[:, HW + at : HW + at + HD]
        value = v.qkv[:, 2 * HW + at : 2 * HW + at + HD]
        d_out = d_attended[:, at : at + HD]
        probs = v.probs[head]
        d_probs = nt(d_out, value)
        row_dot = jnp.sum(probs * d_probs, axis=-1, keepdims=True)
        d_scores = (probs * (d_probs - row_dot)).astype(BF16)
        v.dqkv[:, at : at + HD] = (nn(d_scores, key) * (HD**-0.5)).astype(BF16)
        v.dqkv[:, HW + at : HW + at + HD] = (tn(d_scores, query) * (HD**-0.5)).astype(BF16)
        v.dqkv[:, 2 * HW + at : 2 * HW + at + HD] = tn(probs.astype(BF16), d_out).astype(BF16)
        skewed = pltpu.roll(nn(d_scores, flip), 0, 1, stride=1, stride_axis=0)
        v.ddist[head : head + 1, :] = jnp.sum(skewed, axis=0, keepdims=True)


def table_gradient(v, bucket_ref):
    entry = chunk_entry(iota((EXP * QROW, 1), 0))
    bucket_of = jnp.right_shift(entry * 5462, 16)
    pick = hot(jnp.where(entry >= 0, bucket_of, -1) == bucket_ref[...])
    high, low = split_two(pltpu.roll(v.ddist[...], 1, 1))
    by_head = nt(pick, high) + nt(pick, low)
    column = iota(by_head.shape, 1)
    mine = (entry >= 0) & (entry - bucket_of * H == lax.axis_index("sp") * HH + column) & (column < HH)
    return jnp.sum(jnp.where(mine, by_head, 0.0), axis=-1, keepdims=True)


def here():
    owner = lax.axis_index("ep")
    return (owner // 16, owner // 4 % 4, owner % 4)


def across(axis, shift):
    owner, place = lax.axis_index("ep"), here()[axis]
    return {"ep": owner + ((place + shift) % SIDE - place) * STRIDES[axis]}


def other_core():
    return {"sp": 1 - lax.axis_index("sp")}


def greet():
    barrier = pltpu.get_barrier_semaphore()
    pl.semaphore_signal(barrier, inc=1, device_id=other_core(), device_id_type=MESH)
    for axis in range(3):
        for shift in range(1, SIDE):
            pl.semaphore_signal(barrier, inc=1, device_id=across(axis, shift), device_id_type=MESH)


def meet():
    pl.semaphore_wait(pltpu.get_barrier_semaphore(), 1 + 3 * (SIDE - 1))


def remote(source, target, send, receive, device):
    copy = pltpu.make_async_remote_copy(
        src_ref=source, dst_ref=target, send_sem=send, recv_sem=receive, device_id=device, device_id_type=MESH
    )
    copy.start()
    return copy


class Wave:
    ORDERS = ((2, 1, 0), (0, 2, 1), (1, 0, 2))

    def __init__(self, width, buffers, send, recv, local):
        self.width, self.buffers, self.send, self.recv, self.local = width, buffers, send, recv, local
        self.place, self.copies, self.kept = here(), {}, {}

    def block(self, ref, axis, value, third):
        index = tuple(value if other == axis else pl.ds(0, SIDE) for other in range(3))
        return ref.at[index + (slice(None), pl.ds(third * self.width, self.width))]

    def step(self, phase):
        for third, order in enumerate(self.ORDERS):
            if phase:
                self.settle(phase - 1, third)
            axis = order[phase]
            source, target = self.buffers[phase], self.buffers[phase + 1]
            spot = self.place[axis]
            for shift in (2, 1, 3):
                self.copies[phase, third, shift] = remote(
                    self.block(source, axis, (spot + shift) % SIDE, third),
                    self.block(target, axis, spot, third),
                    self.send.at[phase, third, shift - 1],
                    self.recv.at[phase, third, shift - 1],
                    across(axis, shift),
                )
            own = pltpu.make_async_copy(
                self.block(source, axis, spot, third), self.block(target, axis, spot, third), self.local.at[phase, third]
            )
            own.start()
            self.kept[phase, third] = own

    def settle(self, phase, third):
        for shift in range(1, SIDE):
            self.copies[phase, third, shift].wait_recv()
        self.kept[phase, third].wait()

    def land(self):
        for third in range(3):
            self.settle(2, third)

    def push(self, target, send, recv):
        source = self.buffers[3]
        pushes = []
        for third in range(3):
            self.settle(2, third)
            columns = (slice(None),) * 4 + (pl.ds(third * self.width, self.width),)
            pushes.append(remote(source.at[columns], target.at[columns], send.at[third], recv.at[third], other_core()))
        return pushes

    def sent(self):
        for copy in self.copies.values():
            copy.wait_send()


def experts(v):
    rows, act, bend, win, wout, win_turned, wout_turned = v.rows, v.act, v.bend, v.win, v.wout, v.win_turned, v.wout_turned
    drows_ref, dpre_ref = v.drows, v.dpre
    core_send, core_recv = v.push_send, v.push_recv

    def wave(n, width, buffers):
        return Wave(width, buffers, v.wave_send.at[n], v.wave_recv.at[n], v.wave_local.at[n])

    big = wave(0, BIG, (v.big0, v.big1, v.big2, v.big3))
    small = wave(1, SMALL, (v.small0, v.small1, v.small2, v.small3))
    back_small = wave(2, SMALL, (v.rsmall0, v.rsmall1, v.rsmall2, v.small_back))
    back_big = wave(3, BIG, (v.rbig0, v.rbig1, v.rbig2, v.big_back))
    for phase in range(3):
        big.step(phase)
        small.step(phase)
    pushes = big.push(v.big_theirs, core_send.at[0], core_recv.at[0])
    main, tails = unpacking(False)
    main_turned, tails_turned = unpacking(True)
    load = EXP * CAP
    hidden = win.shape[1]
    step = 512

    def groups(half, ref, width):
        packed = ref[...].reshape(SLOTS, 3 * width)
        for group in range(2):
            held = packed[group * HELD : (group + 1) * HELD]
            rest = 0.0
            for third in range(3):
                rest = rest + nn(tails[third], held[:, third * width : (third + 1) * width])
            first = half * load + group * LOAD
            yield slice(first, first + LOAD), nn(main, held).astype(BF16), rest.astype(BF16)

    def forward(half, source):
        there = slice(half * load, (half + 1) * load)
        for where, first, rest in groups(half, source, BIG):
            rows[where, :] = first
            drows_ref[where, D - BIG :] = rest
        normed = rows[there, :]
        for start in range(0, hidden, step):
            columns = slice(start, start + step)
            pre = nn(normed, win[:, columns])
            square = pre * pre
            slope = 0.7978845608028654
            upper = 0.5 + 0.5 * jnp.tanh(pre * (slope + (slope * 0.044715) * square))
            grown = pre * upper
            act[there, columns] = grown.astype(BF16)
            bend[there, columns] = upper + grown * (1.0 - upper) * (2 * slope + (6 * slope * 0.044715) * square)
        return nn(act[there, :], wout[...]).astype(BF16)

    def backward(half, source):
        there = slice(half * load, (half + 1) * load)
        for where, first, rest in groups(half, source, SMALL):
            drows_ref[where, : 3 * SMALL] = first
            drows_ref[where, 3 * SMALL : 4 * SMALL] = rest
        d_rows = drows_ref[there, :]
        for start in range(0, hidden, step):
            columns = slice(start, start + step)
            dpre_ref[there, columns] = (nn(d_rows, wout_turned[:, columns]) * bend[there, columns]).astype(BF16)
        return nn(dpre_ref[there, :], win_turned[...]).astype(BF16)

    def pack(values, last, width):
        for third in range(3):
            for group in range(2):
                there = slice(group * LOAD, (group + 1) * LOAD)
                own = nn(main_turned, values[there, third * width : (third + 1) * width])
                yield third, group, own + nn(tails_turned[third], last[there, :])

    def pack_small(out):
        return pack(out, out[:, 3 * SMALL : 4 * SMALL], SMALL)

    def pack_big(grad, out):
        return pack(grad, out[:, D - BIG :], BIG)

    def hand_over(packed, outgoing, incoming, n):
        copies = []
        for third, group, values in packed:
            outgoing[third, group * HELD : (group + 1) * HELD] = values.astype(BF16)
            if group:
                copies.append(
                    remote(outgoing.at[third], incoming.at[third], core_send.at[n, third], core_recv.at[n, third], other_core())
                )
        return copies

    def join(packed, incoming, copies, target, width):
        for third, group, values in packed:
            if group == 0:
                copies[third].wait_recv()
            total = (values + incoming[third, group * HELD : (group + 1) * HELD].astype(F32)).astype(BF16)
            target[2 * group : 2 * group + 2, :, :, :, third * width : (third + 1) * width] = total.reshape(
                SIDE // 2, SIDE, SIDE, SLOT, width
            )

    out = forward(0, v.big3)
    for push in pushes:
        push.wait_recv()
    pushes += small.push(v.small_theirs, core_send.at[1], core_recv.at[1])
    out_theirs = forward(1, v.big_theirs)
    small_copies = hand_over(pack_small(out_theirs), v.small_out, v.small_in, 2)
    grad = backward(0, v.small3)
    join(pack_small(out), v.small_in, small_copies, v.rsmall0, SMALL)
    back_small.step(0)
    for push in pushes[3:]:
        push.wait_recv()
    grad_theirs = backward(1, v.small_theirs)
    big_copies = hand_over(pack_big(grad_theirs, out_theirs), v.big_out, v.big_in, 3)
    back_small.step(1)
    join(pack_big(grad, out), v.big_in, big_copies, v.rbig0, BIG)
    back_big.step(0)
    back_small.step(2)
    win[:, :D] = rows[...].T
    back_big.step(1)
    wout[...] = act[...].T
    back_big.step(2)
    for copy in leaving(v):
        copy.start()
    back_small.land()
    back_big.land()
    for copy in pushes + small_copies + big_copies:
        copy.wait_send()
    for one in (big, small, back_small, back_big):
        one.sent()


def load_chunks(v, wq_ref, wk_ref, wv_ref, wo_ref, router_ref, attn_ref, ffn_ref, table_ref):
    v.stage[...] = jnp.zeros_like(v.stage)
    v.out16[...] = jnp.zeros_like(v.out16)
    v.out16[0:6, :] = wo_ref[...]

    def standing(ref):
        size = ref.shape[1]
        values = jnp.broadcast_to(ref[...].astype(F32), (QROW, size))
        kept = jnp.where(iota((QROW, size), 0) == iota((QROW, size), 1), values, 0.0)
        return jnp.sum(kept, axis=1, keepdims=True)

    column = iota((QROW, 64), 1)
    tail = jnp.where(column == 0, standing(attn_ref), 0.0)
    tail = jnp.where(column == 1, standing(ffn_ref), tail)
    tail = jnp.where(column == 2, standing(table_ref), tail).astype(BF16)
    for half in range(2):
        for n, ref in enumerate((wq_ref, wk_ref, wv_ref)):
            v.stage[half, 0:6, n * HW : (n + 1) * HW] = ref[:, half * HW : (half + 1) * HW]
        v.stage[half, 0:6, ROUTER : ROUTER + EXP] = router_ref[...]
        v.stage[half, :, GAIN:] = tail


def own_chunk(v, place):
    sp = lax.axis_index("sp")
    row, col = iota((QROW, QROW), 0), iota((QROW, QROW), 1)
    low = jnp.where((row == col) & (col < 6), 1.0, 0.0)
    high = jnp.where((row == col + 6) & (col < 6), 1.0, 0.0)
    own = jnp.where(sp == 0, low, high).astype(BF16)
    others = jnp.where(sp == 0, high, low).astype(BF16)
    later = (col >= 3).astype(jnp.int32)
    mine = nn(own, v.stage[sp]) + nn(others, v.chunk_got[...])
    v.pack[place[0], place[1], place[2], :, QW:] = mine[:, QW:].astype(BF16)
    for third in range(3):
        there = slice(third * HW, (third + 1) * HW)
        total = mine[:, there]
        for half in range(2):
            pick = hot((col < 6) & (col - 3 * later == third) & (row == 12 + 2 * later + half))
            total = total + nn(pick, v.out16[:, half * HW : (half + 1) * HW])
        v.pack[place[0], place[1], place[2], :, there] = total.astype(BF16)


class Gather:
    def __init__(self, v):
        self.v, self.place, self.copies = v, here(), {}

    def step(self, phase):
        for part, (first, width, order) in enumerate(PARTS):
            index = [pl.ds(0, SIDE) if axis in order[:phase] else self.place[axis] for axis in range(3)]
            block = self.v.pack.at[index[0], index[1], index[2], :, pl.ds(first, width)]
            if phase:
                self.settle(phase - 1, part)
            for shift in (2, 1, 3):
                self.copies[phase, part, shift] = remote(
                    block,
                    block,
                    self.v.gather_send.at[phase, part, shift - 1],
                    self.v.gather_recv.at[phase, part, shift - 1],
                    across(order[phase], shift),
                )

    def settle(self, phase, part):
        for shift in range(1, SIDE):
            self.copies[phase, part, shift].wait_recv()

    def land(self):
        for part in range(3):
            self.settle(2, part)
        for copy in self.copies.values():
            copy.wait_send()


class Reduce:
    def __init__(self, v):
        self.v, self.place, self.copies = v, here(), {}

    def push(self, phase, part, source, target):
        axis = PARTS[part][2][2 - phase]
        for shift in (2, 1, 3):
            self.copies[phase, part, shift] = remote(
                source((self.place[axis] + shift) % SIDE),
                target.at[shift - 1],
                self.v.reduce_send.at[phase, part, shift - 1],
                self.v.reduce_recv.at[phase, part, shift - 1],
                across(axis, shift),
            )

    def added(self, phase, part, own, arrived):
        values = own.astype(F32)
        for shift in range(1, SIDE):
            self.copies[phase, part, shift].wait_recv()
            values = values + arrived[shift - 1].astype(F32)
        return values

    def at(self, axes, axis, value):
        return tuple(value if one == axis else pl.ds(0, SIDE) for one in axes)

    def first(self, part):
        start, width, order = PARTS[part]

        def block(value):
            return self.v.pack.at[self.at((0, 1, 2), order[2], value) + (slice(None), pl.ds(start, width))]

        self.push(0, part, block, self.v.firsts[part])

    def second(self, part):
        start, width, order = PARTS[part]
        own = self.v.pack[self.at((0, 1, 2), order[2], self.place[order[2]]) + (slice(None), pl.ds(start, width))]
        sums = self.v.sums[part]
        sums[...] = self.added(0, part, own, self.v.firsts[part]).astype(BF16)
        self.push(1, part, lambda value: sums.at[self.at(sorted(order[:2]), order[1], value)], self.v.seconds[part])

    def third(self, part):
        order = PARTS[part][2]
        own = self.v.sums[part][self.at(sorted(order[:2]), order[1], self.place[order[1]])]
        pairs = self.v.pairs[part]
        pairs[...] = self.added(1, part, own, self.v.seconds[part]).astype(BF16)
        self.push(2, part, lambda value: pairs.at[value], self.v.thirds[part])

    def total(self, part):
        return self.added(2, part, self.v.pairs[part][self.place[PARTS[part][2][0]]], self.v.thirds[part])


def layer_kernel(names, *refs):
    v = SimpleNamespace(**dict(zip(names, refs, strict=True)))
    for group in ("firsts", "sums", "seconds", "pairs", "thirds"):
        setattr(v, group, [getattr(v, group + str(part)) for part in range(3)])
    greet()
    loads = [pltpu.make_async_copy(v.win_hbm.at[0], v.win, v.load_sem.at[0]), pltpu.make_async_copy(v.wout_hbm.at[0], v.wout, v.load_sem.at[1])]
    for load in loads:
        load.start()
    sp = lax.axis_index("sp")
    place = here()
    count = v.tok.shape[0]
    seq = 2 * count

    def to_core(source, target, n):
        return remote(source, target, v.core_send.at[n], v.core_recv.at[n], other_core())

    load_chunks(v, v.wq, v.wk, v.wv, v.wo, v.router, v.gain_attn, v.gain_ffn, v.bias_table)
    v.seq[sp] = v.tok[...]
    meet()
    chunk_copy = to_core(v.stage.at[1 - sp], v.chunk_got, 0)
    tok_copy = to_core(v.tok, v.seq.at[sp], 1)
    chunk_copy.wait()
    own_chunk(v, place)
    gather = Gather(v)
    gather.step(0)
    place_rows(v, v.routes, count)
    gather.step(1)
    tok_copy.wait()
    inputs = v.seq[...].reshape(seq, D).astype(F32)
    rms = rms_of(inputs)
    gather.step(2)
    for load in loads:
        load.wait()
    v.win_turned[...] = v.win[...].T
    v.wout_turned[...] = v.wout[...].T
    gather.land()
    unpack_chunks(v)
    v.normed[...] = (inputs * rms * v.gains[64:65, :]).astype(BF16)
    distance_bias(v, v.buckets, seq)
    attend(v, seq)
    v.halves[...] = nn(v.attended[...], v.output[...]).reshape(v.halves.shape)
    half_copy = to_core(v.halves.at[1 - sp], v.half_got, 2)
    half_copy.wait()
    v.resid[...] = v.tok[...].astype(F32) + v.halves[sp] + v.half_got[...]
    fill_waves(v, v.cot, count)
    experts(v)
    d_logits, g_ffn = combine(v, v.cot, v.mixed, count)
    v.branch[sp] = v.dresid[...].astype(BF16)
    branch_copy = to_core(v.branch.at[sp], v.branch.at[sp], 3)
    g_router = tn(d_logits, v.ffn[...])
    to_chunk = chunk_hot(True, projection_row)
    to_output = [chunk_hot(True, output_row(third)) for third in range(3)]
    branch_copy.wait()
    attend_back(v, seq)
    d_branch = v.branch[...].reshape(seq, D)
    g_output = tn(v.attended[...], d_branch).astype(BF16)
    reduce = Reduce(v)
    rows = WIDE // 2

    def split(values, x, second):
        return jnp.concatenate([values[x * rows : (x + 1) * rows], second[x * rows : (x + 1) * rows]], axis=0)

    for third in range(3):
        there = slice(third * HW, (third + 1) * HW)
        gradient = tn(v.normed[...], v.dqkv[:, there]).astype(BF16)
        for x in range(SIDE):
            total = nn(to_chunk, split(gradient[: D // 2], x, gradient[D // 2 :]))
            total = total + nn(to_output[third], split(g_output[:, :HW], x, g_output[:, HW:]))
            v.pack[x, :, :, :, there] = total.astype(BF16).reshape(SIDE, SIDE, QROW, HW)
        if third:
            reduce.first(third - 1)
    d_normed = nt(v.dqkv[...], v.full[:, :QW])
    v.halves[...] = d_normed.reshape(v.halves.shape)
    norm_copy = to_core(v.halves.at[1 - sp], v.norm_got, 4)
    inputs = v.seq[...].reshape(seq, D).astype(F32)
    g_attn = jnp.sum(d_normed * inputs * rms_of(inputs), axis=0, keepdims=True)
    row = iota((64, D), 0)
    tail = jnp.zeros((64, D), F32)
    for n, values in enumerate((*split_two(g_attn), *split_two(g_ffn))):
        tail = jnp.where(row == n, values.astype(F32), tail)
    tail = jnp.concatenate([g_router, tail], axis=0).T.astype(BF16)
    high, low = split_two(table_gradient(v, v.buckets))
    column = iota((THICK, 128), 1)
    for x in range(SIDE):
        there = slice(x * THICK, (x + 1) * THICK)
        total = nn(to_chunk, split(tail[: D // 2], x, tail[D // 2 :]))
        total = jnp.where(column == 68, high[there].astype(F32), jnp.where(column == 69, low[there].astype(F32), total))
        v.pack[x, :, :, :, QW:] = total.astype(BF16).reshape(SIDE, SIDE, QROW, 128)
    reduce.first(2)
    norm_copy.wait()
    inputs = v.tok[...].astype(F32)
    d_normed = v.halves[sp] + v.norm_got[...]
    rms = rms_of(inputs)
    u = d_normed * v.gains[64:65, :]
    drop = inputs * (rms * rms * rms) * jnp.mean(u * inputs, axis=-1, keepdims=True)
    v.dtok[0] = v.dresid[...] + rms * u - drop
    for part in range(3):
        reduce.second(part)
    for part in range(3):
        reduce.third(part)
    for part, (first, width, _) in enumerate(PARTS):
        v.total[:, first : first + width] = reduce.total(part)
    total_copy = to_core(v.total, v.theirs, 5)
    for copy in reduce.copies.values():
        copy.wait_send()
    total_copy.wait()
    for copy in leaving(v):
        copy.wait()


def leaving(v):
    pairs = ((v.win.at[:, pl.ds(0, D)], v.turned_hbm), (v.drows, v.drows_hbm), (v.wout, v.act_hbm), (v.dpre, v.dpre_hbm))
    return [pltpu.make_async_copy(source, target, v.leave_sem.at[n]) for n, (source, target) in enumerate(pairs)]


def end_kernel(total, theirs, dtok_ref, mixed_ref, q_ref, k_ref, v_ref, o_ref, router_ref, attn_ref, ffn_ref, table_ref, dtok_out, mixed_out):
    sp = lax.axis_index("sp")
    dtok_out[...] = dtok_ref[...]
    mixed_out[...] = mixed_ref[...]
    for row in range(6):
        for half in range(2):
            there = 12 + row // 3 * 2 + half
            third = row % 3 * HW
            o_ref[row : row + 1, half * HW : (half + 1) * HW] = total[there : there + 1, third : third + HW]
    mine = jnp.where(sp == 0, total[0:6, :], total[6:12, :])
    other = jnp.where(sp == 0, theirs[0:6, :], theirs[6:12, :])
    for n, ref in enumerate((q_ref, k_ref, v_ref)):
        there = slice(n * HW, (n + 1) * HW)
        ref[:, :HW] = jnp.where(sp == 0, mine[:, there], other[:, there])
        ref[:, HW:] = jnp.where(sp == 0, other[:, there], mine[:, there])
    router_ref[...] = mine[:, ROUTER : ROUTER + EXP] + other[:, ROUTER : ROUTER + EXP]
    extra = mine[:, GAIN:] + other[:, GAIN:]
    diagonal = iota((6, 6), 0) == iota((6, 6), 1)
    for n, ref in enumerate((attn_ref, ffn_ref, table_ref)):
        column = extra[:, 2 * n : 2 * n + 1] + extra[:, 2 * n + 1 : 2 * n + 2]
        ref[...] = jnp.sum(jnp.where(diagonal, column, 0.0), axis=0, keepdims=True)[:, : ref.shape[1]]


def layer_buffers(count, hidden, load):
    seq = 2 * count
    cube = (SIDE, SIDE, SIDE)
    bigs, smalls = (*cube, SLOT, 3 * BIG), (*cube, SLOT, 3 * SMALL)
    buffers = {
        "stage": ((2, QROW, PW), BF16),
        "chunk_got": ((QROW, PW), BF16),
        "out16": ((QROW, D), BF16),
        "pack": ((*cube, QROW, PW), BF16),
        "seq": ((2, count, D), BF16),
        "full": ((D, PW), BF16),
        "output": ((HW, D), BF16),
        "gains": ((128, D), F32),
        "normed": ((seq, D), BF16),
        "bias": ((16, seq), F32),
        "qkv": ((seq, QW), BF16),
        "probs": ((HH, seq, seq), F32),
        "attended": ((seq, HW), BF16),
        "halves": ((2, count, D), F32),
        "half_got": ((count, D), F32),
        "norm_got": ((count, D), F32),
        "resid": ((count, D), F32),
        "dresid": ((count, D), F32),
        "ffn": ((count, D), BF16),
        "table": ((count, 128), F32),
        "gates": ((count, 128), F32),
        "branch": ((2, count, D), BF16),
        "dqkv": ((seq, QW), BF16),
        "ddist": ((16, seq), F32),
        "rows": ((load, D), BF16),
        "drows": ((load, D), BF16),
        "act": ((load, hidden), BF16),
        "dpre": ((load, hidden), BF16),
        "bend": ((load, hidden), F32),
        "win": ((D, hidden), BF16),
        "wout": ((hidden, D), BF16),
        "win_turned": ((hidden, D), BF16),
        "wout_turned": ((D, hidden), BF16),
        "big_out": ((3, SLOTS, BIG), BF16),
        "big_in": ((3, SLOTS, BIG), BF16),
        "small_out": ((3, SLOTS, SMALL), BF16),
        "small_in": ((3, SLOTS, SMALL), BF16),
    }
    for name in ("big0", "big1", "big2", "big3", "big_theirs", "rbig0", "rbig1", "rbig2", "big_back"):
        buffers[name] = (bigs, BF16)
    for name in ("small0", "small1", "small2", "small3", "small_theirs", "rsmall0", "rsmall1", "rsmall2", "small_back"):
        buffers[name] = (smalls, BF16)
    for part, (_, width, _) in enumerate(PARTS):
        buffers[f"firsts{part}"] = ((SIDE - 1, SIDE, SIDE, QROW, width), BF16)
        buffers[f"sums{part}"] = ((SIDE, SIDE, QROW, width), BF16)
        buffers[f"seconds{part}"] = ((SIDE - 1, SIDE, QROW, width), BF16)
        buffers[f"pairs{part}"] = ((SIDE, QROW, width), BF16)
        buffers[f"thirds{part}"] = ((SIDE - 1, QROW, width), BF16)
    semaphores = {
        "load_sem": (2,),
        "leave_sem": (4,),
        "core_send": (6,),
        "core_recv": (6,),
        "gather_send": (3, 3, SIDE - 1),
        "gather_recv": (3, 3, SIDE - 1),
        "reduce_send": (3, 3, SIDE - 1),
        "reduce_recv": (3, 3, SIDE - 1),
        "push_send": (4, 3),
        "push_recv": (4, 3),
        "wave_send": (4, 3, 3, SIDE - 1),
        "wave_recv": (4, 3, 3, SIDE - 1),
        "wave_local": (4, 3, 3),
    }
    scratch = {name: pltpu.VMEM(*one) for name, one in buffers.items()}
    return scratch | {name: pltpu.SemaphoreType.DMA(one) for name, one in semaphores.items()}


def shards(tokens, cotangent, w_query, w_key, w_value, w_output, gain_attn, gain_ffn, router, bias_table, w_in, w_out, routes, buckets):
    count = tokens.shape[1]
    load = 2 * EXP * CAP
    hidden = w_in.shape[2]
    in_vmem = pl.BlockSpec(memory_space=pltpu.VMEM)
    anywhere = pl.BlockSpec(memory_space=pl.ANY)
    given = {
        "wq": w_query,
        "wk": w_key,
        "wv": w_value,
        "wo": w_output,
        "router": router,
        "gain_attn": gain_attn[None],
        "gain_ffn": gain_ffn[None],
        "bias_table": bias_table[None],
        "tok": tokens[0],
        "cot": cotangent[0],
        "routes": routes[0].T,
        "buckets": buckets[None],
        "win_hbm": w_in,
        "wout_hbm": w_out,
    }
    made = {
        "turned_hbm": ((D, load), BF16),
        "drows_hbm": ((load, D), BF16),
        "act_hbm": ((hidden, load), BF16),
        "dpre_hbm": ((load, hidden), BF16),
        "total": ((QROW, PW), F32),
        "theirs": ((QROW, PW), F32),
        "dtok": ((1, count, D), F32),
        "mixed": ((1, count, D), BF16),
    }
    scratch = layer_buffers(count, hidden, load)
    names = [*given, *made, *scratch]
    turned, d_rows, act, d_pre, total, theirs, d_tokens, mixed = pl.pallas_call(
        lambda *refs: layer_kernel(names, *refs),
        in_specs=[anywhere if name.endswith("_hbm") else in_vmem for name in given],
        out_specs=[anywhere if name.endswith("_hbm") else in_vmem for name in made],
        out_shape=[jax.ShapeDtypeStruct(*one) for one in made.values()],
        scratch_shapes=list(scratch.values()),
        compiler_params=pltpu.CompilerParams(vmem_limit_bytes=VMEM_LIMIT, collective_id=0, has_side_effects=True),
        cost_estimate=pl.CostEstimate(flops=20 * 10**9, bytes_accessed=20 * 10**6, transcendentals=load * hidden),
    )(*given.values())

    step = 256
    grad_w_in, grad_w_out = pl.pallas_call(
        expert_grad_kernel,
        grid=(hidden // step,),
        in_specs=[
            pl.BlockSpec((D, load), lambda f: (0, 0)),
            pl.BlockSpec((load, D), lambda f: (0, 0)),
            pl.BlockSpec((step, load), lambda f: (f, 0)),
            pl.BlockSpec((load, step), lambda f: (0, f)),
        ],
        out_specs=[
            pl.BlockSpec((1, D, step), lambda f: (0, 0, f)),
            pl.BlockSpec((1, step, D), lambda f: (0, f, 0)),
        ],
        out_shape=[
            jax.ShapeDtypeStruct((1, D, hidden), F32),
            jax.ShapeDtypeStruct((1, hidden, D), F32),
        ],
        compiler_params=pltpu.CompilerParams(vmem_limit_bytes=VMEM_LIMIT),
        cost_estimate=pl.CostEstimate(flops=4 * load * D * hidden, bytes_accessed=20 * 10**6, transcendentals=0),
    )(turned, d_rows, act, d_pre)

    g_query, g_key, g_value, g_output, g_router, g_attn, g_ffn, g_table, d_tokens, mixed = pl.pallas_call(
        end_kernel,
        out_shape=[jax.ShapeDtypeStruct((6, D), F32)] * 4
        + [jax.ShapeDtypeStruct(shape, F32) for shape in ((6, EXP), (1, 6), (1, 6), (1, 3), (1, count, D))]
        + [jax.ShapeDtypeStruct((1, count, D), BF16)],
        compiler_params=pltpu.CompilerParams(vmem_limit_bytes=VMEM_LIMIT),
        cost_estimate=pl.CostEstimate(flops=10**5, bytes_accessed=2 * 10**6, transcendentals=0),
    )(total, theirs, d_tokens, mixed)
    return (mixed, d_tokens, g_query, g_key, g_value, g_output, g_attn[0], g_ffn[0], g_router, g_table[0], grad_w_in, grad_w_out)


def solution(mesh):
    wide = P(("sp", "ep"), None)
    flat = P(("sp", "ep"))
    rows = P("ep", "sp", None)
    return jax.shard_map(
        shards,
        mesh=mesh,
        in_specs=(rows, rows, wide, wide, wide, wide, flat, flat, wide, flat, P("ep", None, "sp"), rows, rows, P()),
        out_specs=(rows, rows, wide, wide, wide, wide, flat, flat, wide, flat, P("ep", None, "sp"), rows),
        check_vma=False,
    )
```

```python
from types import SimpleNamespace

import jax
import jax.numpy as jnp
from jax import lax
from jax.experimental import pallas as pl
from jax.experimental.pallas import tpu as pltpu
from jax.sharding import PartitionSpec as P

D = 768
H = 12
HD = 64
HH = H // 2
HW = HH * HD
EXP = 64
EPS = 1e-06
CAP = 6
SLOT = 8
SLOTS = EXP * SLOT
BIG = 256
SMALL = 128
QROW = 16
QW = 3 * HW
PW = QW + 128
SIDE = 4
STRIDES = (16, 4, 1)
PARTS = ((0, HW, (2, 1, 0)), (HW, HW, (0, 2, 1)), (2 * HW, HW, (1, 0, 2)), (QW, 128, (2, 1, 0)))
MESH = pl.DeviceIdType.MESH
ROUTER = QW
GAIN = QW + 64
F32 = jnp.float32
BF16 = jnp.bfloat16
VMEM_LIMIT = 59 * 1024 * 1024


def iota(shape, axis):
    return lax.broadcasted_iota(jnp.int32, shape, axis)


def nn(left, right):
    return lax.dot_general(left, right, (((1,), (0,)), ((), ())), preferred_element_type=F32)


def nt(left, right):
    return lax.dot_general(left, right, (((1,), (1,)), ((), ())), preferred_element_type=F32)


def tn(left, right):
    return lax.dot_general(left, right, (((0,), (0,)), ((), ())), preferred_element_type=F32)


def chunk_entry(rows):
    owner = jnp.right_shift(rows, 4)
    inner = jnp.bitwise_and(rows, 15)
    half = (inner >= 6).astype(jnp.int32)
    inside = inner - 6 * half
    entry = half * (32 * H // 2) + owner * 3 + inside
    return jnp.where((inner < 12) & (inside < 3), entry, -1)


def hot(condition):
    return jnp.where(condition, 1.0, 0.0).astype(BF16)


PLANE = SIDE * SIDE
WIDE = 2 * 6 * PLANE
THICK = PLANE * QROW


def chunk_hot(turned, place):
    axis = 1 if turned else 0
    row = iota((1, WIDE) if turned else (WIDE, 1), axis)
    rows = iota((THICK, WIDE) if turned else (WIDE, THICK), 1 - axis)
    half = (row >= WIDE // 2).astype(jnp.int32)
    row = row - half * (WIDE // 2)
    owner = jnp.right_shift(row * 10923, 16)
    inner = row - owner * 6
    return hot(rows == place(half, owner * QROW, inner))


def projection_row(half, start, inner):
    return start + 6 * half + inner


def output_row(third):
    def place(half, start, inner):
        later = (inner >= 3).astype(jnp.int32)
        return jnp.where(inner - 3 * later == third, start + 12 + 2 * later + half, -1)

    return place


def rms_of(values):
    return lax.rsqrt(jnp.mean(values * values, axis=-1, keepdims=True) + EPS)


def unpack_chunks(v):
    pick = chunk_hot(False, projection_row)
    picks = [chunk_hot(False, output_row(third)) for third in range(3)]
    rows = WIDE // 2
    for x in range(SIDE):
        held = v.pack[x, :, :, :, :QW].reshape(THICK, QW)
        own = nn(pick, held).astype(BF16)
        v.full[x * rows : (x + 1) * rows, :QW] = own[:rows]
        v.full[D // 2 + x * rows : D // 2 + (x + 1) * rows, :QW] = own[rows:]
        out = sum(nn(picks[third], held[:, third * HW : (third + 1) * HW]) for third in range(3)).astype(BF16)
        v.output[x * rows : (x + 1) * rows, :HW] = out[:rows]
        v.output[x * rows : (x + 1) * rows, HW:] = out[rows:]


def unpack_rest(v):
    pick = chunk_hot(False, projection_row)
    rows = WIDE // 2
    for x in range(SIDE):
        own = nn(pick, v.pack[x, :, :, :, QW:].reshape(THICK, 128)).astype(BF16)
        v.full[x * rows : (x + 1) * rows, QW:] = own[:rows]
        v.full[D // 2 + x * rows : D // 2 + (x + 1) * rows, QW:] = own[rows:]
    v.gains[...] = v.full[:, QW:].astype(F32).T


def distance_bias(v, bucket_ref, seq):
    entry = chunk_entry(iota((EXP * QROW, 1), 0))
    bucket_of = jnp.right_shift(entry * 5462, 16)
    head_of = entry - bucket_of * H
    column = iota((EXP * QROW, 128), 1)
    tail = v.pack[:, :, :, :, QW:].reshape(EXP * QROW, 128)
    here_now = (entry >= 0) & (head_of == lax.axis_index("sp") * HH + column) & (column < HH)
    table = jnp.where(here_now, tail[:, 66:67].astype(F32), 0.0).astype(BF16)
    bucket_here = jnp.where(entry >= 0, bucket_of, -1)
    by_distance = tn(table, hot(bucket_here == bucket_ref[...]))[0:16, :].astype(BF16)
    turn = hot(jnp.bitwise_and(iota((seq, seq), 0) + iota((seq, seq), 1), seq - 1) == 0)
    v.bias[...] = nn(by_distance, turn)


def attend(v, seq):
    v.qkv[...] = nn(v.normed[...], v.full[:, :QW]).astype(BF16)
    causal = iota((seq, seq), 1) <= iota((seq, seq), 0)
    for head in range(HH):
        at = head * HD
        query = v.qkv[:, at : at + HD]
        key = v.qkv[:, HW + at : HW + at + HD]
        value = v.qkv[:, 2 * HW + at : 2 * HW + at + HD]
        bias = pltpu.roll(jnp.broadcast_to(v.bias[head : head + 1, :], (seq, seq)), 0, 1, stride=1, stride_axis=0)
        scores = jnp.where(causal, nt(query, key) * (HD**-0.5) + bias, -jnp.inf)
        peak = jnp.max(scores, axis=-1, keepdims=True)
        grown = jnp.exp(scores - peak)
        probs = grown / jnp.sum(grown, axis=-1, keepdims=True)
        v.probs[head] = probs
        v.attended[:, at : at + HD] = nn(probs.astype(BF16), value).astype(BF16)


def named_experts(v, count):
    return [(v.table[:, 8 + k : 9 + k].astype(jnp.int32) == iota((count, EXP), 1)).astype(F32) for k in range(2)]


def place_rows(v, routes_ref, count):
    row = iota((128, count), 0)
    routes = jnp.where(row == 0, routes_ref[0:1, :], jnp.where(row == 1, routes_ref[1:2, :], 0)).astype(F32).T
    column = iota((count, 128), 1)
    table = jnp.where(column == 8, routes[:, 0:1], jnp.where(column == 9, routes[:, 1:2], -1.0))
    v.table[...] = table
    named = named_experts(v, count)
    before = hot(iota((count, count), 1) < iota((count, count), 0))
    earlier = nn(before, (named[0] + named[1]).astype(BF16))
    for k in range(2):
        rank = jnp.sum(earlier * named[k], axis=-1, keepdims=True)
        start = routes[:, k : k + 1] * SLOT
        upper = (rank >= 3).astype(F32)
        table = jnp.where(column == 4 * k, start + rank, table)
        for third in range(3):
            value = jnp.where(rank - 3 * upper == third, start + CAP + upper, -1.0)
            table = jnp.where(column == 4 * k + 1 + third, value, table)
    v.table[...] = table


def fill_waves(v, cot_ref, count, place):
    normed = (v.resid[...] * rms_of(v.resid[...]) * v.gains[65:66, :]).astype(BF16)
    v.ffn[...] = normed
    logits = nn(normed, v.full[:, ROUTER : ROUTER + EXP])
    chosen = [jnp.sum(logits * one, axis=-1, keepdims=True) for one in named_experts(v, count)]
    peak = jnp.maximum(chosen[0], chosen[1])
    grown = [jnp.exp(one - peak) for one in chosen]
    total = grown[0] + grown[1]
    gates = [one / total for one in grown]
    column = iota((count, 128), 1)
    v.gates[...] = jnp.where(column == 0, gates[0], jnp.where(column == 1, gates[1], 0.0))
    upstream = cot_ref[...].astype(F32)
    spread = [(gates[k] * upstream).astype(BF16) for k in range(2)]
    either = place[0] + place[4]
    for third in range(3):
        there = slice(third * BIG, (third + 1) * BIG)
        big = nn(either, normed[:, there])
        there_small = slice(third * SMALL, (third + 1) * SMALL)
        small = 0.0
        for k in range(2):
            tail = place[4 * k + 1 + third]
            big = big + nn(tail, spread[k][:, D - BIG :])
            small = small + nn(place[4 * k], spread[k][:, there_small]) + nn(tail, spread[k][:, 3 * SMALL : 4 * SMALL])
        v.big0[:, :, :, :, there] = big.astype(BF16).reshape(SIDE, SIDE, SIDE, SLOT, BIG)
        v.small0[:, :, :, :, there_small] = small.astype(BF16).reshape(SIDE, SIDE, SIDE, SLOT, SMALL)


GROUP = 32
LOAD = GROUP * CAP
HELD = GROUP * SLOT


def unpacking(turned):
    axis = 1 if turned else 0
    row = iota((1, LOAD) if turned else (LOAD, 1), axis)
    slots = iota((HELD, LOAD) if turned else (LOAD, HELD), 1 - axis)
    owner = jnp.right_shift(row * 10923, 16)
    inner = row - owner * CAP
    upper = (inner >= 3).astype(jnp.int32)
    tails = [hot(slots == jnp.where(inner - 3 * upper == third, owner * SLOT + CAP + upper, -1)) for third in range(3)]
    return hot(slots == owner * SLOT + inner), tails


def split_two(values):
    high = values.astype(BF16)
    return high, (values - high.astype(F32)).astype(BF16)


def combine(v, cot_ref, mixed_ref, count):
    resid = v.resid[...]
    upstream = cot_ref[...].astype(F32)
    gates = [v.gates[:, k : k + 1] for k in range(2)]
    table = v.table[...].astype(jnp.int32)
    slots = iota((count, SLOTS), 1)
    place = [hot(slots == table[:, n : n + 1]) for n in range(8)]
    big = v.big_back[...].reshape(SLOTS, 3 * BIG)
    small = v.small_back[...].reshape(SLOTS, 3 * SMALL)
    outs = []
    for k in range(2):
        last, most = 0.0, 0.0
        for third in range(3):
            tail = place[4 * k + 1 + third]
            last = last + nn(tail, small[:, third * SMALL : (third + 1) * SMALL])
            most = most + nn(tail, big[:, third * BIG : (third + 1) * BIG])
        outs.append(jnp.concatenate([nn(place[4 * k], small), last, most], axis=1))
    mixed_ref[0] = (resid + (gates[0] * outs[0] + gates[1] * outs[1])).astype(BF16)
    d_gates = [jnp.sum(one * upstream, axis=-1, keepdims=True) for one in outs]
    inner = gates[0] * d_gates[0] + gates[1] * d_gates[1]
    named = named_experts(v, count)
    d_logits = sum(named[k] * (gates[k] * (d_gates[k] - inner)) for k in range(2)).astype(BF16)
    d_normed = nn(place[0] + place[4], big) + nt(d_logits, v.full[:, ROUTER : ROUTER + EXP])
    rms = rms_of(resid)
    u = d_normed * v.gains[65:66, :]
    v.dresid[...] = upstream + rms * u - resid * (rms * rms * rms) * jnp.mean(u * resid, axis=-1, keepdims=True)
    return d_logits, jnp.sum(d_normed * resid * rms, axis=0, keepdims=True)


def attend_back(v, seq):
    d_attended = nt(v.branch[...].reshape(seq, D), v.output[...]).astype(BF16)
    flip = hot(iota((seq, seq), 0) + iota((seq, seq), 1) == seq - 1)
    v.ddist[...] = jnp.zeros_like(v.ddist)
    for head in range(HH):
        at = head * HD
        query = v.qkv[:, at : at + HD]
        key = v.qkv[:, HW + at : HW + at + HD]
        value = v.qkv[:, 2 * HW + at : 2 * HW + at + HD]
        d_out = d_attended[:, at : at + HD]
        probs = v.probs[head]
        d_probs = nt(d_out, value)
        row_dot = jnp.sum(probs * d_probs, axis=-1, keepdims=True)
        d_scores = (probs * (d_probs - row_dot)).astype(BF16)
        v.dqkv[:, at : at + HD] = (nn(d_scores, key) * (HD**-0.5)).astype(BF16)
        v.dqkv[:, HW + at : HW + at + HD] = (tn(d_scores, query) * (HD**-0.5)).astype(BF16)
        v.dqkv[:, 2 * HW + at : 2 * HW + at + HD] = nn(v.probs_turned[head], d_out).astype(BF16)
        skewed = pltpu.roll(nn(d_scores, flip), 0, 1, stride=1, stride_axis=0)
        v.ddist[head : head + 1, :] = jnp.sum(skewed, axis=0, keepdims=True)


def table_gradient(v, bucket_ref):
    entry = chunk_entry(iota((EXP * QROW, 1), 0))
    bucket_of = jnp.right_shift(entry * 5462, 16)
    pick = hot(jnp.where(entry >= 0, bucket_of, -1) == bucket_ref[...])
    high, low = split_two(pltpu.roll(v.ddist[...], 1, 1))
    by_head = nt(pick, high) + nt(pick, low)
    column = iota(by_head.shape, 1)
    mine = (entry >= 0) & (entry - bucket_of * H == lax.axis_index("sp") * HH + column) & (column < HH)
    return jnp.sum(jnp.where(mine, by_head, 0.0), axis=-1, keepdims=True)


def here():
    owner = lax.axis_index("ep")
    return (owner // 16, owner // 4 % 4, owner % 4)


def across(axis, shift):
    owner, place = lax.axis_index("ep"), here()[axis]
    return {"ep": owner + ((place + shift) % SIDE - place) * STRIDES[axis]}


def other_core():
    return {"sp": 1 - lax.axis_index("sp")}


def greet():
    barrier = pltpu.get_barrier_semaphore()
    pl.semaphore_signal(barrier, inc=1, device_id=other_core(), device_id_type=MESH)
    for axis in range(3):
        for shift in range(1, SIDE):
            pl.semaphore_signal(barrier, inc=1, device_id=across(axis, shift), device_id_type=MESH)


def meet():
    pl.semaphore_wait(pltpu.get_barrier_semaphore(), 1 + 3 * (SIDE - 1))


def remote(source, target, send, receive, device):
    copy = pltpu.make_async_remote_copy(
        src_ref=source, dst_ref=target, send_sem=send, recv_sem=receive, device_id=device, device_id_type=MESH
    )
    copy.start()
    return copy


class Wave:
    ORDERS = ((2, 1, 0), (0, 2, 1), (1, 0, 2))

    def __init__(self, width, buffers, send, recv, local):
        self.width, self.buffers, self.send, self.recv, self.local = width, buffers, send, recv, local
        self.place, self.copies, self.kept = here(), {}, {}

    def block(self, ref, axis, value, third):
        index = tuple(value if other == axis else pl.ds(0, SIDE) for other in range(3))
        return ref.at[index + (slice(None), pl.ds(third * self.width, self.width))]

    def step(self, phase):
        for third, order in enumerate(self.ORDERS):
            if phase:
                self.settle(phase - 1, third)
            axis = order[phase]
            source, target = self.buffers[phase], self.buffers[phase + 1]
            spot = self.place[axis]
            for shift in (2, 1, 3):
                self.copies[phase, third, shift] = remote(
                    self.block(source, axis, (spot + shift) % SIDE, third),
                    self.block(target, axis, spot, third),
                    self.send.at[phase, third, shift - 1],
                    self.recv.at[phase, third, shift - 1],
                    across(axis, shift),
                )
            own = pltpu.make_async_copy(
                self.block(source, axis, spot, third), self.block(target, axis, spot, third), self.local.at[phase, third]
            )
            own.start()
            self.kept[phase, third] = own

    def settle(self, phase, third):
        for shift in range(1, SIDE):
            self.copies[phase, third, shift].wait_recv()
        self.kept[phase, third].wait()

    def land(self):
        for third in range(3):
            self.settle(2, third)

    def push(self, target, send, recv):
        source = self.buffers[3]
        pushes = []
        for third in range(3):
            self.settle(2, third)
            columns = (slice(None),) * 4 + (pl.ds(third * self.width, self.width),)
            pushes.append(remote(source.at[columns], target.at[columns], send.at[third], recv.at[third], other_core()))
        return pushes

    def sent(self):
        for copy in self.copies.values():
            copy.wait_send()


def experts(v):
    rows, act, bend, win, wout, win_turned, wout_turned = v.rows, v.act, v.bend, v.win, v.wout, v.win_turned, v.wout_turned
    drows_ref, dpre_ref = v.drows, v.dpre
    core_send, core_recv = v.push_send, v.push_recv

    def wave(n, width, buffers):
        return Wave(width, buffers, v.wave_send.at[n], v.wave_recv.at[n], v.wave_local.at[n])

    big = wave(0, BIG, (v.big0, v.big1, v.big2, v.big3))
    small = wave(1, SMALL, (v.small0, v.small1, v.small2, v.small3))
    back_small = wave(2, SMALL, (v.rsmall0, v.rsmall1, v.rsmall2, v.small_back))
    back_big = wave(3, BIG, (v.rbig0, v.rbig1, v.rbig2, v.big_back))
    for phase in range(3):
        big.step(phase)
        small.step(phase)
    v.normed_turned[...] = v.normed[...].T
    v.attended_turned[...] = v.attended[...].T
    for head in range(HH):
        v.probs_turned[head] = v.probs[head].astype(BF16).T
    pushes = big.push(v.big_theirs, core_send.at[0], core_recv.at[0])
    main, tails = unpacking(False)
    main_turned, tails_turned = unpacking(True)
    load = EXP * CAP
    hidden = win.shape[1]
    step = 512

    def groups(half, ref, width):
        packed = ref[...].reshape(SLOTS, 3 * width)
        for group in range(2):
            held = packed[group * HELD : (group + 1) * HELD]
            rest = 0.0
            for third in range(3):
                rest = rest + nn(tails[third], held[:, third * width : (third + 1) * width])
            first = half * load + group * LOAD
            yield slice(first, first + LOAD), nn(main, held).astype(BF16), rest.astype(BF16)

    def forward(half, source):
        there = slice(half * load, (half + 1) * load)
        for where, first, rest in groups(half, source, BIG):
            rows[where, :] = first
            drows_ref[where, D - BIG :] = rest
        normed = rows[there, :]
        for start in range(0, hidden, step):
            columns = slice(start, start + step)
            pre = nn(normed, win[:, columns])
            square = pre * pre
            slope = 0.7978845608028654
            upper = 0.5 + 0.5 * jnp.tanh(pre * (slope + (slope * 0.044715) * square))
            grown = pre * upper
            act[there, columns] = grown.astype(BF16)
            bend[there, columns] = upper + grown * (1.0 - upper) * (2 * slope + (6 * slope * 0.044715) * square)
        return nn(act[there, :], wout[...]).astype(BF16)

    def backward(half, source):
        there = slice(half * load, (half + 1) * load)
        for where, first, rest in groups(half, source, SMALL):
            drows_ref[where, : 3 * SMALL] = first
            drows_ref[where, 3 * SMALL : 4 * SMALL] = rest
        d_rows = drows_ref[there, :]
        for start in range(0, hidden, step):
            columns = slice(start, start + step)
            dpre_ref[there, columns] = (nn(d_rows, wout_turned[:, columns]) * bend[there, columns]).astype(BF16)
        return nn(dpre_ref[there, :], win_turned[...]).astype(BF16)

    def pack(values, last, width):
        for third in range(3):
            for group in range(2):
                there = slice(group * LOAD, (group + 1) * LOAD)
                own = nn(main_turned, values[there, third * width : (third + 1) * width])
                yield third, group, own + nn(tails_turned[third], last[there, :])

    def pack_small(out):
        return pack(out, out[:, 3 * SMALL : 4 * SMALL], SMALL)

    def pack_big(grad, out):
        return pack(grad, out[:, D - BIG :], BIG)

    def hand_over(packed, outgoing, incoming, n):
        copies = []
        for third, group, values in packed:
            outgoing[third, group * HELD : (group + 1) * HELD] = values.astype(BF16)
            if group:
                copies.append(
                    remote(outgoing.at[third], incoming.at[third], core_send.at[n, third], core_recv.at[n, third], other_core())
                )
        return copies

    def join(packed, incoming, copies, target, width):
        for third, group, values in packed:
            if group == 0:
                copies[third].wait_recv()
            total = (values + incoming[third, group * HELD : (group + 1) * HELD].astype(F32)).astype(BF16)
            target[2 * group : 2 * group + 2, :, :, :, third * width : (third + 1) * width] = total.reshape(
                SIDE // 2, SIDE, SIDE, SLOT, width
            )

    out = forward(0, v.big3)
    for push in pushes:
        push.wait_recv()
    pushes += small.push(v.small_theirs, core_send.at[1], core_recv.at[1])
    out_theirs = forward(1, v.big_theirs)
    small_copies = hand_over(pack_small(out_theirs), v.small_out, v.small_in, 2)
    for push in pushes[3:]:
        push.wait_recv()
    grad_theirs = backward(1, v.small_theirs)
    big_copies = hand_over(pack_big(grad_theirs, out_theirs), v.big_out, v.big_in, 3)
    join(pack_small(out), v.small_in, small_copies, v.rsmall0, SMALL)
    back_small.step(0)
    grad = backward(0, v.small3)
    back_small.step(1)
    join(pack_big(grad, out), v.big_in, big_copies, v.rbig0, BIG)
    back_big.step(0)
    back_small.step(2)
    win[:, :D] = rows[...].T
    back_big.step(1)
    wout[...] = act[...].T
    back_big.step(2)
    for copy in leaving(v):
        copy.start()
    back_small.land()
    back_big.land()
    for copy in pushes + small_copies + big_copies:
        copy.wait_send()
    for one in (big, small, back_small, back_big):
        one.sent()


def load_chunks(v, wq_ref, wk_ref, wv_ref, wo_ref, router_ref, attn_ref, ffn_ref, table_ref):
    v.stage[...] = jnp.zeros_like(v.stage)
    v.out16[...] = jnp.zeros_like(v.out16)
    v.out16[0:6, :] = wo_ref[...]

    def standing(ref):
        size = ref.shape[1]
        values = jnp.broadcast_to(ref[...].astype(F32), (QROW, size))
        kept = jnp.where(iota((QROW, size), 0) == iota((QROW, size), 1), values, 0.0)
        return jnp.sum(kept, axis=1, keepdims=True)

    column = iota((QROW, 64), 1)
    tail = jnp.where(column == 0, standing(attn_ref), 0.0)
    tail = jnp.where(column == 1, standing(ffn_ref), tail)
    tail = jnp.where(column == 2, standing(table_ref), tail).astype(BF16)
    for half in range(2):
        for n, ref in enumerate((wq_ref, wk_ref, wv_ref)):
            v.stage[half, 0:6, n * HW : (n + 1) * HW] = ref[:, half * HW : (half + 1) * HW]
        v.stage[half, 0:6, ROUTER : ROUTER + EXP] = router_ref[...]
        v.stage[half, :, GAIN:] = tail


def own_chunk(v, place):
    sp = lax.axis_index("sp")
    row, col = iota((QROW, QROW), 0), iota((QROW, QROW), 1)
    low = jnp.where((row == col) & (col < 6), 1.0, 0.0)
    high = jnp.where((row == col + 6) & (col < 6), 1.0, 0.0)
    own = jnp.where(sp == 0, low, high).astype(BF16)
    others = jnp.where(sp == 0, high, low).astype(BF16)
    later = (col >= 3).astype(jnp.int32)
    mine = nn(own, v.stage[sp]) + nn(others, v.chunk_got[...])
    v.pack[place[0], place[1], place[2], :, QW:] = mine[:, QW:].astype(BF16)
    for third in range(3):
        there = slice(third * HW, (third + 1) * HW)
        total = mine[:, there]
        for half in range(2):
            pick = hot((col < 6) & (col - 3 * later == third) & (row == 12 + 2 * later + half))
            total = total + nn(pick, v.out16[:, half * HW : (half + 1) * HW])
        v.pack[place[0], place[1], place[2], :, there] = total.astype(BF16)


class Gather:
    def __init__(self, v):
        self.v, self.place, self.copies = v, here(), {}

    def step(self, phase):
        for part, (first, width, order) in enumerate(PARTS):
            index = [pl.ds(0, SIDE) if axis in order[:phase] else self.place[axis] for axis in range(3)]
            block = self.v.pack.at[index[0], index[1], index[2], :, pl.ds(first, width)]
            if phase:
                self.settle(phase - 1, part)
            for shift in (2, 1, 3):
                self.copies[phase, part, shift] = remote(
                    block,
                    block,
                    self.v.gather_send.at[phase, part, shift - 1],
                    self.v.gather_recv.at[phase, part, shift - 1],
                    across(order[phase], shift),
                )

    def settle(self, phase, part):
        for shift in range(1, SIDE):
            self.copies[phase, part, shift].wait_recv()

    def land(self, parts):
        for part in parts:
            self.settle(2, part)

    def sent(self):
        for copy in self.copies.values():
            copy.wait_send()


class Reduce:
    def __init__(self, v):
        self.v, self.place, self.copies = v, here(), {}

    def push(self, phase, part, source, target):
        axis = PARTS[part][2][2 - phase]
        for shift in (2, 1, 3):
            self.copies[phase, part, shift] = remote(
                source((self.place[axis] + shift) % SIDE),
                target.at[shift - 1],
                self.v.reduce_send.at[phase, part, shift - 1],
                self.v.reduce_recv.at[phase, part, shift - 1],
                across(axis, shift),
            )

    def added(self, phase, part, own, arrived):
        values = own.astype(F32)
        for shift in range(1, SIDE):
            self.copies[phase, part, shift].wait_recv()
            values = values + arrived[shift - 1].astype(F32)
        return values

    def at(self, axes, axis, value):
        return tuple(value if one == axis else pl.ds(0, SIDE) for one in axes)

    def first(self, part):
        start, width, order = PARTS[part]

        def block(value):
            return self.v.pack.at[self.at((0, 1, 2), order[2], value) + (slice(None), pl.ds(start, width))]

        self.push(0, part, block, self.v.firsts[part])

    def second(self, part):
        start, width, order = PARTS[part]
        own = self.v.pack[self.at((0, 1, 2), order[2], self.place[order[2]]) + (slice(None), pl.ds(start, width))]
        sums = self.v.sums[part]
        sums[...] = self.added(0, part, own, self.v.firsts[part]).astype(BF16)
        self.push(1, part, lambda value: sums.at[self.at(sorted(order[:2]), order[1], value)], self.v.seconds[part])

    def third(self, part):
        order = PARTS[part][2]
        own = self.v.sums[part][self.at(sorted(order[:2]), order[1], self.place[order[1]])]
        pairs = self.v.pairs[part]
        pairs[...] = self.added(1, part, own, self.v.seconds[part]).astype(BF16)
        self.push(2, part, lambda value: pairs.at[value], self.v.thirds[part])

    def total(self, part):
        return self.added(2, part, self.v.pairs[part][self.place[PARTS[part][2][0]]], self.v.thirds[part])


def layer_kernel(names, *refs):
    v = SimpleNamespace(**dict(zip(names, refs, strict=True)))
    for group in ("firsts", "sums", "seconds", "pairs", "thirds"):
        setattr(v, group, [getattr(v, group + str(part)) for part in range(4)])
    greet()
    loads = [pltpu.make_async_copy(v.win_hbm.at[0], v.win, v.load_sem.at[0]), pltpu.make_async_copy(v.wout_hbm.at[0], v.wout, v.load_sem.at[1])]
    for load in loads:
        load.start()
    sp = lax.axis_index("sp")
    place = here()
    count = v.tok.shape[0]
    seq = 2 * count

    def to_core(source, target, n):
        return remote(source, target, v.core_send.at[n], v.core_recv.at[n], other_core())

    load_chunks(v, v.wq, v.wk, v.wv, v.wo, v.router, v.gain_attn, v.gain_ffn, v.bias_table)
    v.seq[sp] = v.tok[...]
    meet()
    chunk_copy = to_core(v.stage.at[1 - sp], v.chunk_got, 0)
    tok_copy = to_core(v.tok, v.seq.at[sp], 1)
    chunk_copy.wait()
    own_chunk(v, place)
    gather = Gather(v)
    gather.step(0)
    place_rows(v, v.routes, count)
    gather.step(1)
    tok_copy.wait()
    inputs = v.seq[...].reshape(seq, D).astype(F32)
    rms = rms_of(inputs)
    gather.step(2)
    for load in loads:
        load.wait()
    v.win_turned[...] = v.win[...].T
    v.wout_turned[...] = v.wout[...].T
    gather.land(range(3))
    unpack_chunks(v)
    gather.land(range(3, 4))
    unpack_rest(v)
    gather.sent()
    v.normed[...] = (inputs * rms * v.gains[64:65, :]).astype(BF16)
    distance_bias(v, v.buckets, seq)
    attend(v, seq)
    v.halves[...] = nn(v.attended[...], v.output[...]).reshape(v.halves.shape)
    half_copy = to_core(v.halves.at[1 - sp], v.half_got, 2)
    slots = iota((SLOTS, count), 0)
    turned = v.table[...].T.astype(jnp.int32)
    slot_hots = [hot(slots == turned[n : n + 1, :]) for n in range(8)]
    half_copy.wait()
    v.resid[...] = v.tok[...].astype(F32) + v.halves[sp] + v.half_got[...]
    fill_waves(v, v.cot, count, slot_hots)
    experts(v)
    d_logits, g_ffn = combine(v, v.cot, v.mixed, count)
    v.branch[sp] = v.dresid[...].astype(BF16)
    branch_copy = to_core(v.branch.at[sp], v.branch.at[sp], 3)
    g_router = tn(d_logits, v.ffn[...])
    to_chunk = chunk_hot(True, projection_row)
    to_output = [chunk_hot(True, output_row(third)) for third in range(3)]
    branch_copy.wait()
    attend_back(v, seq)
    d_branch = v.branch[...].reshape(seq, D)
    g_output = nn(v.attended_turned[...], d_branch).astype(BF16)
    reduce = Reduce(v)
    rows = WIDE // 2

    def split(values, x, second):
        return jnp.concatenate([values[x * rows : (x + 1) * rows], second[x * rows : (x + 1) * rows]], axis=0)

    for third in range(3):
        there = slice(third * HW, (third + 1) * HW)
        gradient = nn(v.normed_turned[...], v.dqkv[:, there]).astype(BF16)
        for x in range(SIDE):
            total = nn(to_chunk, split(gradient[: D // 2], x, gradient[D // 2 :]))
            total = total + nn(to_output[third], split(g_output[:, :HW], x, g_output[:, HW:]))
            v.pack[x, :, :, :, there] = total.astype(BF16).reshape(SIDE, SIDE, QROW, HW)
        reduce.first(third)
    d_normed = nt(v.dqkv[...], v.full[:, :QW])
    v.halves[...] = d_normed.reshape(v.halves.shape)
    norm_copy = to_core(v.halves.at[1 - sp], v.norm_got, 4)
    inputs = v.seq[...].reshape(seq, D).astype(F32)
    g_attn = jnp.sum(d_normed * inputs * rms_of(inputs), axis=0, keepdims=True)
    row = iota((64, D), 0)
    tail = jnp.zeros((64, D), F32)
    for n, values in enumerate((*split_two(g_attn), *split_two(g_ffn))):
        tail = jnp.where(row == n, values.astype(F32), tail)
    tail = jnp.concatenate([g_router, tail], axis=0).T.astype(BF16)
    high, low = split_two(table_gradient(v, v.buckets))
    column = iota((THICK, 128), 1)
    for x in range(SIDE):
        there = slice(x * THICK, (x + 1) * THICK)
        total = nn(to_chunk, split(tail[: D // 2], x, tail[D // 2 :]))
        total = jnp.where(column == 68, high[there].astype(F32), jnp.where(column == 69, low[there].astype(F32), total))
        v.pack[x, :, :, :, QW:] = total.astype(BF16).reshape(SIDE, SIDE, QROW, 128)
    reduce.first(3)
    norm_copy.wait()
    inputs = v.tok[...].astype(F32)
    d_normed = v.halves[sp] + v.norm_got[...]
    rms = rms_of(inputs)
    u = d_normed * v.gains[64:65, :]
    drop = inputs * (rms * rms * rms) * jnp.mean(u * inputs, axis=-1, keepdims=True)
    v.dtok[0] = v.dresid[...] + rms * u - drop
    for part in range(4):
        reduce.second(part)
    for part in range(4):
        reduce.third(part)
    for part, (first, width, _) in enumerate(PARTS):
        v.total[:, first : first + width] = reduce.total(part)
    total_copy = to_core(v.total, v.theirs, 5)
    for copy in reduce.copies.values():
        copy.wait_send()
    total_copy.wait()
    for copy in leaving(v):
        copy.wait()


def leaving(v):
    pairs = ((v.win.at[:, pl.ds(0, D)], v.turned_hbm), (v.drows, v.drows_hbm), (v.wout, v.act_hbm), (v.dpre, v.dpre_hbm))
    return [pltpu.make_async_copy(source, target, v.leave_sem.at[n]) for n, (source, target) in enumerate(pairs)]


def end_kernel(turned_hbm, drows_hbm, act_hbm, dpre_hbm, total, theirs, dtok_ref, mixed_ref, gin_hbm, gout_hbm, dtok_out, mixed_out, q_ref, k_ref, v_ref, o_ref, router_ref, attn_ref, ffn_ref, table_ref, turned, drows, act, dpre, gin, gout, sem):
    sp = lax.axis_index("sp")
    pieces = 6
    wide, tall = D // pieces, act.shape[0] // pieces

    def copy(source, target, n):
        one = pltpu.make_async_copy(source, target, sem.at[n])
        one.start()
        return one

    drows_copy = copy(drows_hbm, drows, 0)
    act_copies = [copy(act_hbm.at[pl.ds(n * tall, tall)], act.at[pl.ds(n * tall, tall)], 1 + n) for n in range(pieces)]
    rest = [copy(turned_hbm, turned, 7), copy(dpre_hbm, dpre, 8)]
    leaving_copies = []
    dtok_out[...] = dtok_ref[...]
    mixed_out[...] = mixed_ref[...]
    for row in range(6):
        for half in range(2):
            there = 12 + row // 3 * 2 + half
            third = row % 3 * HW
            o_ref[row : row + 1, half * HW : (half + 1) * HW] = total[there : there + 1, third : third + HW]
    mine = jnp.where(sp == 0, total[0:6, :], total[6:12, :])
    other = jnp.where(sp == 0, theirs[0:6, :], theirs[6:12, :])
    for n, ref in enumerate((q_ref, k_ref, v_ref)):
        there = slice(n * HW, (n + 1) * HW)
        ref[:, :HW] = jnp.where(sp == 0, mine[:, there], other[:, there])
        ref[:, HW:] = jnp.where(sp == 0, other[:, there], mine[:, there])
    router_ref[...] = mine[:, ROUTER : ROUTER + EXP] + other[:, ROUTER : ROUTER + EXP]
    extra = mine[:, GAIN:] + other[:, GAIN:]
    diagonal = iota((6, 6), 0) == iota((6, 6), 1)
    for n, ref in enumerate((attn_ref, ffn_ref, table_ref)):
        column = extra[:, 2 * n : 2 * n + 1] + extra[:, 2 * n + 1 : 2 * n + 2]
        ref[...] = jnp.sum(jnp.where(diagonal, column, 0.0), axis=0, keepdims=True)[:, : ref.shape[1]]
    drows_copy.wait()
    for n in range(pieces):
        act_copies[n].wait()
        there = pl.ds(n * tall, tall)
        gout[there, :] = nn(act[there, :], drows[...])
        leaving_copies.append(copy(gout.at[there], gout_hbm.at[0, there], 9 + n))
    for one in rest:
        one.wait()
    for n in range(pieces):
        there = pl.ds(n * wide, wide)
        gin[there, :] = nn(turned[there, :], dpre[...])
        leaving_copies.append(copy(gin.at[there], gin_hbm.at[0, there], 15 + n))
    for one in leaving_copies:
        one.wait()


def layer_buffers(count, hidden, load):
    seq = 2 * count
    cube = (SIDE, SIDE, SIDE)
    bigs, smalls = (*cube, SLOT, 3 * BIG), (*cube, SLOT, 3 * SMALL)
    buffers = {
        "stage": ((2, QROW, PW), BF16),
        "chunk_got": ((QROW, PW), BF16),
        "out16": ((QROW, D), BF16),
        "pack": ((*cube, QROW, PW), BF16),
        "seq": ((2, count, D), BF16),
        "full": ((D, PW), BF16),
        "output": ((HW, D), BF16),
        "gains": ((128, D), F32),
        "normed": ((seq, D), BF16),
        "bias": ((16, seq), F32),
        "qkv": ((seq, QW), BF16),
        "probs": ((HH, seq, seq), F32),
        "attended": ((seq, HW), BF16),
        "normed_turned": ((D, seq), BF16),
        "attended_turned": ((HW, seq), BF16),
        "probs_turned": ((HH, seq, seq), BF16),
        "halves": ((2, count, D), F32),
        "half_got": ((count, D), F32),
        "norm_got": ((count, D), F32),
        "resid": ((count, D), F32),
        "dresid": ((count, D), F32),
        "ffn": ((count, D), BF16),
        "table": ((count, 128), F32),
        "gates": ((count, 128), F32),
        "branch": ((2, count, D), BF16),
        "dqkv": ((seq, QW), BF16),
        "ddist": ((16, seq), F32),
        "rows": ((load, D), BF16),
        "drows": ((load, D), BF16),
        "act": ((load, hidden), BF16),
        "dpre": ((load, hidden), BF16),
        "bend": ((load, hidden), F32),
        "win": ((D, hidden), BF16),
        "wout": ((hidden, D), BF16),
        "win_turned": ((hidden, D), BF16),
        "wout_turned": ((D, hidden), BF16),
        "big_out": ((3, SLOTS, BIG), BF16),
        "big_in": ((3, SLOTS, BIG), BF16),
        "small_out": ((3, SLOTS, SMALL), BF16),
        "small_in": ((3, SLOTS, SMALL), BF16),
    }
    for name in ("big0", "big1", "big2", "big3", "big_theirs", "rbig0", "rbig1", "rbig2", "big_back"):
        buffers[name] = (bigs, BF16)
    for name in ("small0", "small1", "small2", "small3", "small_theirs", "rsmall0", "rsmall1", "rsmall2", "small_back"):
        buffers[name] = (smalls, BF16)
    for part, (_, width, _) in enumerate(PARTS):
        buffers[f"firsts{part}"] = ((SIDE - 1, SIDE, SIDE, QROW, width), BF16)
        buffers[f"sums{part}"] = ((SIDE, SIDE, QROW, width), BF16)
        buffers[f"seconds{part}"] = ((SIDE - 1, SIDE, QROW, width), BF16)
        buffers[f"pairs{part}"] = ((SIDE, QROW, width), BF16)
        buffers[f"thirds{part}"] = ((SIDE - 1, QROW, width), BF16)
    semaphores = {
        "load_sem": (2,),
        "leave_sem": (4,),
        "core_send": (6,),
        "core_recv": (6,),
        "gather_send": (3, 4, SIDE - 1),
        "gather_recv": (3, 4, SIDE - 1),
        "reduce_send": (3, 4, SIDE - 1),
        "reduce_recv": (3, 4, SIDE - 1),
        "push_send": (4, 3),
        "push_recv": (4, 3),
        "wave_send": (4, 3, 3, SIDE - 1),
        "wave_recv": (4, 3, 3, SIDE - 1),
        "wave_local": (4, 3, 3),
    }
    scratch = {name: pltpu.VMEM(*one) for name, one in buffers.items()}
    return scratch | {name: pltpu.SemaphoreType.DMA(one) for name, one in semaphores.items()}


def shards(tokens, cotangent, w_query, w_key, w_value, w_output, gain_attn, gain_ffn, router, bias_table, w_in, w_out, routes, buckets):
    count = tokens.shape[1]
    load = 2 * EXP * CAP
    hidden = w_in.shape[2]
    in_vmem = pl.BlockSpec(memory_space=pltpu.VMEM)
    anywhere = pl.BlockSpec(memory_space=pl.ANY)
    given = {
        "wq": w_query,
        "wk": w_key,
        "wv": w_value,
        "wo": w_output,
        "router": router,
        "gain_attn": gain_attn[None],
        "gain_ffn": gain_ffn[None],
        "bias_table": bias_table[None],
        "tok": tokens[0],
        "cot": cotangent[0],
        "routes": routes[0].T,
        "buckets": buckets[None],
        "win_hbm": w_in,
        "wout_hbm": w_out,
    }
    made = {
        "turned_hbm": ((D, load), BF16),
        "drows_hbm": ((load, D), BF16),
        "act_hbm": ((hidden, load), BF16),
        "dpre_hbm": ((load, hidden), BF16),
        "total": ((QROW, PW), F32),
        "theirs": ((QROW, PW), F32),
        "dtok": ((1, count, D), F32),
        "mixed": ((1, count, D), BF16),
    }
    scratch = layer_buffers(count, hidden, load)
    names = [*given, *made, *scratch]
    turned, d_rows, act, d_pre, total, theirs, d_tokens, mixed = pl.pallas_call(
        lambda *refs: layer_kernel(names, *refs),
        in_specs=[anywhere if name.endswith("_hbm") else in_vmem for name in given],
        out_specs=[anywhere if name.endswith("_hbm") else in_vmem for name in made],
        out_shape=[jax.ShapeDtypeStruct(*one) for one in made.values()],
        scratch_shapes=list(scratch.values()),
        compiler_params=pltpu.CompilerParams(vmem_limit_bytes=VMEM_LIMIT, collective_id=0, has_side_effects=True),
        cost_estimate=pl.CostEstimate(flops=20 * 10**9, bytes_accessed=20 * 10**6, transcendentals=load * hidden),
    )(*given.values())

    grad_w_in, grad_w_out, d_tokens, mixed, g_query, g_key, g_value, g_output, g_router, g_attn, g_ffn, g_table = pl.pallas_call(
        end_kernel,
        in_specs=[anywhere] * 4 + [in_vmem] * 4,
        out_specs=[anywhere] * 2 + [in_vmem] * 10,
        out_shape=[
            jax.ShapeDtypeStruct((1, D, hidden), F32),
            jax.ShapeDtypeStruct((1, hidden, D), F32),
            jax.ShapeDtypeStruct((1, count, D), F32),
            jax.ShapeDtypeStruct((1, count, D), BF16),
        ]
        + [jax.ShapeDtypeStruct(shape, F32) for shape in ((6, D),) * 4 + ((6, EXP), (1, 6), (1, 6), (1, 3))],
        scratch_shapes=[
            pltpu.VMEM((D, load), BF16),
            pltpu.VMEM((load, D), BF16),
            pltpu.VMEM((hidden, load), BF16),
            pltpu.VMEM((load, hidden), BF16),
            pltpu.VMEM((D, hidden), F32),
            pltpu.VMEM((hidden, D), F32),
            pltpu.SemaphoreType.DMA((21,)),
        ],
        compiler_params=pltpu.CompilerParams(vmem_limit_bytes=VMEM_LIMIT),
        cost_estimate=pl.CostEstimate(flops=4 * load * D * hidden, bytes_accessed=20 * 10**6, transcendentals=0),
    )(turned, d_rows, act, d_pre, total, theirs, d_tokens, mixed)
    return (mixed, d_tokens, g_query, g_key, g_value, g_output, g_attn[0], g_ffn[0], g_router, g_table[0], grad_w_in, grad_w_out)


def solution(mesh):
    wide = P(("sp", "ep"), None)
    flat = P(("sp", "ep"))
    rows = P("ep", "sp", None)
    return jax.shard_map(
        shards,
        mesh=mesh,
        in_specs=(rows, rows, wide, wide, wide, wide, flat, flat, wide, flat, P("ep", None, "sp"), rows, rows, P()),
        out_specs=(rows, rows, wide, wide, wide, wide, flat, flat, wide, flat, P("ep", None, "sp"), rows),
        check_vma=False,
    )
```
